32 devices in a mesh: region: 16 (over z, y, x), dom: 2 (over core).
Axes of the slice: x: 2, y: 2, z: 4, core: 2. Of those that a mesh axis runs over, the one named last changes fastest.
Arguments:
- fine_state: float32 [16384, 128], P(('region', 'dom')), may hold values from -6 to 6
- fine_nbr: int32 [16, 16384], P(None, ('region', 'dom')), may hold values from 0 to 575
- fine_mask: int32 [16, 16384], P(None, ('region', 'dom')), may hold values 0 or 1
- send_rows: int32 [4, 512], P(None, ('region', 'dom')), may hold values from 0 to 511
- coarse_nbr: int32 [16, 4096], P(None, ('region', 'dom')), may hold values from 0 to 255
- coarse_mask: int32 [16, 4096], P(None, ('region', 'dom')), may hold values 0 or 1
- parent: int32 [16384], P(('region', 'dom')), may hold values from 0 to 4095, as said below
- interp_share: int32 [16384], P(('region', 'dom')), may hold values from 1 to 4
- edge_w: float32 [4, 3, 128, 128], replicated, may hold values from -0.375 to 0.375
- node_w: float32 [4, 3, 128, 128], replicated, may hold values from -0.375 to 0.375
- biases: float32 [4, 4, 128], replicated, may hold values from -3 to 3
Outputs:
- fine_out: float32 [16384, 128], P(('region', 'dom'))
- coarse_out: float32 [4096, 128], P(('region', 'dom'))
The draws below stay inside these ranges and needn't reach their ends.
Inputs may be any that keep to these rules, and one draw needn't show every extreme that they name: `parent`: of the 512 fine nodes of block (r, d), 448 have parents in coarse blocks of region r, at most 384 in any one block and exactly 384 in some block; 32 have parents in blocks of region r-1 and 32 in blocks of region r+1 (periodic), at most 32 in any one block and exactly 32 in some block of each.
All inputs are finite; a program needn't handle non-finite values. No bound on the sum of `fine_mask` or of `coarse_mask` on one device may be relied on, other than what follows from the above.
Results may differ from the reference program's by a relative error of at most 0.0001.
Values sent between devices are 32-bit elements; how exact they have to be, the bound alone decides.
No kernel may reach another device: no remote copies, remote signals or barrier semaphores. Data moves between devices by JAX's collectives and lax.ppermute only.
A program may use at most 64 MiB of HBM per device.

```python
import jax
import jax.numpy as jnp
from jax import lax

W = 128
SLOTS = 16
LAYERS = 4
F = 512
H = 16
C = 128
SIDE = 32
CAP = 384
SCAP = 32
FN = 16384
CN = 4096
RC = 256
N_REGION = 16
N_DOM = 2
DEVICES = 32


def bin_counts(count_key, bins, total, most):
    split_keys = jax.random.split(count_key, 2)
    big_bin = jax.random.randint(split_keys[0], (), 0, bins)
    units = (bins - 1) * most
    unit_label = jnp.arange(units, dtype=jnp.int32) // most
    shuffled = jax.random.permutation(split_keys[1], units)
    taken = (jnp.arange(units, dtype=jnp.int32) < total - most).astype(jnp.int32)
    extra = jnp.zeros((bins - 1,), jnp.int32).at[unit_label[shuffled]].add(taken)
    positions = jnp.arange(bins, dtype=jnp.int32)
    other_index = jnp.clip(positions - (positions > big_bin).astype(jnp.int32), 0, bins - 2)
    return jnp.where(positions == big_bin, most, extra[other_index]).astype(jnp.int32)


def labels_of(counts, length):
    ends = jnp.cumsum(counts)
    return jnp.sum((ends[None, :] <= jnp.arange(length, dtype=jnp.int32)[:, None]).astype(jnp.int32), axis=1)


def owner_draw(device_key, device_number):
    split_keys = jax.random.split(device_key, 5)
    own_len = F - 2 * SIDE
    region_now = device_number // N_DOM
    own_dom = labels_of(bin_counts(split_keys[0], N_DOM, own_len, CAP), own_len)
    low_dom = labels_of(bin_counts(split_keys[1], N_DOM, SIDE, SCAP), SIDE)
    high_dom = labels_of(bin_counts(split_keys[2], N_DOM, SIDE, SCAP), SIDE)
    regions_of = jnp.concatenate([jnp.zeros((own_len,), jnp.int32) + region_now, jnp.zeros((SIDE,), jnp.int32) + (region_now + N_REGION - 1) % N_REGION, jnp.zeros((SIDE,), jnp.int32) + (region_now + 1) % N_REGION])
    doms_of = jnp.concatenate([own_dom, low_dom, high_dom])
    owner_dev = regions_of * N_DOM + doms_of
    owner_dev = owner_dev[jax.random.permutation(split_keys[3], F)]
    local_parent = jax.random.randint(split_keys[4], (F,), 0, C)
    return (owner_dev * C + local_parent).astype(jnp.int32)


def draw_parent(key, part):
    device_keys = jax.random.split(key, DEVICES)
    numbers = jnp.arange(DEVICES, dtype=jnp.int32)
    return jax.vmap(owner_draw)(device_keys, numbers).reshape(FN).astype(jnp.int32)


def touch_ends(values, stream_key, low, high):
    shape = values.shape
    spot = [jax.random.randint(jax.random.fold_in(stream_key, axis), (), 0, shape[axis]) for axis in range(len(shape))]
    values = values.at[tuple(spot)].set(low)
    longest = shape.index(max(shape))
    spot[longest] = (spot[longest] + 1) % shape[longest]
    return values.at[tuple(spot)].set(high)


def steps_of(own_key, dims, cuts, smallest, top_value):
    def one(axis_at, parts):
        heights = jax.random.uniform(jax.random.fold_in(jax.random.fold_in(own_key, 6), axis_at), (parts,), jnp.float32, smallest / len(cuts), top_value / len(cuts))
        return jnp.repeat(jnp.exp(heights), dims[axis_at] // parts).reshape((-1,) + (1,) * (len(dims) - axis_at - 1))

    loudness = one(*cuts[0])
    for cut in cuts[1:]:
        loudness = loudness * one(*cut)
    return loudness


def scatter_about(stream_key, shape, scale, most, cuts=(), kind=jnp.bfloat16):
    result = jax.random.normal(stream_key, shape, jnp.float32) * scale
    if len(cuts) > 0:
        result = steps_of(stream_key, shape, cuts, -0.22, 0.18) * result
    return jnp.clip(result, min=-most, max=most).astype(kind)


def setup_inputs(seed: int = 0) -> dict:
    key_list = jax.random.split(jax.random.key(seed), 12)
    fine_state = scatter_about(key_list[0], (FN, W), 1.0, 6.0, ((0, 32),), jnp.float32)
    fine_nbr = touch_ends(jax.random.randint(key_list[1], (SLOTS, FN), 0, F + 4 * H), jax.random.fold_in(key_list[1], 1), 0, (F + 4 * H) - 1).astype(jnp.int32)
    fine_mask = touch_ends((jax.random.randint(key_list[2], (SLOTS, FN), 0, 16) < 13).astype(jnp.int32), jax.random.fold_in(key_list[2], 1), 0, 1)
    send_rows = touch_ends(jax.random.randint(key_list[3], (4, DEVICES * H), 0, F), jax.random.fold_in(key_list[3], 1), 0, F - 1).astype(jnp.int32)
    coarse_nbr = touch_ends(jax.random.randint(key_list[4], (SLOTS, CN), 0, RC), jax.random.fold_in(key_list[4], 1), 0, RC - 1).astype(jnp.int32)
    coarse_mask = touch_ends((jax.random.randint(key_list[5], (SLOTS, CN), 0, 16) < 13).astype(jnp.int32), jax.random.fold_in(key_list[5], 1), 0, 1)
    parent = draw_parent(jax.random.fold_in(key_list[11], 71), 0)
    interp_share = touch_ends(jax.random.randint(key_list[7], (FN,), 1, 5), jax.random.fold_in(key_list[7], 1), 1, 4).astype(jnp.int32)
    edge_w = scatter_about(key_list[8], (LAYERS, 3, W, W), (2 * W) ** -0.5, 0.375, (), jnp.float32)
    node_w = scatter_about(key_list[9], (LAYERS, 3, W, W), (2 * W) ** -0.5, 0.375, (), jnp.float32)
    biases = scatter_about(key_list[10], (LAYERS, 4, W), 0.5, 3.0, (), jnp.float32)
    return {"fine_state": fine_state, "fine_nbr": fine_nbr, "fine_mask": fine_mask, "send_rows": send_rows, "coarse_nbr": coarse_nbr, "coarse_mask": coarse_mask, "parent": parent, "interp_share": interp_share, "edge_w": edge_w, "node_w": node_w, "biases": biases}


epsilon = 1e-05

def product(left_side, right_side):
    return jnp.dot(left_side, right_side, precision=lax.Precision.HIGHEST, preferred_element_type=jnp.float32)

def normed(values):
    center = values - lax.optimization_barrier(jnp.mean(values, axis=-1, keepdims=True))
    spread = lax.optimization_barrier(jnp.mean(center * center, axis=-1, keepdims=True))
    return center * lax.rsqrt(spread + epsilon)

def message_layer(own_rows, source_proj, neighbours, validity, edge_w, node_w, biases, layer_idx):
    own_term = product(own_rows, edge_w[layer_idx, 0]) + biases[layer_idx, 0]

    def one_slot(running, slot_data):
        index_row, valid_row = slot_data
        hidden = jax.nn.relu(own_term + jnp.take(source_proj, index_row, axis=0))
        message = normed(product(hidden, edge_w[layer_idx, 2]) + biases[layer_idx, 1])
        return (running + valid_row.astype(jnp.float32)[:, None] * message, None)
    gathered, unused = lax.scan(one_slot, jnp.zeros(own_rows.shape, jnp.float32), (neighbours, validity))
    inner_act = jax.nn.relu(product(own_rows, node_w[layer_idx, 0]) + product(gathered, node_w[layer_idx, 1]) + biases[layer_idx, 2])
    return own_rows + normed(product(inner_act, node_w[layer_idx, 2]) + biases[layer_idx, 3])

def fine_layer(fine_rows, fine_nbr, fine_mask, send_rows, edge_w, node_w, biases, layer_idx):
    device_grid = fine_rows.reshape(N_REGION, N_DOM, F, W)
    send_lists = send_rows.reshape(4, N_REGION, N_DOM, H)

    def picked(direction):
        return jnp.take_along_axis(device_grid, send_lists[direction][..., None], axis=2)
    from_region_low = jnp.roll(picked(0), 1, axis=0)
    from_region_high = jnp.roll(picked(1), -1, axis=0)
    from_dom_low = jnp.roll(picked(2), 1, axis=1)
    from_dom_high = jnp.roll(picked(3), -1, axis=1)
    extended = jnp.concatenate([device_grid, from_region_low, from_region_high, from_dom_low, from_dom_high], axis=2)
    extended = extended.reshape(DEVICES, F + 4 * H, W)
    own_blocks = fine_rows.reshape(DEVICES, F, W)
    nbr_blocks = fine_nbr.reshape(SLOTS, DEVICES, F).transpose(1, 0, 2)
    mask_blocks = fine_mask.reshape(SLOTS, DEVICES, F).transpose(1, 0, 2)

    def per_device(device_items):
        own_rows, ext_rows, nbr_rows, mask_rows = device_items
        return message_layer(own_rows, product(ext_rows, edge_w[layer_idx, 1]), nbr_rows, mask_rows, edge_w, node_w, biases, layer_idx)
    return lax.map(per_device, (own_blocks, extended, nbr_blocks, mask_blocks)).reshape(FN, W)

def coarse_layer(coarse_rows, coarse_nbr, coarse_mask, edge_w, node_w, biases, layer_idx):
    grouped = coarse_rows.reshape(N_REGION, RC, W)
    nbr_groups = coarse_nbr.reshape(SLOTS, N_REGION, RC).transpose(1, 0, 2)
    mask_groups = coarse_mask.reshape(SLOTS, N_REGION, RC).transpose(1, 0, 2)

    def per_region(region_items):
        own_rows, nbr_rows, mask_rows = region_items
        return message_layer(own_rows, product(own_rows, edge_w[layer_idx, 1]), nbr_rows, mask_rows, edge_w, node_w, biases, layer_idx)
    return lax.map(per_region, (grouped, nbr_groups, mask_groups)).reshape(CN, W)

def reference(fine_state, fine_nbr, fine_mask, send_rows, coarse_nbr, coarse_mask, parent, interp_share, edge_w, node_w, biases):
    fine_rows = fine_layer(fine_state, fine_nbr, fine_mask, send_rows, edge_w, node_w, biases, 0)
    weights_num = interp_share.astype(jnp.float32)
    summed = jax.ops.segment_sum(weights_num[:, None] * fine_rows, parent, num_segments=CN)
    totals = jax.ops.segment_sum(weights_num, parent, num_segments=CN)
    coarse_rows = summed / jnp.maximum(totals, 1.0)[:, None]
    coarse_rows = coarse_layer(coarse_rows, coarse_nbr, coarse_mask, edge_w, node_w, biases, 1)
    coarse_rows = coarse_layer(coarse_rows, coarse_nbr, coarse_mask, edge_w, node_w, biases, 2)
    fine_rows = fine_rows + (weights_num / 4.0)[:, None] * jnp.take(coarse_rows, parent, axis=0)
    fine_rows = fine_layer(fine_rows, fine_nbr, fine_mask, send_rows, edge_w, node_w, biases, 3)
    return (fine_rows, coarse_rows)
```

```python
import functools

import jax
import jax.numpy as jnp
from jax import lax
from jax.experimental import pallas as pl
from jax.experimental.pallas import tpu as pltpu
from jax.sharding import PartitionSpec as P

epsilon = 1e-05
f32 = jnp.float32
bf16 = jnp.bfloat16
LANES = 128
VMEM_BYTES = 32 * 2**20


def split(values):
    high = values.astype(bf16)
    low = (values - high.astype(f32)).astype(bf16)
    return high, low


def left_factor(weight):
    high, low = split(weight.T)
    return jnp.concatenate(
        [jnp.concatenate([high, high], axis=1), jnp.concatenate([low, low], axis=1)], axis=0
    )


def folded(stacked):
    half = stacked.shape[0] // 2
    return stacked[:half] + stacked[half:]


def times(factor, columns):
    high, low = split(columns)
    stacked = jnp.concatenate([high, low], axis=0)
    return folded(jnp.dot(factor, stacked, preferred_element_type=f32))


def centered(weight):
    return weight - jnp.mean(weight, axis=-1, keepdims=True)


def bias_column(row, width):
    block = jnp.broadcast_to(row, (LANES, row.shape[-1])).T
    return jnp.concatenate([block] * (width // LANES), axis=1)


def scaled(columns):
    spread = jnp.mean(columns * columns, axis=0, keepdims=True)
    return columns * lax.rsqrt(spread + epsilon)


def lane_gather(source, index):
    features = source.shape[0]
    blocks = source.shape[1] // LANES
    pieces = []
    for start in range(0, index.shape[1], LANES):
        wide = jnp.broadcast_to(index[:, start : start + LANES], (features, LANES))
        inner = wide & (LANES - 1)
        outer = wide // LANES
        found = jnp.take_along_axis(source[:, :LANES], inner, axis=1)
        for block in range(1, blocks):
            piece = source[:, block * LANES : (block + 1) * LANES]
            found = jnp.where(outer == block, jnp.take_along_axis(piece, inner, axis=1), found)
        pieces.append(found)
    return jnp.concatenate(pieces, axis=1)


def layer_columns(own, sources, neighbours, validity, edge_ref, node_ref, bias_ref):
    count = own.shape[1]
    biases = bias_ref[0]
    own_term = times(left_factor(edge_ref[0, 0]), own) + bias_column(biases[0:1], count)
    source_proj = times(left_factor(edge_ref[0, 1]), sources)
    second = left_factor(centered(edge_ref[0, 2]))
    second_bias = bias_column(centered(biases[1:2]), count)
    gathered = jnp.zeros(own.shape, f32)
    for slot in range(neighbours.shape[0]):
        index_row = neighbours[slot : slot + 1, :]
        valid_row = validity[slot : slot + 1, :]
        hidden = jnp.maximum(own_term + lane_gather(source_proj, index_row), 0.0)
        message = times(second, hidden) + second_bias
        spread = jnp.mean(message * message, axis=0, keepdims=True)
        gathered = gathered + message * (lax.rsqrt(spread + epsilon) * valid_row.astype(f32))
    inner_act = jnp.maximum(
        times(left_factor(node_ref[0, 0]), own)
        + times(left_factor(node_ref[0, 1]), gathered)
        + bias_column(biases[2:3], count),
        0.0,
    )
    update = times(left_factor(centered(node_ref[0, 2])), inner_act)
    return own + scaled(update + bias_column(centered(biases[3:4]), count))


def iota(shape, axis):
    return lax.broadcasted_iota(jnp.int32, shape, axis)


def hot(rows, index):
    return (iota((rows, index.shape[1]), 0) == index).astype(f32)


def pick_kernel(
    rim, send_ref, parent_s, share_s, state_ref, nbr_ref, mask_ref, even_ref, odd_ref, dom_ref
):
    even = lax.rem(lax.axis_index("region"), 2) == 0
    first = jnp.where(even, 1, 0)
    lane = iota((1, LANES), 1)

    def fill(out, out_base, direction, lane_base, parents, shares):
        for k in range(rim):
            row = send_ref[direction, k]
            out[pl.ds(out_base + k, 1), :] = state_ref[pl.ds(row, 1), :]
            here = lane == lane_base + k
            parents = jnp.where(here, parent_s[row].astype(f32), parents)
            shares = jnp.where(here, share_s[row].astype(f32), shares)
        return parents, shares

    zero = jnp.zeros((1, LANES), f32)
    for out, direction in ((even_ref, first), (odd_ref, 1 - first)):
        parents, shares = fill(out, 0, direction, direction * rim, zero, zero)
        out[rim : rim + 8, :] = jnp.zeros((8, LANES), f32)
        out[rim : rim + 1, :] = parents
        out[rim + 1 : rim + 2, :] = shares
    parents, shares = fill(dom_ref, 0, 2, 2 * rim, zero, zero)
    parents, shares = fill(dom_ref, rim, 3, 3 * rim, parents, shares)
    base = 2 * rim
    dom_ref[base : base + 8, :] = jnp.zeros((8, LANES), f32)
    dom_ref[base : base + 1, :] = parents
    dom_ref[base + 1 : base + 2, :] = shares
    slots = nbr_ref.shape[0]
    dom_ref[base + 8 : base + 8 + slots, :] = nbr_ref[...].astype(f32)
    dom_ref[base + 8 + slots : base + 8 + 2 * slots, :] = mask_ref[...].astype(f32)


def rim_rows(rim, even, recv_even, recv_odd, recv_dom):
    low = jnp.where(even, recv_even, recv_odd)
    high = jnp.where(even, recv_odd, recv_even)
    pad = jnp.zeros((LANES - 4 * rim, low.shape[1]), f32)
    return jnp.concatenate([low, high, recv_dom, pad], axis=0)


def fine_kernel(
    rim,
    group,
    side,
    regions,
    send_ref,
    state_ref,
    recv_even,
    recv_odd,
    recv_dom,
    nbr_ref,
    mask_ref,
    parent_ref,
    share_ref,
    edge_ref,
    node_ref,
    bias_ref,
    fine_ref,
    even_ref,
    odd_ref,
    dom_ref,
    rows_ref,
):
    region = lax.axis_index("region")
    even = lax.rem(region, 2) == 0
    own = state_ref[...].T
    outer = rim_rows(rim, even, recv_even[:rim], recv_odd[:rim], recv_dom[: 2 * rim]).T
    sources = jnp.concatenate([own, outer], axis=1)
    fine = layer_columns(own, sources, nbr_ref, mask_ref, edge_ref, node_ref, bias_ref)
    fine_ref[...] = fine
    rows = fine.T
    rows_ref[...] = rows
    count = rows.shape[0]
    pair = jnp.concatenate(split(rows), axis=1)

    def weighted(selection):
        both = jnp.dot(selection.astype(bf16), pair, preferred_element_type=f32)
        return both[:, :LANES] + both[:, LANES:]

    parent = parent_ref[...]
    share = share_ref[...].astype(f32)
    chosen = hot(group, parent - region * group) * share
    dom_ref[0:group, :] = weighted(chosen)
    ones = jnp.ones((8, count), f32)
    totals = lax.dot_general(
        ones, chosen, (((1,), (1,)), ((), ())), preferred_element_type=f32
    )
    for block in range(group // LANES):
        dom_ref[group + 8 * block : group + 8 * (block + 1), :] = totals[
            :, block * LANES : (block + 1) * LANES
        ]
    base = group + 8 * (group // LANES)
    for k in range(2 * rim):
        row = send_ref[2 + k // rim, k % rim]
        dom_ref[base + k : base + k + 1, :] = rows_ref[pl.ds(row, 1), :]

    below = lax.rem(region + regions - 1, regions)
    above = lax.rem(region + 1, regions)
    earlier = (iota((count, count), 0) < iota((count, count), 1)).astype(bf16)
    first = jnp.where(even, 1, 0)
    for out, target, direction in (
        (even_ref, jnp.where(even, below, above), first),
        (odd_ref, jnp.where(even, above, below), 1 - first),
    ):
        local = parent - target * group
        inside = (local >= 0) & (local < group)
        member = jnp.where(inside, 1.0, 0.0)
        rank = jnp.dot(
            jnp.broadcast_to(member, (8, count)).astype(bf16), earlier, preferred_element_type=f32
        )[0:1]
        place = jnp.where(inside, rank.astype(jnp.int32), -1)
        picked = hot(LANES, place)
        out[0:side, :] = weighted((picked * share)[:side])
        facts = jnp.concatenate(
            [local.astype(f32), share, jnp.zeros((6, count), f32)], axis=0
        )
        out[side : side + 8, :] = lax.dot_general(
            facts,
            picked,
            (((1,), (1,)), ((), ())),
            precision=lax.Precision.HIGHEST,
            preferred_element_type=f32,
        )
        for k in range(rim):
            row = send_ref[direction, k]
            out[side + 8 + k : side + 9 + k, :] = rows_ref[pl.ds(row, 1), :]
        out[side + 8 + rim :, :] = jnp.zeros((out.shape[0] - side - 8 - rim, LANES), f32)


def coarse_kernel(
    rim,
    group,
    side,
    mine_ref,
    other_ref,
    even_mine,
    odd_mine,
    even_other,
    odd_other,
    nbr_ref,
    mask_ref,
    recv_dom,
    edge_one,
    node_one,
    bias_one,
    edge_two,
    node_two,
    bias_two,
    group_ref,
    out_ref,
    rows_ref,
):
    dom = lax.axis_index("dom")
    total = mine_ref[0:group, :] + other_ref[0:group, :]
    weight = [
        mine_ref[group + 8 * b : group + 8 * b + 8, :]
        + other_ref[group + 8 * b : group + 8 * b + 8, :]
        for b in range(group // LANES)
    ]
    weight = jnp.concatenate(weight, axis=1)
    for block in (even_mine, odd_mine, even_other, odd_other):
        depth = block.shape[0]
        known = iota((1, depth), 1) < side
        index = jnp.where(known, block[side : side + 1, :depth].astype(jnp.int32), -1)
        share = jnp.where(known, block[side + 1 : side + 2, :depth], 0.0)
        chosen = hot(group, index)
        both = jnp.dot(
            chosen.astype(bf16),
            jnp.concatenate(split(block[...]), axis=1),
            preferred_element_type=f32,
        )
        total = total + (both[:, :LANES] + both[:, LANES:])
        weight = weight + lax.dot_general(
            jnp.broadcast_to(share, (8, depth)),
            chosen,
            (((1,), (1,)), ((), ())),
            preferred_element_type=f32,
        )
    columns = total.T / jnp.maximum(weight[0:1], 1.0)
    base = 2 * rim + 8
    slots = nbr_ref.shape[0]
    mine_first = dom == 0

    def ordered(mine, other):
        return jnp.concatenate(
            [jnp.where(mine_first, mine, other), jnp.where(mine_first, other, mine)], axis=1
        )

    nbr = ordered(nbr_ref[...], recv_dom[base : base + slots, :].astype(jnp.int32))
    mask = ordered(mask_ref[...], recv_dom[base + slots : base + 2 * slots, :].astype(jnp.int32))
    columns = layer_columns(columns, columns, nbr, mask, edge_one, node_one, bias_one)
    columns = layer_columns(columns, columns, nbr, mask, edge_two, node_two, bias_two)
    group_ref[...] = columns
    rows_ref[...] = columns.T
    own = out_ref.shape[0]
    out_ref[...] = rows_ref[pl.ds(pl.multiple_of(dom * own, own), own), :]


def last_kernel(
    rim,
    group,
    side,
    regions,
    fine_ref,
    rim_even,
    rim_odd,
    rim_dom,
    meta_even,
    meta_odd,
    meta_dom,
    coarse_mine,
    coarse_even,
    coarse_odd,
    coarse_even_two,
    coarse_odd_two,
    nbr_ref,
    mask_ref,
    parent_ref,
    share_ref,
    edge_ref,
    node_ref,
    bias_ref,
    out_ref,
):
    region = lax.axis_index("region")
    even = lax.rem(region, 2) == 0
    even_two = lax.rem(region // 2, 2) == 0
    count = fine_ref.shape[1]
    base = side + 8
    dom_base = group + 8 * (group // LANES)
    outer = rim_rows(
        rim,
        even,
        rim_even[base : base + rim, :],
        rim_odd[base : base + rim, :],
        rim_dom[dom_base : dom_base + 2 * rim, :],
    ).T
    facts = (
        meta_even[rim : rim + 8, :]
        + meta_odd[rim : rim + 8, :]
        + meta_dom[2 * rim : 2 * rim + 8, :]
    )
    known = iota((1, LANES), 1) < 4 * rim
    outer_parent = jnp.where(known, facts[0:1].astype(jnp.int32), -1)
    outer_share = jnp.where(known, facts[1:2], 0.0)
    parent = jnp.concatenate([parent_ref[...], outer_parent], axis=1)
    share = jnp.concatenate([share_ref[...].astype(f32), outer_share], axis=1)

    def found(block, home, index):
        chosen = hot(group, index - home * group).astype(bf16)
        stacked = jnp.concatenate(split(block[...]), axis=0)
        return folded(jnp.dot(stacked, chosen, preferred_element_type=f32))

    def shifted(steps):
        return lax.rem(region + steps + regions, regions)

    added = found(coarse_mine, region, parent)
    added = added + found(coarse_even, jnp.where(even, shifted(-1), shifted(1)), parent)
    added = added + found(coarse_odd, jnp.where(even, shifted(1), shifted(-1)), parent)
    far = found(coarse_even_two, jnp.where(even_two, shifted(-2), shifted(2)), outer_parent)
    far = far + found(coarse_odd_two, jnp.where(even_two, shifted(2), shifted(-2)), outer_parent)
    added = jnp.concatenate([added[:, :count], added[:, count:] + far], axis=1)
    sources = jnp.concatenate([fine_ref[...], outer], axis=1) + (share * 0.25) * added
    result = layer_columns(
        sources[:, :count], sources, nbr_ref, mask_ref, edge_ref, node_ref, bias_ref
    )
    out_ref[...] = result.T


def whole():
    return pl.BlockSpec(memory_space=pltpu.VMEM)


def scalars():
    return pl.BlockSpec(memory_space=pltpu.SMEM)


def layer_specs(layer, feature_dim):
    return [
        pl.BlockSpec((1, 3, feature_dim, feature_dim), lambda step: (layer, 0, 0, 0)),
        pl.BlockSpec((1, 3, feature_dim, feature_dim), lambda step: (layer, 0, 0, 0)),
        pl.BlockSpec((1, 4, feature_dim), lambda step: (layer, 0, 0)),
    ]


def kernel_call(body, in_specs, outs, scratch=()):
    return pl.pallas_call(
        body,
        grid=(1,),
        in_specs=in_specs,
        out_specs=tuple(whole() for _ in outs),
        out_shape=tuple(jax.ShapeDtypeStruct(shape, f32) for shape in outs),
        scratch_shapes=list(scratch),
        compiler_params=pltpu.CompilerParams(vmem_limit_bytes=VMEM_BYTES),
    )


def swap(value, axis, partner, count):
    return lax.ppermute(value, axis, [(source, partner(source) % count) for source in range(count)])


def body(
    fine_state,
    fine_nbr,
    fine_mask,
    send_rows,
    coarse_nbr,
    coarse_mask,
    parent,
    interp_share,
    edge_w,
    node_w,
    biases,
):
    count, width = fine_state.shape
    own_coarse = coarse_nbr.shape[1]
    slots = coarse_nbr.shape[0]
    regions = lax.axis_size("region")
    domains = lax.axis_size("dom")
    group = domains * own_coarse
    rim = send_rows.shape[1]
    side = count // (8 * domains)
    weights = (edge_w, node_w, biases)

    def even_swap(value):
        return swap(value, "region", lambda r: r - 1 if r % 2 == 0 else r + 1, regions)

    def odd_swap(value):
        return swap(value, "region", lambda r: r + 1 if r % 2 == 0 else r - 1, regions)

    def even_two_swap(value):
        return swap(value, "region", lambda r: r - 2 if r // 2 % 2 == 0 else r + 2, regions)

    def odd_two_swap(value):
        return swap(value, "region", lambda r: r + 2 if r // 2 % 2 == 0 else r - 2, regions)

    def dom_swap(value):
        return swap(value, "dom", lambda d: d + 1, domains)

    even_out, odd_out, dom_out = kernel_call(
        functools.partial(pick_kernel, rim),
        [scalars(), scalars(), scalars(), whole(), whole(), whole()],
        [(rim + 8, width), (rim + 8, width), (2 * rim + 8 + 2 * slots, width)],
    )(send_rows, parent, interp_share, fine_state, coarse_nbr, coarse_mask)
    meta_even = even_swap(even_out)
    meta_odd = odd_swap(odd_out)
    meta_dom = dom_swap(dom_out)

    parent_row = parent[None, :]
    share_row = interp_share[None, :]
    block_rows = side + 8 + rim + 8
    dom_rows = group + 8 * (group // LANES) + 2 * rim
    fine_one, even_out, odd_out, mine = kernel_call(
        functools.partial(fine_kernel, rim, group, side, regions),
        [scalars()] + [whole()] * 8 + layer_specs(0, width),
        [(width, count), (block_rows, width), (block_rows, width), (dom_rows, width)],
        [pltpu.VMEM((count, width), f32)],
    )(
        send_rows,
        fine_state,
        meta_even,
        meta_odd,
        meta_dom,
        fine_nbr,
        fine_mask,
        parent_row,
        share_row,
        *weights,
    )
    even_mine = even_swap(even_out)
    odd_mine = odd_swap(odd_out)
    other = dom_swap(mine)
    even_other = dom_swap(even_mine)
    odd_other = dom_swap(odd_mine)

    coarse_group, coarse_out = kernel_call(
        functools.partial(coarse_kernel, rim, group, side),
        [whole()] * 9 + layer_specs(1, width) + layer_specs(2, width),
        [(width, group), (own_coarse, width)],
        [pltpu.VMEM((group, width), f32)],
    )(
        mine,
        other,
        even_mine,
        odd_mine,
        even_other,
        odd_other,
        coarse_nbr,
        coarse_mask,
        meta_dom,
        *weights,
        *weights,
    )
    coarse_even = even_swap(coarse_group)
    coarse_even_two = even_two_swap(coarse_group)
    coarse_odd = odd_swap(coarse_group)
    coarse_odd_two = odd_two_swap(coarse_group)

    (fine_out,) = kernel_call(
        functools.partial(last_kernel, rim, group, side, regions),
        [whole()] * 16 + layer_specs(3, width),
        [(count, width)],
    )(
        fine_one,
        even_mine,
        odd_mine,
        other,
        meta_even,
        meta_odd,
        meta_dom,
        coarse_group,
        coarse_even,
        coarse_odd,
        coarse_even_two,
        coarse_odd_two,
        fine_nbr,
        fine_mask,
        parent_row,
        share_row,
        *weights,
    )
    return (fine_out, coarse_out)


def solution(mesh):
    return jax.shard_map(
        body,
        mesh=mesh,
        in_specs=(
            P(("region", "dom"), None),
            P(None, ("region", "dom")),
            P(None, ("region", "dom")),
            P(None, ("region", "dom")),
            P(None, ("region", "dom")),
            P(None, ("region", "dom")),
            P(("region", "dom")),
            P(("region", "dom")),
            P(),
            P(),
            P(),
        ),
        out_specs=(P(("region", "dom"), None), P(("region", "dom"), None)),
        check_vma=False,
    )
```

```python
import functools

import jax
import jax.numpy as jnp
from jax import lax
from jax.experimental import pallas as pl
from jax.experimental.pallas import tpu as pltpu
from jax.sharding import PartitionSpec as P

epsilon = 1e-05
f32 = jnp.float32
bf16 = jnp.bfloat16
LANES = 128
VMEM_BYTES = 32 * 2**20


def split(values):
    high = values.astype(bf16)
    low = (values - high.astype(f32)).astype(bf16)
    return high, low


def halves(weight):
    return jnp.concatenate(split(weight.T), axis=0)


def folded(stacked):
    half = stacked.shape[0] // 2
    return stacked[:half] + stacked[half:]


def times(factor, columns):
    stacked = jnp.concatenate(split(columns), axis=0)
    wide = jnp.concatenate([factor, factor], axis=1)
    return folded(jnp.dot(wide, stacked, preferred_element_type=f32))


def centered(weight):
    return weight - jnp.mean(weight, axis=-1, keepdims=True)


def bias_block(row):
    return jnp.broadcast_to(row, (LANES, row.shape[-1])).T


def spread_out(block, width):
    return jnp.concatenate([block] * (width // LANES), axis=1)


def scaled(columns):
    spread = jnp.mean(columns * columns, axis=0, keepdims=True)
    return columns * lax.rsqrt(spread + epsilon)


def iota(shape, axis):
    return lax.broadcasted_iota(jnp.int32, shape, axis)


def hot(rows, index):
    return (iota((rows, index.shape[1]), 0) == index).astype(f32)


def block_gather(block, index):
    features = block.shape[0]
    pieces = []
    for start in range(0, index.shape[1], LANES):
        wide = jnp.broadcast_to(index[:, start : start + LANES], (features, LANES))
        found = jnp.take_along_axis(block, wide & (LANES - 1), axis=1)
        pieces.append(jnp.where((wide >= 0) & (wide < LANES), found, 0.0))
    return jnp.concatenate(pieces, axis=1)


def hot_gather(stacked, index):
    chosen = hot(stacked.shape[1], index).astype(bf16)
    return folded(jnp.dot(stacked, chosen, preferred_element_type=f32))


def stacked_halves(columns):
    return jnp.concatenate(split(columns), axis=0)


def prepare(edge, node, bias, factors, columns):
    for place, weight in enumerate(
        (edge[0], edge[1], centered(edge[2]), node[0], node[1], centered(node[2]))
    ):
        factors[place] = halves(weight)
    for place in range(4):
        row = bias[place : place + 1]
        columns[place] = bias_block(centered(row) if place % 2 else row)


def edge_sum(own_term, gather, validity, factor, column):
    count = own_term.shape[1]
    second_bias = spread_out(column, count)
    total = jnp.zeros(own_term.shape, f32)
    for slot in range(validity.shape[0]):
        hidden = jnp.maximum(own_term + gather(slot), 0.0)
        message = times(factor, hidden) + second_bias
        spread = jnp.mean(message * message, axis=0, keepdims=True)
        valid = validity[slot : slot + 1, :].astype(f32)
        total = total + message * (lax.rsqrt(spread + epsilon) * valid)
    return total


def node_step(own, node_term, gathered, factors, columns):
    count = own.shape[1]
    inner_act = jnp.maximum(node_term + times(factors[4], gathered), 0.0)
    update = times(factors[5], inner_act) + spread_out(columns[3], count)
    return own + scaled(update)


def own_product(factors, columns, place, own):
    bias = spread_out(columns[0 if place == 0 else 2], own.shape[1])
    return times(factors[place], own) + bias


def fetch(copies, semaphores):
    started = []
    for place, (source, target) in enumerate(copies):
        copy = pltpu.make_async_copy(source, target, semaphores.at[place])
        copy.start()
        started.append(copy)
    return started


def pick_kernel(
    rim,
    send_hbm,
    parent_hbm,
    share_hbm,
    state_hbm,
    nbr_hbm,
    mask_hbm,
    even_ref,
    odd_ref,
    dom_ref,
    send_ref,
    parent_s,
    share_s,
    state_ref,
    nbr_ref,
    mask_ref,
    semaphores,
):
    copies = fetch(
        (
            (send_hbm, send_ref),
            (parent_hbm, parent_s),
            (share_hbm, share_s),
            (state_hbm, state_ref),
            (nbr_hbm, nbr_ref),
            (mask_hbm, mask_ref),
        ),
        semaphores,
    )
    for copy in copies:
        copy.wait()
    even = lax.rem(lax.axis_index("region"), 2) == 0
    first = jnp.where(even, 1, 0)
    lane = iota((1, LANES), 1)

    def fill(out, out_base, direction, lane_base, parents, shares):
        for k in range(rim):
            row = send_ref[direction, k]
            out[pl.ds(out_base + k, 1), :] = state_ref[pl.ds(row, 1), :]
            here = lane == lane_base + k
            parents = jnp.where(here, parent_s[row].astype(f32), parents)
            shares = jnp.where(here, share_s[row].astype(f32), shares)
        return parents, shares

    zero = jnp.zeros((1, LANES), f32)
    for out, direction in ((even_ref, first), (odd_ref, 1 - first)):
        parents, shares = fill(out, 0, direction, direction * rim, zero, zero)
        out[rim : rim + 8, :] = jnp.zeros((8, LANES), f32)
        out[rim : rim + 1, :] = parents
        out[rim + 1 : rim + 2, :] = shares
    parents, shares = fill(dom_ref, 0, 2, 2 * rim, zero, zero)
    parents, shares = fill(dom_ref, rim, 3, 3 * rim, parents, shares)
    base = 2 * rim
    dom_ref[base : base + 8, :] = jnp.zeros((8, LANES), f32)
    dom_ref[base : base + 1, :] = parents
    dom_ref[base + 1 : base + 2, :] = shares
    slots = nbr_ref.shape[0]
    dom_ref[base + 8 : base + 8 + slots, :] = nbr_ref[...].astype(f32)
    dom_ref[base + 8 + slots : base + 8 + 2 * slots, :] = mask_ref[...].astype(f32)


def rim_rows(rim, even, recv_even, recv_odd, recv_dom):
    low = jnp.where(even, recv_even, recv_odd)
    high = jnp.where(even, recv_odd, recv_even)
    pad = jnp.zeros((LANES - 4 * rim, low.shape[1]), f32)
    return jnp.concatenate([low, high, recv_dom, pad], axis=0)


def before_kernel(
    rim,
    group,
    side,
    regions,
    token_ref,
    state_hbm,
    nbr_hbm,
    mask_hbm,
    parent_hbm,
    share_hbm,
    edge_hbm,
    node_hbm,
    bias_hbm,
    own_ref,
    term_ref,
    node_term_ref,
    partial_ref,
    nbr_ref,
    valid_ref,
    factors,
    columns,
    pick_ref,
    place_ref,
    facts_ref,
    state_ref,
    mask_ref,
    parent_ref,
    share_ref,
    edge_ref,
    node_ref,
    bias_ref,
    semaphores,
):
    copies = fetch(
        (
            (state_hbm, state_ref),
            (edge_hbm.at[0], edge_ref),
            (bias_hbm.at[0], bias_ref),
            (node_hbm.at[0], node_ref),
            (nbr_hbm, nbr_ref),
            (parent_hbm, parent_ref),
            (share_hbm, share_ref),
            (mask_hbm, mask_ref),
        ),
        semaphores,
    )
    for copy in copies:
        copy.wait()
    own = state_ref[...].T
    own_ref[...] = own
    valid_ref[...] = mask_ref[...].astype(f32)
    prepare(edge_ref, node_ref, bias_ref, factors, columns)
    term_ref[...] = own_product(factors, columns, 0, own)
    node_term_ref[...] = own_product(factors, columns, 3, own)
    stacked = stacked_halves(times(factors[1], own))
    for slot in range(nbr_ref.shape[0]):
        partial_ref[slot] = hot_gather(stacked, nbr_ref[slot : slot + 1, :])
    parent = parent_ref[...]
    count = parent.shape[1]
    region = lax.axis_index("region")
    place = side_places(parent, region, regions, group, rim, side)
    place_ref[...] = jnp.broadcast_to(place, place_ref.shape)
    picked = hot(LANES, place)
    share = share_ref[...].astype(f32)
    facts = jnp.concatenate([parent.astype(f32), share, jnp.zeros((6, count), f32)], axis=0)
    facts_ref[...] = lax.dot_general(
        facts,
        picked,
        (((1,), (1,)), ((), ())),
        precision=lax.Precision.HIGHEST,
        preferred_element_type=f32,
    )
    pick_ref[...] = (picked[4 * rim : 4 * rim + 2 * side] * share).astype(bf16)


def weighted(selection, rows):
    pair = jnp.concatenate(split(rows), axis=1)
    both = jnp.dot(selection.astype(bf16), pair, preferred_element_type=f32)
    return both[:, :LANES] + both[:, LANES:]


def fine_kernel(
    rim,
    side,
    send_hbm,
    own_ref,
    term_ref,
    node_term_ref,
    partial_ref,
    nbr_ref,
    valid_ref,
    factors,
    columns,
    pick_ref,
    facts_ref,
    recv_even,
    recv_odd,
    recv_dom,
    fine_ref,
    rows_ref,
    even_ref,
    odd_ref,
    send_ref,
    semaphores,
):
    copies = fetch(((send_hbm, send_ref),), semaphores)
    even = lax.rem(lax.axis_index("region"), 2) == 0
    outer = rim_rows(rim, even, recv_even[:rim], recv_odd[:rim], recv_dom[: 2 * rim]).T
    block = times(factors[1], outer)
    count = own_ref.shape[1]

    def gather(slot):
        return partial_ref[slot] + block_gather(block, nbr_ref[slot : slot + 1, :] - count)

    gathered = edge_sum(term_ref[...], gather, valid_ref, factors[2], columns[1])
    fine = node_step(own_ref[...], node_term_ref[...], gathered, factors, columns)
    fine_ref[...] = fine
    rows = fine.T
    rows_ref[...] = rows
    late = weighted(pick_ref[...], rows)
    first = jnp.where(even, 1, 0)
    for copy in copies:
        copy.wait()
    for out, is_low in ((even_ref, even), (odd_ref, jnp.logical_not(even))):
        out[0:side, :] = jnp.where(is_low, late[:side], late[side:])
        out[side : side + 8, :] = facts_ref[...]
    for out, direction in ((even_ref, first), (odd_ref, 1 - first)):
        for k in range(rim):
            row = send_ref[direction, k]
            out[side + 8 + k : side + 9 + k, :] = rows_ref[pl.ds(row, 1), :]
        out[side + 8 + rim :, :] = jnp.zeros((out.shape[0] - side - 8 - rim, LANES), f32)


def side_places(parent, region, regions, group, rim, side):
    count = parent.shape[1]
    earlier = (iota((count, count), 0) < iota((count, count), 1)).astype(bf16)
    place = jnp.full(parent.shape, -1, jnp.int32)
    for number, steps in enumerate((regions - 1, 1)):
        local = parent - lax.rem(region + steps, regions) * group
        inside = (local >= 0) & (local < group)
        member = jnp.broadcast_to(jnp.where(inside, 1.0, 0.0), (8, count)).astype(bf16)
        rank = jnp.dot(member, earlier, preferred_element_type=f32)[0:1].astype(jnp.int32)
        place = jnp.where(inside, rank + (4 * rim + number * side), place)
    return place


def prepare_kernel(
    rim,
    group,
    token_ref,
    rows_ref,
    nbr_ref,
    place_ref,
    side_facts,
    meta_even,
    meta_odd,
    meta_dom,
    edge_hbm,
    node_hbm,
    bias_hbm,
    parent_hbm,
    share_hbm,
    send_hbm,
    coarse_nbr_hbm,
    coarse_mask_hbm,
    factors,
    columns,
    late_ref,
    mine_ref,
    group_nbr,
    group_valid,
    edge_ref,
    node_ref,
    bias_ref,
    parent_ref,
    share_ref,
    send_ref,
    coarse_nbr,
    coarse_mask,
    semaphores,
):
    copies = fetch(
        (
            (parent_hbm, parent_ref),
            (share_hbm, share_ref),
            (send_hbm, send_ref),
            (coarse_nbr_hbm, coarse_nbr),
            (coarse_mask_hbm, coarse_mask),
            (edge_hbm, edge_ref),
            (node_hbm, node_ref),
            (bias_hbm, bias_ref),
        ),
        semaphores,
    )
    index = nbr_ref[...]
    slots, count = index.shape
    for start in range(0, count, LANES):
        now = index[:, start : start + LANES]
        late = jnp.where(now >= count, now - count, -1)
        for base in range(0, count, LANES):
            table = jnp.broadcast_to(place_ref[0:1, base : base + LANES], (slots, LANES))
            inner = now - base
            found = jnp.take_along_axis(table, inner & (LANES - 1), axis=1)
            late = jnp.where((inner >= 0) & (inner < LANES), found, late)
        late_ref[:, start : start + LANES] = late
    for copy in copies:
        copy.wait()
    region = lax.axis_index("region")
    share = share_ref[...].astype(f32)
    chosen = hot(group, parent_ref[...] - region * group) * share
    mine_ref[0:group, :] = weighted(chosen, rows_ref[...])
    totals = lax.dot_general(
        jnp.ones((8, count), f32), chosen, (((1,), (1,)), ((), ())), preferred_element_type=f32
    )
    base = group
    for start in range(0, group, LANES):
        mine_ref[base : base + 8, :] = totals[:, start : start + LANES]
        base += 8
    for k in range(2 * rim):
        row = send_ref[2 + k // rim, k % rim]
        mine_ref[base + k : base + k + 1, :] = rows_ref[pl.ds(row, 1), :]
    base += 2 * rim
    facts = (
        meta_even[rim : rim + 8, :]
        + meta_odd[rim : rim + 8, :]
        + meta_dom[2 * rim : 2 * rim + 8, :]
    )
    rims = iota(facts.shape, 1) < 4 * rim
    mine_ref[base : base + 8, :] = jnp.where(rims, facts, side_facts[...])
    base = 2 * rim + 8
    mine_first = lax.axis_index("dom") == 0

    def ordered(mine, other):
        return jnp.concatenate(
            [jnp.where(mine_first, mine, other), jnp.where(mine_first, other, mine)], axis=1
        )

    group_nbr[...] = ordered(
        coarse_nbr[...], meta_dom[base : base + slots, :].astype(jnp.int32)
    )
    group_valid[...] = ordered(
        coarse_mask[...].astype(f32), meta_dom[base + slots : base + 2 * slots, :]
    )
    for layer in range(factors.shape[0]):
        prepare(
            edge_ref.at[layer + 1],
            node_ref.at[layer + 1],
            bias_ref.at[layer + 1],
            factors.at[layer],
            columns.at[layer],
        )


def gather_side_kernel(rim, group, side, regions, mine_ref, even_mine, odd_mine, sum_ref):
    region = lax.axis_index("region")
    total = mine_ref[0:group, :]
    base = group + 8 * (group // LANES)
    weight = [mine_ref[group + 8 * b : group + 8 * b + 8, :] for b in range(group // LANES)]
    weight = jnp.concatenate(weight, axis=1)
    for block in (even_mine, odd_mine):
        depth = block.shape[0]
        facts = block[side : side + 8, :]
        index = facts[0:1].astype(jnp.int32) - region * group
        chosen = hot(group, jnp.where(iota((1, LANES), 1) < 4 * rim, -1, index))
        weight = weight + lax.dot_general(
            jnp.broadcast_to(facts[1:2], (8, LANES)),
            chosen,
            (((1,), (1,)), ((), ())),
            preferred_element_type=f32,
        )
        rows = block[0:side, :]
        spread = jnp.concatenate(
            [jnp.zeros((4 * rim, LANES), f32), rows, rows]
            + [jnp.zeros((LANES - 4 * rim - 2 * side, LANES), f32)] * (LANES > 4 * rim + 2 * side),
            axis=0,
        )
        both = jnp.dot(
            chosen.astype(bf16),
            jnp.concatenate(split(spread), axis=1),
            preferred_element_type=f32,
        )
        total = total + (both[:, :LANES] + both[:, LANES:])
    sum_ref[0:group, :] = total
    for b in range(group // LANES):
        sum_ref[group + 8 * b : group + 8 * b + 8, :] = weight[:, b * LANES : (b + 1) * LANES]
    sum_ref[base:, :] = mine_ref[base:, :]


def coarse_layer(own, nbr, valid, factors, columns):
    term = own_product(factors, columns, 0, own)
    stacked = stacked_halves(times(factors[1], own))

    def gather(slot):
        return hot_gather(stacked, nbr[slot : slot + 1, :])

    gathered = edge_sum(term, gather, valid, factors[2], columns[1])
    return node_step(own, own_product(factors, columns, 3, own), gathered, factors, columns)


def coarse_kernel(
    group,
    mine_ref,
    other_ref,
    nbr_ref,
    valid_ref,
    factors,
    columns,
    group_ref,
    out_ref,
    rows_ref,
):
    dom = lax.axis_index("dom")
    total = mine_ref[0:group, :] + other_ref[0:group, :]
    weight = [
        mine_ref[group + 8 * b : group + 8 * b + 1, :]
        + other_ref[group + 8 * b : group + 8 * b + 1, :]
        for b in range(group // LANES)
    ]
    own = total.T / jnp.maximum(jnp.concatenate(weight, axis=1), 1.0)
    own = coarse_layer(own, nbr_ref, valid_ref, factors.at[0], columns.at[0])
    own = coarse_layer(own, nbr_ref, valid_ref, factors.at[1], columns.at[1])
    group_ref[...] = own
    rows_ref[...] = own.T
    rows = out_ref.shape[0]
    out_ref[...] = rows_ref[pl.ds(pl.multiple_of(dom * rows, rows), rows), :]


def between_kernel(
    rim,
    group,
    side,
    fine_ref,
    even_mine,
    odd_mine,
    mine_ref,
    other_ref,
    coarse_mine,
    nbr_ref,
    parent_hbm,
    share_hbm,
    factors,
    columns,
    own_ref,
    late_ref,
    partial_ref,
    parent_ref,
    share_ref,
    semaphores,
):
    copies = fetch(((parent_hbm, parent_ref), (share_hbm, share_ref)), semaphores)
    region = lax.axis_index("region")
    even = lax.rem(region, 2) == 0
    base = side + 8
    dom_base = group + 8 * (group // LANES)
    outer = rim_rows(
        rim,
        even,
        even_mine[base : base + rim, :],
        odd_mine[base : base + rim, :],
        other_ref[dom_base : dom_base + 2 * rim, :],
    ).T
    facts = mine_ref[dom_base + 2 * rim : dom_base + 2 * rim + 8, :]
    stacked = stacked_halves(coarse_mine[...])
    local = facts[0:1].astype(jnp.int32) - region * group
    late_ref[...] = outer + (facts[1:2] * 0.25) * hot_gather(stacked, local)
    for copy in copies:
        copy.wait()
    share = share_ref[...].astype(f32) * 0.25
    own = fine_ref[...] + share * hot_gather(stacked, parent_ref[...] - region * group)
    own_ref[...] = own
    stacked = stacked_halves(times(factors[2, 1], own))
    for slot in range(nbr_ref.shape[0]):
        partial_ref[slot] = hot_gather(stacked, nbr_ref[slot : slot + 1, :])


def side_kernel(
    rim, group, regions, late_in, mine_ref, other_ref, first_ref, second_ref, late_ref, back_ref
):
    region = lax.axis_index("region")
    near = lax.axis_index("dom") == 0
    base = group + 8 * (group // LANES) + 2 * rim
    facts = jnp.concatenate([mine_ref[base : base + 8, :], other_ref[base : base + 8, :]], axis=1)
    index = facts[0:1].astype(jnp.int32)

    def home(here, distance):
        below = (lax.rem(region // distance, 2) == 0) == here
        return lax.rem(region + jnp.where(below, regions - distance, distance), regions)

    late = None
    for block, here in ((first_ref, True), (second_ref, False)):
        place = jnp.where(near, home(here, 1), home(here, 2))
        found = hot_gather(stacked_halves(block[...]), index - place * group)
        late = found if late is None else late + found
    late = late * (facts[1:2] * 0.25)
    late_ref[...] = late_in[...] + late[:, :LANES]
    back_ref[...] = late[:, LANES:]


def last_kernel(
    own_ref,
    late_in,
    back_ref,
    partial_ref,
    late_index,
    place_ref,
    valid_ref,
    factors,
    columns,
    out_ref,
):
    late = late_in[...] + back_ref[...]
    own = own_ref[...] + block_gather(late, place_ref[0:1, :])
    factors = factors.at[2]
    columns = columns.at[2]
    block = times(factors[1], late)

    def gather(slot):
        return partial_ref[slot] + block_gather(block, late_index[slot : slot + 1, :])

    term = own_product(factors, columns, 0, own)
    gathered = edge_sum(term, gather, valid_ref, factors[2], columns[1])
    node_term = own_product(factors, columns, 3, own)
    out_ref[...] = node_step(own, node_term, gathered, factors, columns).T


def whole():
    return pl.BlockSpec(memory_space=pltpu.VMEM)


def far():
    return pl.BlockSpec(memory_space=pltpu.HBM)


def kept(value):
    return pltpu.with_memory_space_constraint(value, pltpu.HBM)


def scalars():
    return pl.BlockSpec(memory_space=pltpu.SMEM)


def kernel_call(body, in_specs, outs, scratch=(), copies=1, flops=0):
    outs = [(out, f32) if isinstance(out[0], int) else out for out in outs]
    return pl.pallas_call(
        body,
        in_specs=in_specs,
        out_specs=tuple(whole() for _ in outs),
        out_shape=tuple(jax.ShapeDtypeStruct(shape, kind) for shape, kind in outs),
        scratch_shapes=list(scratch) + [pltpu.SemaphoreType.DMA((copies,))] * (copies > 0),
        compiler_params=pltpu.CompilerParams(vmem_limit_bytes=VMEM_BYTES),
        cost_estimate=pl.CostEstimate(
            flops=flops, bytes_accessed=4 * 2**20, transcendentals=0
        ),
    )


def swap(value, axis, partner, count):
    return lax.ppermute(value, axis, [(source, partner(source) % count) for source in range(count)])


def body(
    fine_state,
    fine_nbr,
    fine_mask,
    send_rows,
    coarse_nbr,
    coarse_mask,
    parent,
    interp_share,
    edge_w,
    node_w,
    biases,
):
    count, width = fine_state.shape
    own_coarse = coarse_nbr.shape[1]
    slots = coarse_nbr.shape[0]
    regions = lax.axis_size("region")
    domains = lax.axis_size("dom")
    group = domains * own_coarse
    rim = send_rows.shape[1]
    side = count // (8 * domains)
    fine_state, fine_nbr, fine_mask, send_rows, coarse_nbr, coarse_mask = (
        kept(value)
        for value in (fine_state, fine_nbr, fine_mask, send_rows, coarse_nbr, coarse_mask)
    )
    parent_row = kept(parent[None, :])
    share_row = kept(interp_share[None, :])
    parent, interp_share = kept(parent), kept(interp_share)
    weights = (kept(edge_w), kept(node_w), kept(biases))
    i32 = jnp.int32

    def even_partner(r):
        return r - 1 if r % 2 == 0 else r + 1

    def odd_partner(r):
        return r + 1 if r % 2 == 0 else r - 1

    def even_two_partner(r):
        return r - 2 if r // 2 % 2 == 0 else r + 2

    def odd_two_partner(r):
        return r + 2 if r // 2 % 2 == 0 else r - 2

    def even_swap(value):
        return swap(value, "region", even_partner, regions)

    def odd_swap(value):
        return swap(value, "region", odd_partner, regions)

    def dom_swap(value):
        return swap(value, "dom", lambda d: d + 1, domains)

    def both_swap(value, near, distant):
        pairs = []
        for r in range(regions):
            for d in range(domains):
                target = (near(r) if d == 0 else distant(r)) % regions
                pairs.append((r * domains + d, target * domains + d))
        return lax.ppermute(value, ("region", "dom"), pairs)

    even_out, odd_out, dom_out = kernel_call(
        functools.partial(pick_kernel, rim),
        [far()] * 6,
        [(rim + 8, width), (rim + 8, width), (2 * rim + 8 + 2 * slots, width)],
        [
            pltpu.SMEM(send_rows.shape, i32),
            pltpu.SMEM(parent.shape, i32),
            pltpu.SMEM(interp_share.shape, i32),
            pltpu.VMEM(fine_state.shape, f32),
            pltpu.VMEM(coarse_nbr.shape, i32),
            pltpu.VMEM(coarse_mask.shape, i32),
        ],
        copies=6,
    )(send_rows, parent, interp_share, fine_state, coarse_nbr, coarse_mask)
    meta_even = even_swap(even_out)
    meta_odd = odd_swap(odd_out)
    meta_dom = dom_swap(dom_out)

    columns_shape = (width, count)
    weight_scratch = [
        pltpu.VMEM(edge_w.shape[1:], f32),
        pltpu.VMEM(node_w.shape[1:], f32),
        pltpu.VMEM(biases.shape[1:], f32),
    ]
    row_scratch = [pltpu.VMEM((1, count), i32), pltpu.VMEM((1, count), i32)]
    (
        own,
        term,
        node_term,
        partial,
        nbr,
        valid,
        factors,
        columns,
        pick,
        place,
        side_facts,
    ) = kernel_call(
        functools.partial(before_kernel, rim, group, side, regions),
        [whole()] + [far()] * 8,
        [
            columns_shape,
            columns_shape,
            columns_shape,
            (slots, width, count),
            (fine_nbr.shape, i32),
            fine_mask.shape,
            ((6, 2 * width, width), bf16),
            (4, width, LANES),
            ((2 * side, count), bf16),
            ((8, count), i32),
            (8, LANES),
        ],
        [pltpu.VMEM(fine_state.shape, f32), pltpu.VMEM(fine_mask.shape, i32)]
        + row_scratch
        + weight_scratch,
        copies=8,
        flops=4 * 10**9,
    )(even_out, fine_state, fine_nbr, fine_mask, parent_row, share_row, *weights)

    block_rows = side + 8 + rim + 8
    dom_rows = group + 8 * (group // LANES) + 2 * rim + 8
    fine_one, rows, even_out, odd_out = kernel_call(
        functools.partial(fine_kernel, rim, side),
        [far()] + [whole()] * 13,
        [columns_shape, (count, width), (block_rows, width), (block_rows, width)],
        [pltpu.SMEM(send_rows.shape, i32)],
    )(
        send_rows,
        own,
        term,
        node_term,
        partial,
        nbr,
        valid,
        factors,
        columns,
        pick,
        side_facts,
        meta_even,
        meta_odd,
        meta_dom,
    )
    even_mine = even_swap(even_out)
    odd_mine = odd_swap(odd_out)

    later = edge_w.shape[0] - 1
    factors, columns, late_index, mine, group_nbr, group_valid = kernel_call(
        functools.partial(prepare_kernel, rim, group),
        [whole()] * 8 + [far()] * 8,
        [
            ((later, 6, 2 * width, width), bf16),
            (later, 4, width, LANES),
            (fine_nbr.shape, i32),
            (dom_rows, width),
            ((slots, group), i32),
            (slots, group),
        ],
        [
            pltpu.VMEM(edge_w.shape, f32),
            pltpu.VMEM(node_w.shape, f32),
            pltpu.VMEM(biases.shape, f32),
        ]
        + row_scratch
        + [
            pltpu.SMEM(send_rows.shape, i32),
            pltpu.VMEM(coarse_nbr.shape, i32),
            pltpu.VMEM(coarse_mask.shape, i32),
        ],
        copies=8,
        flops=2 * 10**9,
    )(
        even_out,
        rows,
        nbr,
        place,
        side_facts,
        meta_even,
        meta_odd,
        meta_dom,
        *weights,
        parent_row,
        share_row,
        send_rows,
        coarse_nbr,
        coarse_mask,
    )
    (mine,) = kernel_call(
        functools.partial(gather_side_kernel, rim, group, side, regions),
        [whole()] * 3,
        [(dom_rows, width)],
        copies=0,
    )(mine, even_mine, odd_mine)
    other = dom_swap(mine)

    coarse_group, coarse_out = kernel_call(
        functools.partial(coarse_kernel, group),
        [whole()] * 6,
        [(width, group), (own_coarse, width)],
        [pltpu.VMEM((group, width), f32)],
        copies=0,
    )(mine, other, group_nbr, group_valid, factors, columns)
    first = both_swap(coarse_group, even_partner, even_two_partner)
    second = both_swap(coarse_group, odd_partner, odd_two_partner)

    own, late, partial = kernel_call(
        functools.partial(between_kernel, rim, group, side),
        [whole()] * 7 + [far()] * 2 + [whole()] * 2,
        [columns_shape, (width, LANES), (slots, width, count)],
        row_scratch,
        copies=2,
        flops=4 * 10**9,
    )(
        fine_one,
        even_mine,
        odd_mine,
        mine,
        other,
        coarse_group,
        nbr,
        parent_row,
        share_row,
        factors,
        columns,
    )
    late, back = kernel_call(
        functools.partial(side_kernel, rim, group, regions),
        [whole()] * 5,
        [(width, LANES), (width, LANES)],
        copies=0,
    )(late, mine, other, first, second)
    back = dom_swap(back)
    (fine_out,) = kernel_call(
        last_kernel, [whole()] * 9, [(count, width)], copies=0
    )(own, late, back, partial, late_index, place, valid, factors, columns)
    return (fine_out, coarse_out)


def solution(mesh):
    return jax.shard_map(
        body,
        mesh=mesh,
        in_specs=(
            P(("region", "dom"), None),
            P(None, ("region", "dom")),
            P(None, ("region", "dom")),
            P(None, ("region", "dom")),
            P(None, ("region", "dom")),
            P(None, ("region", "dom")),
            P(("region", "dom")),
            P(("region", "dom")),
            P(),
            P(),
            P(),
        ),
        out_specs=(P(("region", "dom"), None), P(("region", "dom"), None)),
        check_vma=False,
    )
```

```python
import functools

import jax
import jax.numpy as jnp
from jax import lax
from jax.experimental import pallas as pl
from jax.experimental.pallas import tpu as pltpu
from jax.sharding import PartitionSpec as P

epsilon = 1e-05
f32 = jnp.float32
bf16 = jnp.bfloat16
LANES = 128
WIDE = 512
VMEM_BYTES = 32 * 2**20


def split(values):
    high = values.astype(bf16)
    low = (values - high.astype(f32)).astype(bf16)
    return high, low


def halves(weight):
    return jnp.concatenate(split(weight.T), axis=0)


def folded(stacked):
    half = stacked.shape[0] // 2
    return stacked[:half] + stacked[half:]


def times(factor, columns):
    stacked = jnp.concatenate(split(columns), axis=0)
    wide = jnp.concatenate([factor, factor], axis=1)
    return folded(jnp.dot(wide, stacked, preferred_element_type=f32))


def centered(weight):
    return weight - jnp.mean(weight, axis=-1, keepdims=True)


def bias_block(row):
    return jnp.broadcast_to(row, (LANES, row.shape[-1])).T


def spread_out(block, width):
    return jnp.concatenate([block] * (width // LANES), axis=1)


def scaled(columns):
    spread = jnp.mean(columns * columns, axis=0, keepdims=True)
    return columns * lax.rsqrt(spread + epsilon)


def iota(shape, axis):
    return lax.broadcasted_iota(jnp.int32, shape, axis)


def hot(rows, index):
    return (iota((rows, index.shape[1]), 0) == index).astype(f32)


def block_gather(block, index):
    features = block.shape[0]
    pieces = []
    for start in range(0, index.shape[1], LANES):
        wide = jnp.broadcast_to(index[:, start : start + LANES], (features, LANES))
        found = jnp.take_along_axis(block, wide & (LANES - 1), axis=1)
        pieces.append(jnp.where((wide >= 0) & (wide < LANES), found, 0.0))
    return jnp.concatenate(pieces, axis=1)


def hot_gather(stacked, index):
    chosen = hot(stacked.shape[1], index).astype(bf16)
    return folded(jnp.dot(stacked, chosen, preferred_element_type=f32))


def stacked_halves(columns):
    return jnp.concatenate(split(columns), axis=0)


def prepare(edge, node, bias, factors, columns):
    for place, weight in enumerate(
        (edge[0], edge[1], centered(edge[2]), node[0], node[1], centered(node[2]))
    ):
        factors[place] = halves(weight)
    for place in range(4):
        row = bias[place : place + 1]
        columns[place] = bias_block(centered(row) if place % 2 else row)


def edge_sum(before, validity, factor, column):
    slots, count = validity.shape
    second_bias = spread_out(column, count)
    total = None
    for slot in range(slots):
        message = times(factor, jnp.maximum(before(slot), 0.0)) + second_bias
        spread = jnp.mean(message * message, axis=0, keepdims=True)
        message = message * (lax.rsqrt(spread + epsilon) * validity[slot : slot + 1, :])
        total = message if total is None else total + message
    return total


def node_step(own, node_term, gathered, factors, columns):
    count = own.shape[1]
    inner_act = jnp.maximum(node_term + times(factors[4], gathered), 0.0)
    update = times(factors[5], inner_act) + spread_out(columns[3], count)
    return own + scaled(update)


def own_products(factors, columns, places, own):
    stacked = stacked_halves(own)
    rows = [jnp.concatenate([factors[place]] * 2, axis=1) for place in places]
    both = jnp.dot(jnp.concatenate(rows, axis=0), stacked, preferred_element_type=f32)
    results = []
    for number, place in enumerate(places):
        rows = 2 * own.shape[0]
        result = folded(both[number * rows : (number + 1) * rows])
        if place in (0, 3):
            result = result + spread_out(columns[0 if place == 0 else 2], own.shape[1])
        results.append(result)
    return results


def pick_columns(columns, index):
    picked = None
    for start in range(0, columns.shape[1], LANES):
        block = columns[:, start : start + LANES]
        wide = jnp.broadcast_to(index - start, block.shape)
        found = jnp.take_along_axis(block, wide & (LANES - 1), axis=1)
        picked = found if picked is None else jnp.where(wide >= 0, found, picked)
    return picked


def wide_row(rows, first, number):
    return jnp.concatenate([rows[slot : slot + 1, :] for slot in range(first, first + number)], axis=1)


def fetch(copies, semaphores):
    started = []
    for place, (source, target) in enumerate(copies):
        copy = pltpu.make_async_copy(source, target, semaphores.at[place])
        copy.start()
        started.append(copy)
    return started


def pick_kernel(
    rim,
    send_hbm,
    parent_hbm,
    share_hbm,
    state_hbm,
    coarse_nbr_hbm,
    coarse_mask_hbm,
    parent_row_hbm,
    share_row_hbm,
    nbr_hbm,
    mask_hbm,
    edge_hbm,
    node_hbm,
    bias_hbm,
    even_ref,
    odd_ref,
    dom_ref,
    rows_ref,
    state_ref,
    parent_ref,
    share_ref,
    nbr_ref,
    mask_ref,
    edge_ref,
    node_ref,
    bias_ref,
    send_s,
    parent_s,
    share_s,
    coarse_nbr,
    coarse_mask,
    semaphores,
):
    copies = fetch(
        (
            (send_hbm, send_s),
            (parent_hbm, parent_s),
            (share_hbm, share_s),
            (state_hbm, state_ref),
            (coarse_nbr_hbm, coarse_nbr),
            (coarse_mask_hbm, coarse_mask),
            (nbr_hbm, nbr_ref),
            (parent_row_hbm, parent_ref),
            (share_row_hbm, share_ref),
            (edge_hbm.at[0], edge_ref),
            (node_hbm.at[0], node_ref),
            (bias_hbm.at[0], bias_ref),
            (mask_hbm, mask_ref),
        ),
        semaphores,
    )
    for copy in copies[:4]:
        copy.wait()
    even = lax.rem(lax.axis_index("region"), 2) == 0
    first = jnp.where(even, 1, 0)
    lane = iota((1, LANES), 1)

    def fill(out, out_base, direction, lane_base, facts):
        for k in range(rim):
            row = send_s[direction, k]
            out[pl.ds(out_base + k, 1), :] = state_ref[pl.ds(row, 1), :]
            here = lane == lane_base + k
            new = (parent_s[row], share_s[row], row)
            facts = [jnp.where(here, value, fact) for value, fact in zip(new, facts)]
        return facts

    def put(out, base, facts):
        out[base : base + 8, :] = jnp.zeros((8, LANES), f32)
        out[base : base + 1, :] = facts[0].astype(f32)
        out[base + 1 : base + 2, :] = facts[1].astype(f32)

    zero = jnp.zeros((1, LANES), jnp.int32)
    own_rows = zero
    for out, direction in ((even_ref, first), (odd_ref, 1 - first)):
        facts = fill(out, 0, direction, direction * rim, [zero] * 3)
        put(out, rim, facts)
        own_rows = own_rows + facts[2]
    facts = fill(dom_ref, 0, 2, 2 * rim, [zero] * 3)
    facts = fill(dom_ref, rim, 3, 3 * rim, facts)
    base = 2 * rim
    put(dom_ref, base, facts)
    rows_ref[...] = jnp.broadcast_to(own_rows + facts[2], rows_ref.shape)
    for copy in copies[4:]:
        copy.wait()
    slots = coarse_nbr.shape[0]
    dom_ref[base + 8 : base + 8 + slots, :] = coarse_nbr[...].astype(f32)
    dom_ref[base + 8 + slots : base + 8 + 2 * slots, :] = coarse_mask[...].astype(f32)


def rim_rows(rim, even, recv_even, recv_odd, recv_dom):
    low = jnp.where(even, recv_even, recv_odd)
    high = jnp.where(even, recv_odd, recv_even)
    pad = jnp.zeros((LANES - 4 * rim, low.shape[1]), f32)
    return jnp.concatenate([low, high, recv_dom, pad], axis=0)


def before_kernel(
    rim,
    group,
    side,
    regions,
    state_ref,
    rows_ref,
    parent_ref,
    share_ref,
    nbr_ref,
    mask_ref,
    edge_ref,
    node_ref,
    bias_ref,
    edge_hbm,
    node_hbm,
    bias_hbm,
    own_ref,
    node_term_ref,
    partial_ref,
    valid_ref,
    factors,
    columns,
    place_ref,
    facts_ref,
    own_first,
    node_term_first,
    partial_first,
    nbr_first,
    valid_first,
    later_edge,
    later_node,
    later_bias,
    semaphores,
):
    later = later_edge.shape[0]
    copies = fetch(
        (
            (edge_hbm.at[pl.ds(1, later)], later_edge),
            (node_hbm.at[pl.ds(1, later)], later_node),
            (bias_hbm.at[pl.ds(1, later)], later_bias),
        ),
        semaphores,
    )
    parent = parent_ref[...]
    count = parent.shape[1]
    region = lax.axis_index("region")
    place = side_places(parent, region, regions, group, rim, side)
    place_ref[...] = jnp.broadcast_to(place, place_ref.shape)
    facts = jnp.concatenate(
        [
            parent.astype(f32),
            share_ref[...].astype(f32),
            iota((1, count), 1).astype(f32),
            jnp.zeros((5, count), f32),
        ],
        axis=0,
    )
    facts = lax.dot_general(
        facts,
        hot(LANES, place),
        (((1,), (1,)), ((), ())),
        precision=lax.Precision.HIGHEST,
        preferred_element_type=f32,
    )
    facts_ref[...] = facts
    rims = iota((1, LANES), 1) < 4 * rim
    chosen = jnp.where(rims, rows_ref[0:1, :], facts[2:3].astype(jnp.int32))
    own = state_ref[...].T
    own_ref[...] = own
    valid = mask_ref[...].astype(f32)
    valid_ref[...] = valid
    prepare(edge_ref, node_ref, bias_ref, factors, columns)
    term, source, node_term = own_products(factors, columns, (0, 1, 3), own)
    node_term_ref[...] = node_term
    stacked = stacked_halves(source)
    slots = nbr_ref.shape[0]
    for slot in range(slots):
        partial_ref[slot] = term + hot_gather(stacked, nbr_ref[slot : slot + 1, :])
    own = pick_columns(own, chosen)
    own_first[...] = own
    term, node_term = own_products(factors, columns, (0, 3), own)
    node_term_first[...] = node_term
    valid_first[...] = pick_columns(valid, chosen)
    nbr = pick_columns(nbr_ref[...], chosen)
    nbr_first[...] = nbr
    together = WIDE // LANES
    for slot in range(0, slots, together):
        found = hot_gather(stacked, wide_row(nbr, slot, together))
        for number in range(together):
            partial_first[slot + number] = (
                term + found[:, number * LANES : (number + 1) * LANES]
            )
    for copy in copies:
        copy.wait()


def weighted(selection, rows):
    pair = jnp.concatenate(split(rows), axis=1)
    both = jnp.dot(selection.astype(bf16), pair, preferred_element_type=f32)
    return both[:, :LANES] + both[:, LANES:]


def first_kernel(
    rim,
    side,
    own_ref,
    node_term_ref,
    partial_ref,
    nbr_ref,
    valid_ref,
    count,
    factors,
    columns,
    facts_ref,
    recv_even,
    recv_odd,
    recv_dom,
    even_ref,
    odd_ref,
    dom_ref,
    block_ref,
):
    even = lax.rem(lax.axis_index("region"), 2) == 0
    outer = rim_rows(rim, even, recv_even[:rim], recv_odd[:rim], recv_dom[: 2 * rim]).T
    block = times(factors[1], outer)
    block_ref[...] = block

    def before(slot):
        return partial_ref[slot] + block_gather(block, nbr_ref[slot : slot + 1, :] - count)

    gathered = edge_sum(before, valid_ref, factors[2], columns[1])
    fine = node_step(own_ref[...], node_term_ref[...], gathered, factors, columns)
    rows = fine.T
    dom_ref[...] = rows[2 * rim : 4 * rim, :]
    late = (fine * facts_ref[1:2, :]).T
    low, high = late[4 * rim : 4 * rim + side], late[4 * rim + side : 4 * rim + 2 * side]
    up, down = rows[:rim], rows[rim : 2 * rim]
    for out, is_low in ((even_ref, even), (odd_ref, jnp.logical_not(even))):
        out[0:side, :] = jnp.where(is_low, low, high)
        out[side : side + 8, :] = facts_ref[...]
        out[side + 8 : side + 8 + rim, :] = jnp.where(is_low, down, up)
        out[side + 8 + rim :, :] = jnp.zeros((out.shape[0] - side - 8 - rim, LANES), f32)


def fine_kernel(
    rim,
    group,
    own_ref,
    node_term_ref,
    partial_ref,
    nbr_ref,
    valid_ref,
    factors,
    columns,
    block_ref,
    parent_ref,
    share_ref,
    dom_rows,
    side_facts,
    meta_even,
    meta_odd,
    meta_dom,
    fine_ref,
    mine_ref,
):
    block = block_ref[...]
    count = own_ref.shape[1]

    def before(slot):
        return partial_ref[slot] + block_gather(block, nbr_ref[slot : slot + 1, :] - count)

    gathered = edge_sum(before, valid_ref, factors[2], columns[1])
    fine = node_step(own_ref[...], node_term_ref[...], gathered, factors, columns)
    fine_ref[...] = fine
    region = lax.axis_index("region")
    share = share_ref[...].astype(f32)
    chosen = hot(group, parent_ref[...] - region * group) * share
    mine_ref[0:group, :] = weighted(chosen, fine.T)
    totals = lax.dot_general(
        jnp.ones((8, count), f32), chosen, (((1,), (1,)), ((), ())), preferred_element_type=f32
    )
    base = group
    for start in range(0, group, LANES):
        mine_ref[base : base + 8, :] = totals[:, start : start + LANES]
        base += 8
    mine_ref[base : base + 2 * rim, :] = dom_rows[...]
    base += 2 * rim
    facts = (
        meta_even[rim : rim + 8, :]
        + meta_odd[rim : rim + 8, :]
        + meta_dom[2 * rim : 2 * rim + 8, :]
    )
    rims = iota(facts.shape, 1) < 4 * rim
    mine_ref[base : base + 8, :] = jnp.where(rims, facts, side_facts[...])


def side_places(parent, region, regions, group, rim, side):
    count = parent.shape[1]
    earlier = (iota((count, count), 0) < iota((count, count), 1)).astype(bf16)
    place = jnp.full(parent.shape, -1, jnp.int32)
    for number, steps in enumerate((regions - 1, 1)):
        local = parent - lax.rem(region + steps, regions) * group
        inside = (local >= 0) & (local < group)
        member = jnp.broadcast_to(jnp.where(inside, 1.0, 0.0), (8, count)).astype(bf16)
        rank = jnp.dot(member, earlier, preferred_element_type=f32)[0:1].astype(jnp.int32)
        place = jnp.where(inside, rank + (4 * rim + number * side), place)
    return place


def prepare_kernel(
    rim,
    token_ref,
    sent_dom,
    meta_dom,
    edge_ref,
    node_ref,
    bias_ref,
    factors,
    columns,
    chosen_ref,
    valid_ref,
):
    slots, group = valid_ref.shape
    first = lax.axis_index("dom") == 0
    sent, received = sent_dom[2 * rim + 8 :, :], meta_dom[2 * rim + 8 :, :]
    tiles = jnp.concatenate(
        [jnp.where(first, sent, received), jnp.where(first, received, sent)], axis=1
    )
    valid_ref[...] = tiles[slots:]
    for slot in range(slots):
        chosen_ref[slot] = hot(group, tiles[slot : slot + 1].astype(jnp.int32)).astype(bf16)
    for layer in range(factors.shape[0]):
        prepare(
            edge_ref.at[layer],
            node_ref.at[layer],
            bias_ref.at[layer],
            factors.at[layer],
            columns.at[layer],
        )


def late_places(nbr_ref, place_ref, late_ref):
    index = nbr_ref[...]
    slots, count = index.shape
    for start in range(0, count, LANES):
        now = index[:, start : start + LANES]
        late = jnp.where(now >= count, now - count, -1)
        for base in range(0, count, LANES):
            table = jnp.broadcast_to(place_ref[0:1, base : base + LANES], (slots, LANES))
            inner = now - base
            found = jnp.take_along_axis(table, inner & (LANES - 1), axis=1)
            late = jnp.where((inner >= 0) & (inner < LANES), found, late)
        late_ref[:, start : start + LANES] = late


def gather_side_kernel(rim, group, side, regions, mine_ref, even_mine, odd_mine, sum_ref):
    region = lax.axis_index("region")
    total = mine_ref[0:group, :]
    base = group + 8 * (group // LANES)
    weight = [mine_ref[group + 8 * b : group + 8 * b + 8, :] for b in range(group // LANES)]
    weight = jnp.concatenate(weight, axis=1)
    for block in (even_mine, odd_mine):
        depth = block.shape[0]
        facts = block[side : side + 8, :]
        index = facts[0:1].astype(jnp.int32) - region * group
        chosen = hot(group, jnp.where(iota((1, LANES), 1) < 4 * rim, -1, index))
        weight = weight + lax.dot_general(
            jnp.broadcast_to(facts[1:2], (8, LANES)),
            chosen,
            (((1,), (1,)), ((), ())),
            preferred_element_type=f32,
        )
        rows = block[0:side, :]
        spread = jnp.concatenate(
            [jnp.zeros((4 * rim, LANES), f32), rows, rows]
            + [jnp.zeros((LANES - 4 * rim - 2 * side, LANES), f32)] * (LANES > 4 * rim + 2 * side),
            axis=0,
        )
        both = jnp.dot(
            chosen.astype(bf16),
            jnp.concatenate(split(spread), axis=1),
            preferred_element_type=f32,
        )
        total = total + (both[:, :LANES] + both[:, LANES:])
    sum_ref[0:group, :] = total
    for b in range(group // LANES):
        sum_ref[group + 8 * b : group + 8 * b + 8, :] = weight[:, b * LANES : (b + 1) * LANES]
    sum_ref[base:, :] = mine_ref[base:, :]


def coarse_layer(own, chosen, valid, factors, columns):
    (term,) = own_products(factors, columns, (0,), own)
    (node_term,) = own_products(factors, columns, (3,), own)
    stacked = stacked_halves(times(factors[1], own))
    found = jnp.dot(stacked, chosen, preferred_element_type=f32)
    count = own.shape[1]

    def before(slot):
        return folded(found[:, slot * count : (slot + 1) * count]) + term

    gathered = edge_sum(before, valid, factors[2], columns[1])
    return node_step(own, node_term, gathered, factors, columns)


def coarse_kernel(
    group,
    mine_ref,
    other_ref,
    chosen_ref,
    valid_ref,
    factors,
    columns,
    group_ref,
    out_ref,
    rows_ref,
):
    dom = lax.axis_index("dom")
    total = mine_ref[0:group, :] + other_ref[0:group, :]
    weight = [
        mine_ref[group + 8 * b : group + 8 * b + 1, :]
        + other_ref[group + 8 * b : group + 8 * b + 1, :]
        for b in range(group // LANES)
    ]
    own = total.T / jnp.maximum(jnp.concatenate(weight, axis=1), 1.0)
    chosen = jnp.concatenate([chosen_ref[slot] for slot in range(chosen_ref.shape[0])], axis=1)
    valid = valid_ref[...]
    own = coarse_layer(own, chosen, valid, factors.at[0], columns.at[0])
    own = coarse_layer(own, chosen, valid, factors.at[1], columns.at[1])
    group_ref[...] = own
    rows_ref[...] = own.T
    rows = out_ref.shape[0]
    out_ref[...] = rows_ref[pl.ds(pl.multiple_of(dom * rows, rows), rows), :]


def between_kernel(
    rim,
    group,
    side,
    fine_ref,
    even_mine,
    odd_mine,
    mine_ref,
    other_ref,
    coarse_mine,
    nbr_ref,
    place_ref,
    parent_ref,
    share_ref,
    edge_ref,
    node_ref,
    bias_ref,
    own_ref,
    late_ref,
    partial_ref,
    late_index,
    factors,
    columns,
):
    last = edge_ref.shape[0] - 1
    prepare(edge_ref.at[last], node_ref.at[last], bias_ref.at[last], factors, columns)
    region = lax.axis_index("region")
    even = lax.rem(region, 2) == 0
    base = side + 8
    dom_base = group + 8 * (group // LANES)
    outer = rim_rows(
        rim,
        even,
        even_mine[base : base + rim, :],
        odd_mine[base : base + rim, :],
        other_ref[dom_base : dom_base + 2 * rim, :],
    ).T
    facts = mine_ref[dom_base + 2 * rim : dom_base + 2 * rim + 8, :]
    stacked = stacked_halves(coarse_mine[...])
    local = facts[0:1].astype(jnp.int32) - region * group
    late_ref[...] = outer + (facts[1:2] * 0.25) * hot_gather(stacked, local)
    share = share_ref[...].astype(f32) * 0.25
    own = fine_ref[...] + share * hot_gather(stacked, parent_ref[...] - region * group)
    own_ref[...] = own
    stacked = stacked_halves(times(factors[1], own))
    for slot in range(nbr_ref.shape[0]):
        partial_ref[slot] = hot_gather(stacked, nbr_ref[slot : slot + 1, :])
    late_places(nbr_ref, place_ref, late_index)


def side_kernel(
    rim, group, regions, late_in, mine_ref, other_ref, first_ref, second_ref, late_ref, back_ref
):
    region = lax.axis_index("region")
    near = lax.axis_index("dom") == 0
    base = group + 8 * (group // LANES) + 2 * rim
    facts = jnp.concatenate([mine_ref[base : base + 8, :], other_ref[base : base + 8, :]], axis=1)
    index = facts[0:1].astype(jnp.int32)

    def home(here, distance):
        below = (lax.rem(region // distance, 2) == 0) == here
        return lax.rem(region + jnp.where(below, regions - distance, distance), regions)

    late = None
    for block, here in ((first_ref, True), (second_ref, False)):
        place = jnp.where(near, home(here, 1), home(here, 2))
        found = hot_gather(stacked_halves(block[...]), index - place * group)
        late = found if late is None else late + found
    late = late * (facts[1:2] * 0.25)
    late_ref[...] = late_in[...] + late[:, :LANES]
    back_ref[...] = late[:, LANES:]


def last_kernel(
    own_ref,
    late_in,
    back_ref,
    partial_ref,
    late_index,
    place_ref,
    valid_ref,
    factors,
    columns,
    out_ref,
):
    late = late_in[...] + back_ref[...]
    own = own_ref[...] + block_gather(late, place_ref[0:1, :])
    block = times(factors[1], late)
    term, node_term = own_products(factors, columns, (0, 3), own)

    def before(slot):
        return partial_ref[slot] + block_gather(block, late_index[slot : slot + 1, :]) + term

    gathered = edge_sum(before, valid_ref, factors[2], columns[1])
    out_ref[...] = node_step(own, node_term, gathered, factors, columns).T


def whole():
    return pl.BlockSpec(memory_space=pltpu.VMEM)


def far():
    return pl.BlockSpec(memory_space=pltpu.HBM)


def kept(value):
    return pltpu.with_memory_space_constraint(value, pltpu.HBM)


def scalars():
    return pl.BlockSpec(memory_space=pltpu.SMEM)


def kernel_call(body, in_specs, outs, scratch=(), copies=0, flops=0):
    outs = [(out, f32) if isinstance(out[0], int) else out for out in outs]
    return pl.pallas_call(
        body,
        in_specs=in_specs,
        out_specs=tuple(whole() for _ in outs),
        out_shape=tuple(jax.ShapeDtypeStruct(shape, kind) for shape, kind in outs),
        scratch_shapes=list(scratch) + [pltpu.SemaphoreType.DMA((copies,))] * (copies > 0),
        compiler_params=pltpu.CompilerParams(vmem_limit_bytes=VMEM_BYTES),
        cost_estimate=pl.CostEstimate(
            flops=flops, bytes_accessed=4 * 2**20, transcendentals=0
        ),
    )


def swap(value, axis, partner, count):
    return lax.ppermute(value, axis, [(source, partner(source) % count) for source in range(count)])


def body(
    fine_state,
    fine_nbr,
    fine_mask,
    send_rows,
    coarse_nbr,
    coarse_mask,
    parent,
    interp_share,
    edge_w,
    node_w,
    biases,
):
    count, width = fine_state.shape
    own_coarse = coarse_nbr.shape[1]
    slots = coarse_nbr.shape[0]
    regions = lax.axis_size("region")
    domains = lax.axis_size("dom")
    group = domains * own_coarse
    rim = send_rows.shape[1]
    side = count // (8 * domains)
    fine_state, fine_nbr, fine_mask, send_rows, coarse_nbr, coarse_mask = (
        kept(value)
        for value in (fine_state, fine_nbr, fine_mask, send_rows, coarse_nbr, coarse_mask)
    )
    parent_row = kept(parent[None, :])
    share_row = kept(interp_share[None, :])
    parent, interp_share = kept(parent), kept(interp_share)
    weights = (kept(edge_w), kept(node_w), kept(biases))
    i32 = jnp.int32

    def even_partner(r):
        return r - 1 if r % 2 == 0 else r + 1

    def odd_partner(r):
        return r + 1 if r % 2 == 0 else r - 1

    def even_two_partner(r):
        return r - 2 if r // 2 % 2 == 0 else r + 2

    def odd_two_partner(r):
        return r + 2 if r // 2 % 2 == 0 else r - 2

    def even_swap(value):
        return swap(value, "region", even_partner, regions)

    def odd_swap(value):
        return swap(value, "region", odd_partner, regions)

    def dom_swap(value):
        return swap(value, "dom", lambda d: d + 1, domains)

    def both_swap(value, near, distant):
        pairs = []
        for r in range(regions):
            for d in range(domains):
                target = (near(r) if d == 0 else distant(r)) % regions
                pairs.append((r * domains + d, target * domains + d))
        return lax.ppermute(value, ("region", "dom"), pairs)

    columns_shape = (width, count)
    row_shape = ((1, count), i32)
    fine_slots = (fine_nbr.shape, i32)
    (
        even_out,
        odd_out,
        dom_out,
        sent_rows,
        state,
        parents,
        shares,
        nbr,
        mask,
        edge_first,
        node_first,
        bias_first,
    ) = kernel_call(
        functools.partial(pick_kernel, rim),
        [far()] * 13,
        [
            (rim + 8, width),
            (rim + 8, width),
            (2 * rim + 8 + 2 * slots, width),
            ((8, LANES), i32),
            fine_state.shape,
            row_shape,
            row_shape,
            fine_slots,
            fine_slots,
            edge_w.shape[1:],
            node_w.shape[1:],
            biases.shape[1:],
        ],
        [
            pltpu.SMEM(send_rows.shape, i32),
            pltpu.SMEM(parent.shape, i32),
            pltpu.SMEM(interp_share.shape, i32),
            pltpu.VMEM(coarse_nbr.shape, i32),
            pltpu.VMEM(coarse_mask.shape, i32),
        ],
        copies=13,
    )(
        send_rows,
        parent,
        interp_share,
        fine_state,
        coarse_nbr,
        coarse_mask,
        parent_row,
        share_row,
        fine_nbr,
        fine_mask,
        *weights,
    )
    meta_even = even_swap(even_out)
    meta_odd = odd_swap(odd_out)
    meta_dom = dom_swap(dom_out)

    later = edge_w.shape[0] - 1
    (
        own,
        node_term,
        partial,
        valid,
        factors,
        columns,
        place,
        side_facts,
        own_some,
        node_term_some,
        partial_some,
        nbr_some,
        valid_some,
        edge_later,
        node_later,
        bias_later,
    ) = kernel_call(
        functools.partial(before_kernel, rim, group, side, regions),
        [whole()] * 9 + [far()] * 3,
        [
            columns_shape,
            columns_shape,
            (slots, width, count),
            fine_mask.shape,
            ((6, 2 * width, width), bf16),
            (4, width, LANES),
            ((8, count), i32),
            (8, LANES),
            (width, LANES),
            (width, LANES),
            (slots, width, LANES),
            ((slots, LANES), i32),
            (slots, LANES),
            (later,) + edge_w.shape[1:],
            (later,) + node_w.shape[1:],
            (later,) + biases.shape[1:],
        ],
        copies=3,
        flops=4 * 10**9,
    )(
        state,
        sent_rows,
        parents,
        shares,
        nbr,
        mask,
        edge_first,
        node_first,
        bias_first,
        *weights,
    )

    block_rows = side + 8 + rim + 8
    dom_rows = group + 8 * (group // LANES) + 2 * rim + 8

    def first_body(*refs):
        first_kernel(rim, side, *refs[:5], count, *refs[5:])

    even_out, odd_out, dom_some, block = kernel_call(
        first_body,
        [whole()] * 11,
        [(block_rows, width), (block_rows, width), (2 * rim, width), (width, LANES)],
    )(
        own_some,
        node_term_some,
        partial_some,
        nbr_some,
        valid_some,
        factors,
        columns,
        side_facts,
        meta_even,
        meta_odd,
        meta_dom,
    )
    even_mine = even_swap(even_out)
    odd_mine = odd_swap(odd_out)

    fine_one, mine = kernel_call(
        functools.partial(fine_kernel, rim, group),
        [whole()] * 15,
        [columns_shape, (dom_rows, width)],
        flops=4 * 10**9,
    )(
        own,
        node_term,
        partial,
        nbr,
        valid,
        factors,
        columns,
        block,
        parents,
        shares,
        dom_some,
        side_facts,
        meta_even,
        meta_odd,
        meta_dom,
    )
    (mine,) = kernel_call(
        functools.partial(gather_side_kernel, rim, group, side, regions),
        [whole()] * 3,
        [(dom_rows, width)],
    )(mine, even_mine, odd_mine)
    other = dom_swap(mine)

    factors, columns, group_chosen, group_valid = kernel_call(
        functools.partial(prepare_kernel, rim),
        [whole()] * 6,
        [
            ((later - 1, 6, 2 * width, width), bf16),
            (later - 1, 4, width, LANES),
            ((slots, group, group), bf16),
            (slots, group),
        ],
        flops=10**9,
    )(mine, dom_out, meta_dom, edge_later, node_later, bias_later)

    coarse_group, coarse_out = kernel_call(
        functools.partial(coarse_kernel, group),
        [whole()] * 6,
        [(width, group), (own_coarse, width)],
        [pltpu.VMEM((group, width), f32)],
    )(mine, other, group_chosen, group_valid, factors, columns)
    first = both_swap(coarse_group, even_partner, even_two_partner)
    second = both_swap(coarse_group, odd_partner, odd_two_partner)

    own, late, partial, late_index, factors, columns = kernel_call(
        functools.partial(between_kernel, rim, group, side),
        [whole()] * 13,
        [
            columns_shape,
            (width, LANES),
            (slots, width, count),
            fine_slots,
            ((6, 2 * width, width), bf16),
            (4, width, LANES),
        ],
        flops=4 * 10**9,
    )(
        fine_one,
        even_mine,
        odd_mine,
        mine,
        other,
        coarse_group,
        nbr,
        place,
        parents,
        shares,
        edge_later,
        node_later,
        bias_later,
    )
    late, back = kernel_call(
        functools.partial(side_kernel, rim, group, regions),
        [whole()] * 5,
        [(width, LANES), (width, LANES)],
    )(late, mine, other, first, second)
    back = dom_swap(back)
    (fine_out,) = kernel_call(last_kernel, [whole()] * 9, [(count, width)])(
        own, late, back, partial, late_index, place, valid, factors, columns
    )
    return (fine_out, coarse_out)


def solution(mesh):
    return jax.shard_map(
        body,
        mesh=mesh,
        in_specs=(
            P(("region", "dom"), None),
            P(None, ("region", "dom")),
            P(None, ("region", "dom")),
            P(None, ("region", "dom")),
            P(None, ("region", "dom")),
            P(None, ("region", "dom")),
            P(("region", "dom")),
            P(("region", "dom")),
            P(),
            P(),
            P(),
        ),
        out_specs=(P(("region", "dom"), None), P(("region", "dom"), None)),
        check_vma=False,
    )
```

```python
import functools

import jax
import jax.numpy as jnp
from jax import lax
from jax.experimental import pallas as pl
from jax.experimental.pallas import tpu as pltpu
from jax.sharding import PartitionSpec as P

epsilon = 1e-05
f32 = jnp.float32
bf16 = jnp.bfloat16
LANES = 128
WIDE = 512
VMEM_BYTES = 32 * 2**20


def split(values):
    high = values.astype(bf16)
    low = (values - high.astype(f32)).astype(bf16)
    return high, low


def halves(weight):
    return jnp.concatenate(split(weight.T), axis=0)


def folded(stacked):
    half = stacked.shape[0] // 2
    return stacked[:half] + stacked[half:]


def times(factor, columns):
    stacked = jnp.concatenate(split(columns), axis=0)
    wide = jnp.concatenate([factor, factor], axis=1)
    return folded(jnp.dot(wide, stacked, preferred_element_type=f32))


def centered(weight):
    return weight - jnp.mean(weight, axis=-1, keepdims=True)


def bias_block(row):
    return jnp.broadcast_to(row, (LANES, row.shape[-1])).T


def spread_out(block, width):
    return jnp.concatenate([block] * (width // LANES), axis=1)


def scaled(columns):
    spread = jnp.mean(columns * columns, axis=0, keepdims=True)
    return columns * lax.rsqrt(spread + epsilon)


def iota(shape, axis):
    return lax.broadcasted_iota(jnp.int32, shape, axis)


def hot(rows, index):
    return (iota((rows, index.shape[1]), 0) == index).astype(f32)


def block_gather(block, index):
    features = block.shape[0]
    pieces = []
    for start in range(0, index.shape[1], LANES):
        wide = jnp.broadcast_to(index[:, start : start + LANES], (features, LANES))
        found = jnp.take_along_axis(block, wide & (LANES - 1), axis=1)
        pieces.append(jnp.where((wide >= 0) & (wide < LANES), found, 0.0))
    return jnp.concatenate(pieces, axis=1)


def hot_gather(stacked, index):
    chosen = hot(stacked.shape[1], index).astype(bf16)
    return folded(jnp.dot(stacked, chosen, preferred_element_type=f32))


def stacked_halves(columns):
    return jnp.concatenate(split(columns), axis=0)


def prepare(edge, node, bias, factors, columns):
    for place, weight in enumerate(
        (edge[0], edge[1], centered(edge[2]), node[0], node[1], centered(node[2]))
    ):
        factors[place] = halves(weight)
    for place in range(4):
        row = bias[place : place + 1]
        columns[place] = bias_block(centered(row) if place % 2 else row)


def edge_sum(before, validity, factor, column):
    slots, count = validity.shape
    second_bias = spread_out(column, count)
    total = None
    for slot in range(slots):
        message = times(factor, jnp.maximum(before(slot), 0.0)) + second_bias
        spread = jnp.mean(message * message, axis=0, keepdims=True)
        message = message * (lax.rsqrt(spread + epsilon) * validity[slot : slot + 1, :])
        total = message if total is None else total + message
    return total


def node_step(own, node_term, gathered, factors, columns):
    count = own.shape[1]
    inner_act = jnp.maximum(node_term + times(factors[4], gathered), 0.0)
    update = times(factors[5], inner_act) + spread_out(columns[3], count)
    return own + scaled(update)


def own_products(factors, columns, places, own):
    stacked = stacked_halves(own)
    rows = [jnp.concatenate([factors[place]] * 2, axis=1) for place in places]
    both = jnp.dot(jnp.concatenate(rows, axis=0), stacked, preferred_element_type=f32)
    results = []
    for number, place in enumerate(places):
        rows = 2 * own.shape[0]
        result = folded(both[number * rows : (number + 1) * rows])
        if place in (0, 3):
            result = result + spread_out(columns[0 if place == 0 else 2], own.shape[1])
        results.append(result)
    return results


def pick_columns(columns, index):
    picked = None
    for start in range(0, columns.shape[1], LANES):
        block = columns[:, start : start + LANES]
        wide = jnp.broadcast_to(index - start, block.shape)
        found = jnp.take_along_axis(block, wide & (LANES - 1), axis=1)
        picked = found if picked is None else jnp.where(wide >= 0, found, picked)
    return picked


def wide_row(rows, first, number):
    return jnp.concatenate([rows[slot : slot + 1, :] for slot in range(first, first + number)], axis=1)


def fetch(copies, semaphores):
    started = []
    for place, (source, target) in enumerate(copies):
        copy = pltpu.make_async_copy(source, target, semaphores.at[place])
        copy.start()
        started.append(copy)
    return started


def pick_kernel(
    rim,
    send_hbm,
    state_hbm,
    coarse_nbr_hbm,
    coarse_mask_hbm,
    parent_hbm,
    share_hbm,
    nbr_hbm,
    mask_hbm,
    edge_hbm,
    node_hbm,
    bias_hbm,
    even_ref,
    odd_ref,
    dom_ref,
    rows_ref,
    state_ref,
    parent_ref,
    share_ref,
    nbr_ref,
    mask_ref,
    edge_ref,
    node_ref,
    bias_ref,
    send_s,
    coarse_nbr,
    coarse_mask,
    semaphores,
):
    copies = fetch(
        (
            (send_hbm, send_s),
            (state_hbm, state_ref),
            (coarse_nbr_hbm, coarse_nbr),
            (coarse_mask_hbm, coarse_mask),
            (edge_hbm.at[0], edge_ref),
            (node_hbm.at[0], node_ref),
            (nbr_hbm, nbr_ref),
            (parent_hbm, parent_ref),
            (share_hbm, share_ref),
            (bias_hbm.at[0], bias_ref),
            (mask_hbm, mask_ref),
        ),
        semaphores,
    )
    for copy in copies[:2]:
        copy.wait()
    even = lax.rem(lax.axis_index("region"), 2) == 0
    first = jnp.where(even, 1, 0)
    lane = iota((1, LANES), 1)

    def fill(out, out_base, direction, lane_base, rows):
        for k in range(rim):
            row = send_s[direction, k]
            out[pl.ds(out_base + k, 1), :] = state_ref[pl.ds(row, 1), :]
            rows = jnp.where(lane == lane_base + k, row, rows)
        return rows

    rows = fill(even_ref, 0, first, first * rim, jnp.zeros((1, LANES), jnp.int32))
    rows = fill(odd_ref, 0, 1 - first, (1 - first) * rim, rows)
    rows = fill(dom_ref, 0, 2, 2 * rim, rows)
    rows = fill(dom_ref, rim, 3, 3 * rim, rows)
    rows_ref[...] = jnp.broadcast_to(rows, rows_ref.shape)
    for copy in copies[2:]:
        copy.wait()
    slots = coarse_nbr.shape[0]
    base = 2 * rim
    dom_ref[base : base + slots, :] = coarse_nbr[...].astype(f32)
    dom_ref[base + slots : base + 2 * slots, :] = coarse_mask[...].astype(f32)


def rim_rows(rim, even, recv_even, recv_odd, recv_dom):
    low = jnp.where(even, recv_even, recv_odd)
    high = jnp.where(even, recv_odd, recv_even)
    pad = jnp.zeros((LANES - 4 * rim, low.shape[1]), f32)
    return jnp.concatenate([low, high, recv_dom, pad], axis=0)


def before_kernel(
    rim,
    group,
    side,
    regions,
    state_ref,
    rows_ref,
    parent_ref,
    share_ref,
    nbr_ref,
    mask_ref,
    edge_ref,
    node_ref,
    bias_ref,
    edge_hbm,
    node_hbm,
    bias_hbm,
    own_ref,
    node_term_ref,
    partial_ref,
    valid_ref,
    factors,
    columns,
    place_ref,
    facts_ref,
    own_first,
    node_term_first,
    partial_first,
    nbr_first,
    valid_first,
    later_edge,
    later_node,
    later_bias,
    semaphores,
):
    later = later_edge.shape[0]
    copies = fetch(
        (
            (edge_hbm.at[pl.ds(1, later)], later_edge),
            (node_hbm.at[pl.ds(1, later)], later_node),
            (bias_hbm.at[pl.ds(1, later)], later_bias),
        ),
        semaphores,
    )
    parent = parent_ref[...]
    count = parent.shape[1]
    region = lax.axis_index("region")
    place = side_places(parent, region, regions, group, rim, side)
    place_ref[...] = jnp.broadcast_to(place, place_ref.shape)
    numbers = lax.dot_general(
        jnp.broadcast_to(iota((1, count), 1).astype(f32), (8, count)),
        hot(LANES, place),
        (((1,), (1,)), ((), ())),
        precision=lax.Precision.HIGHEST,
        preferred_element_type=f32,
    )
    rims = iota((1, LANES), 1) < 4 * rim
    chosen = jnp.where(rims, rows_ref[0:1, :], numbers[0:1].astype(jnp.int32))
    facts = [parent.astype(f32), share_ref[...].astype(f32), place.astype(f32)]
    facts = jnp.concatenate(facts + [jnp.zeros((5, count), f32)], axis=0)
    facts_ref[...] = pick_columns(facts, chosen)
    own = state_ref[...].T
    own_ref[...] = own
    valid = mask_ref[...].astype(f32)
    valid_ref[...] = valid
    prepare(edge_ref, node_ref, bias_ref, factors, columns)
    term, source, node_term = own_products(factors, columns, (0, 1, 3), own)
    node_term_ref[...] = node_term
    stacked = stacked_halves(source)
    slots = nbr_ref.shape[0]
    for slot in range(slots):
        partial_ref[slot] = term + hot_gather(stacked, nbr_ref[slot : slot + 1, :])
    own = pick_columns(own, chosen)
    own_first[...] = own
    term, node_term = own_products(factors, columns, (0, 3), own)
    node_term_first[...] = node_term
    valid_first[...] = pick_columns(valid, chosen)
    nbr = pick_columns(nbr_ref[...], chosen)
    nbr_first[...] = nbr
    together = WIDE // LANES
    for slot in range(0, slots, together):
        found = hot_gather(stacked, wide_row(nbr, slot, together))
        for number in range(together):
            partial_first[slot + number] = (
                term + found[:, number * LANES : (number + 1) * LANES]
            )
    for copy in copies:
        copy.wait()


def weighted(selection, rows):
    pair = jnp.concatenate(split(rows), axis=1)
    both = jnp.dot(selection.astype(bf16), pair, preferred_element_type=f32)
    return both[:, :LANES] + both[:, LANES:]


def first_kernel(
    rim,
    side,
    own_ref,
    node_term_ref,
    partial_ref,
    nbr_ref,
    valid_ref,
    count,
    factors,
    columns,
    facts_ref,
    recv_even,
    recv_odd,
    recv_dom,
    even_ref,
    odd_ref,
    dom_ref,
    block_ref,
):
    even = lax.rem(lax.axis_index("region"), 2) == 0
    outer = rim_rows(rim, even, recv_even[:rim], recv_odd[:rim], recv_dom[: 2 * rim]).T
    block = times(factors[1], outer)
    block_ref[...] = block

    def before(slot):
        return partial_ref[slot] + block_gather(block, nbr_ref[slot : slot + 1, :] - count)

    gathered = edge_sum(before, valid_ref, factors[2], columns[1])
    fine = node_step(own_ref[...], node_term_ref[...], gathered, factors, columns)
    rows = fine.T
    dom_ref[...] = rows[2 * rim : 4 * rim, :]
    late = (fine * facts_ref[1:2, :]).T
    low, high = late[4 * rim : 4 * rim + side], late[4 * rim + side : 4 * rim + 2 * side]
    up, down = rows[:rim], rows[rim : 2 * rim]
    for out, is_low in ((even_ref, even), (odd_ref, jnp.logical_not(even))):
        out[0:side, :] = jnp.where(is_low, low, high)
        out[side : side + 8, :] = facts_ref[...]
        out[side + 8 : side + 8 + rim, :] = jnp.where(is_low, down, up)
        out[side + 8 + rim :, :] = jnp.zeros((out.shape[0] - side - 8 - rim, LANES), f32)


def fine_kernel(
    rim,
    group,
    own_ref,
    node_term_ref,
    partial_ref,
    nbr_ref,
    valid_ref,
    factors,
    columns,
    block_ref,
    parent_ref,
    share_ref,
    dom_rows,
    side_facts,
    fine_ref,
    mine_ref,
):
    block = block_ref[...]
    count = own_ref.shape[1]

    def before(slot):
        return partial_ref[slot] + block_gather(block, nbr_ref[slot : slot + 1, :] - count)

    gathered = edge_sum(before, valid_ref, factors[2], columns[1])
    fine = node_step(own_ref[...], node_term_ref[...], gathered, factors, columns)
    fine_ref[...] = fine
    region = lax.axis_index("region")
    share = share_ref[...].astype(f32)
    chosen = hot(group, parent_ref[...] - region * group) * share
    mine_ref[0:group, :] = weighted(chosen, fine.T)
    totals = lax.dot_general(
        jnp.ones((8, count), f32), chosen, (((1,), (1,)), ((), ())), preferred_element_type=f32
    )
    base = group
    for start in range(0, group, LANES):
        mine_ref[base : base + 8, :] = totals[:, start : start + LANES]
        base += 8
    mine_ref[base : base + 2 * rim, :] = dom_rows[...]
    base += 2 * rim
    mine_ref[base : base + 8, :] = side_facts[...]


def side_places(parent, region, regions, group, rim, side):
    count = parent.shape[1]
    earlier = (iota((count, count), 0) < iota((count, count), 1)).astype(bf16)
    place = jnp.full(parent.shape, -1, jnp.int32)
    for number, steps in enumerate((regions - 1, 1)):
        local = parent - lax.rem(region + steps, regions) * group
        inside = (local >= 0) & (local < group)
        member = jnp.broadcast_to(jnp.where(inside, 1.0, 0.0), (8, count)).astype(bf16)
        rank = jnp.dot(member, earlier, preferred_element_type=f32)[0:1].astype(jnp.int32)
        place = jnp.where(inside, rank + (4 * rim + number * side), place)
    return place


def prepare_kernel(
    rim,
    token_ref,
    sent_dom,
    meta_dom,
    edge_ref,
    node_ref,
    bias_ref,
    factors,
    columns,
    chosen_ref,
    valid_ref,
):
    slots, group = valid_ref.shape
    first = lax.axis_index("dom") == 0
    sent, received = sent_dom[2 * rim :, :], meta_dom[2 * rim :, :]
    tiles = jnp.concatenate(
        [jnp.where(first, sent, received), jnp.where(first, received, sent)], axis=1
    )
    valid_ref[...] = tiles[slots:]
    for slot in range(slots):
        chosen_ref[slot] = hot(group, tiles[slot : slot + 1].astype(jnp.int32)).astype(bf16)
    for layer in range(factors.shape[0]):
        prepare(
            edge_ref.at[layer],
            node_ref.at[layer],
            bias_ref.at[layer],
            factors.at[layer],
            columns.at[layer],
        )


def late_places(nbr_ref, place_ref, late_ref):
    index = nbr_ref[...]
    slots, count = index.shape
    for start in range(0, count, LANES):
        now = index[:, start : start + LANES]
        late = jnp.where(now >= count, now - count, -1)
        for base in range(0, count, LANES):
            table = jnp.broadcast_to(place_ref[0:1, base : base + LANES], (slots, LANES))
            inner = now - base
            found = jnp.take_along_axis(table, inner & (LANES - 1), axis=1)
            late = jnp.where((inner >= 0) & (inner < LANES), found, late)
        late_ref[:, start : start + LANES] = late


def gather_side_kernel(rim, group, side, regions, mine_ref, even_mine, odd_mine, sum_ref):
    region = lax.axis_index("region")
    total = mine_ref[0:group, :]
    base = group + 8 * (group // LANES)
    weight = [mine_ref[group + 8 * b : group + 8 * b + 8, :] for b in range(group // LANES)]
    weight = jnp.concatenate(weight, axis=1)
    for block in (even_mine, odd_mine):
        depth = block.shape[0]
        facts = block[side : side + 8, :]
        index = facts[0:1].astype(jnp.int32) - region * group
        chosen = hot(group, jnp.where(iota((1, LANES), 1) < 4 * rim, -1, index))
        weight = weight + lax.dot_general(
            jnp.broadcast_to(facts[1:2], (8, LANES)),
            chosen,
            (((1,), (1,)), ((), ())),
            preferred_element_type=f32,
        )
        rows = block[0:side, :]
        spread = jnp.concatenate(
            [jnp.zeros((4 * rim, LANES), f32), rows, rows]
            + [jnp.zeros((LANES - 4 * rim - 2 * side, LANES), f32)] * (LANES > 4 * rim + 2 * side),
            axis=0,
        )
        both = jnp.dot(
            chosen.astype(bf16),
            jnp.concatenate(split(spread), axis=1),
            preferred_element_type=f32,
        )
        total = total + (both[:, :LANES] + both[:, LANES:])
    sum_ref[0:group, :] = total
    for b in range(group // LANES):
        sum_ref[group + 8 * b : group + 8 * b + 8, :] = weight[:, b * LANES : (b + 1) * LANES]
    count = mine_ref.shape[0]
    sum_ref[base:count, :] = mine_ref[base:, :]
    even = lax.rem(region, 2) == 0
    below, above = even_mine[side : side + 8, :], odd_mine[side : side + 8, :]
    sum_ref[count : count + 8, :] = jnp.where(even, below, above)
    sum_ref[count + 8 : count + 16, :] = jnp.where(even, above, below)


def known_facts(group, rim, dom, mine_ref, other_ref):
    base = group + 8 * (group // LANES) + 2 * rim
    first = dom == 0
    facts = []
    for place in range(3):
        rows = slice(base + 8 * place, base + 8 * place + 8)
        mine, other = mine_ref[rows, :], other_ref[rows, :]
        facts.append((jnp.where(first, mine, other), jnp.where(first, other, mine)))
    return facts


def moved(rows, steps):
    index = (iota(rows.shape, 1) - steps) & (LANES - 1)
    return jnp.take_along_axis(rows, index, axis=1)


def first_is_below(region, near):
    return lax.rem(jnp.where(near, region, region // 2), 2) == 0


def asked_columns(rim, side, region, dom, facts):
    own, below, above = facts
    near = dom == 0
    lane = iota((8, LANES), 1)
    base = 4 * rim
    up = [jnp.where(near, mine, theirs) for mine, theirs in zip(own, above)]
    down = [jnp.where(near, mine, theirs) for mine, theirs in zip(own, below)]
    up_rims = jnp.where(lane < rim, up[0], moved(up[1], rim))
    down_rims = jnp.where(lane < rim, moved(down[0], -rim), down[1])
    up_sides = jnp.where(lane < base + side, above[0], moved(above[1], side))
    down_sides = jnp.where(lane < base + side, moved(below[0], -side), below[1])
    asked = []
    for rims, sides in ((up_rims, up_sides), (down_rims, down_sides)):
        sides = jnp.where((lane >= base) & near, sides, -1.0)
        asked.append(jnp.where(lane < 2 * rim, rims, sides)[0:1].astype(jnp.int32))
    first_below = first_is_below(region, near)
    up, down = asked
    return jnp.where(first_below, down, up), jnp.where(first_below, up, down)


def answer_lanes(rim, side, dom, core, place):
    lane = iota((1, LANES), 1)
    base = 4 * rim
    near = dom == 0
    second = core == 1
    from_dom = (lane >= 2 * rim) & (lane < base)
    low_place = (place >= base) & (place < base + side)
    low = jnp.where(lane < rim, lane + jnp.where(second, rim, 0), -1)
    high = jnp.where((lane >= rim) & (lane < 2 * rim), lane - jnp.where(second, 0, rim), -1)
    near_low = jnp.where(
        from_dom,
        jnp.where(low_place, place + jnp.where(second, 0, side), -1),
        jnp.where(
            (lane >= base) & (lane < base + side), lane + jnp.where(second, side, 0), low
        ),
    )
    near_high = jnp.where(
        from_dom,
        jnp.where(place >= base + side, place - jnp.where(second, side, 0), -1),
        jnp.where(lane >= base + side, lane - jnp.where(second, 0, side), high),
    )
    return jnp.where(near, near_low, low), jnp.where(near, near_high, high)


def coarse_layer(own, chosen, valid, factors, columns):
    (term,) = own_products(factors, columns, (0,), own)
    (node_term,) = own_products(factors, columns, (3,), own)
    stacked = stacked_halves(times(factors[1], own))
    found = jnp.dot(stacked, chosen, preferred_element_type=f32)
    count = own.shape[1]

    def before(slot):
        return folded(found[:, slot * count : (slot + 1) * count]) + term

    gathered = edge_sum(before, valid, factors[2], columns[1])
    return node_step(own, node_term, gathered, factors, columns)


def coarse_kernel(
    rim,
    group,
    side,
    mine_ref,
    other_ref,
    chosen_ref,
    valid_ref,
    factors,
    columns,
    group_ref,
    out_ref,
    first_ref,
    second_ref,
    rows_ref,
):
    region, dom = lax.axis_index("region"), lax.axis_index("dom")
    facts = known_facts(group, rim, dom, mine_ref, other_ref)
    asked = asked_columns(rim, side, region, dom, facts)
    asked = jnp.concatenate(asked, axis=1) - region * group
    total = mine_ref[0:group, :] + other_ref[0:group, :]
    weight = [
        mine_ref[group + 8 * b : group + 8 * b + 1, :]
        + other_ref[group + 8 * b : group + 8 * b + 1, :]
        for b in range(group // LANES)
    ]
    own = total.T / jnp.maximum(jnp.concatenate(weight, axis=1), 1.0)
    chosen = jnp.concatenate([chosen_ref[slot] for slot in range(chosen_ref.shape[0])], axis=1)
    valid = valid_ref[...]
    own = coarse_layer(own, chosen, valid, factors.at[0], columns.at[0])
    own = coarse_layer(own, chosen, valid, factors.at[1], columns.at[1])
    group_ref[...] = own
    answers = hot_gather(stacked_halves(own), asked)
    first_ref[...] = answers[:, :LANES]
    second_ref[...] = answers[:, LANES:]
    rows_ref[...] = own.T
    rows = out_ref.shape[0]
    out_ref[...] = rows_ref[pl.ds(pl.multiple_of(dom * rows, rows), rows), :]


def between_kernel(
    rim,
    group,
    side,
    fine_ref,
    even_mine,
    odd_mine,
    mine_ref,
    other_ref,
    coarse_mine,
    nbr_ref,
    place_ref,
    parent_ref,
    share_ref,
    edge_ref,
    node_ref,
    bias_ref,
    own_ref,
    late_ref,
    partial_ref,
    late_index,
    weight_ref,
    lanes_ref,
    factors,
    columns,
):
    last = edge_ref.shape[0] - 1
    prepare(edge_ref.at[last], node_ref.at[last], bias_ref.at[last], factors, columns)
    region = lax.axis_index("region")
    even = lax.rem(region, 2) == 0
    base = side + 8
    dom_base = group + 8 * (group // LANES)
    outer = rim_rows(
        rim,
        even,
        even_mine[base : base + rim, :],
        odd_mine[base : base + rim, :],
        other_ref[dom_base : dom_base + 2 * rim, :],
    ).T
    dom = lax.axis_index("dom")
    facts = known_facts(group, rim, dom, mine_ref, other_ref)
    own_facts, below, above = facts
    lane = iota((8, LANES), 1)
    late_facts = []
    for core in range(2):
        rims = jnp.where(lane < rim, below[core], above[core])
        sides = jnp.where(lane < 4 * rim, own_facts[1 - core], own_facts[core])
        late_facts.append(jnp.where(lane < 2 * rim, rims, sides))
    first = dom == 0
    mine = jnp.where(first, late_facts[0], late_facts[1])
    theirs = jnp.where(first, late_facts[1], late_facts[0])
    weight_ref[...] = jnp.concatenate([mine, theirs], axis=1) * 0.25
    places = [own_facts[1 - core][2:3].astype(jnp.int32) for core in range(2)]
    lanes = [
        answer_lanes(rim, side, dom, core, jnp.where(core == 0, places[0], places[1]))
        for core in (dom, 1 - dom)
    ]
    for row in range(2):
        pair = jnp.concatenate([lanes[0][row], lanes[1][row]], axis=1)
        lanes_ref[8 * row : 8 * row + 8, :] = jnp.broadcast_to(pair, (8, 2 * LANES))
    stacked = stacked_halves(coarse_mine[...])
    local = mine[0:1].astype(jnp.int32) - region * group
    late_ref[...] = outer + (mine[1:2] * 0.25) * hot_gather(stacked, local)
    share = share_ref[...].astype(f32) * 0.25
    own = fine_ref[...] + share * hot_gather(stacked, parent_ref[...] - region * group)
    own_ref[...] = own
    stacked = stacked_halves(times(factors[1], own))
    for slot in range(nbr_ref.shape[0]):
        partial_ref[slot] = hot_gather(stacked, nbr_ref[slot : slot + 1, :])
    late_places(nbr_ref, place_ref, late_index)


def side_kernel(weight_ref, lanes_ref, late_in, first_in, second_in, late_ref, back_ref):
    first_below = first_is_below(lax.axis_index("region"), lax.axis_index("dom") == 0)
    first, second = first_in[...], second_in[...]
    low, high = jnp.where(first_below, first, second), jnp.where(first_below, second, first)
    late = block_gather(low, lanes_ref[0:1, :]) + block_gather(high, lanes_ref[8:9, :])
    late = late * weight_ref[1:2, :]
    late_ref[...] = late_in[...] + late[:, :LANES]
    back_ref[...] = late[:, LANES:]


def last_kernel(
    own_ref,
    late_in,
    back_ref,
    partial_ref,
    late_index,
    place_ref,
    valid_ref,
    factors,
    columns,
    out_ref,
):
    late = late_in[...] + back_ref[...]
    own = own_ref[...] + block_gather(late, place_ref[0:1, :])
    block = times(factors[1], late)
    term, node_term = own_products(factors, columns, (0, 3), own)

    def before(slot):
        return partial_ref[slot] + block_gather(block, late_index[slot : slot + 1, :]) + term

    gathered = edge_sum(before, valid_ref, factors[2], columns[1])
    out_ref[...] = node_step(own, node_term, gathered, factors, columns).T


def whole():
    return pl.BlockSpec(memory_space=pltpu.VMEM)


def far():
    return pl.BlockSpec(memory_space=pltpu.HBM)


def kept(value):
    return pltpu.with_memory_space_constraint(value, pltpu.HBM)


def scalars():
    return pl.BlockSpec(memory_space=pltpu.SMEM)


def kernel_call(body, in_specs, outs, scratch=(), copies=0, flops=0):
    outs = [(out, f32) if isinstance(out[0], int) else out for out in outs]
    return pl.pallas_call(
        body,
        in_specs=in_specs,
        out_specs=tuple(whole() for _ in outs),
        out_shape=tuple(jax.ShapeDtypeStruct(shape, kind) for shape, kind in outs),
        scratch_shapes=list(scratch) + [pltpu.SemaphoreType.DMA((copies,))] * (copies > 0),
        compiler_params=pltpu.CompilerParams(vmem_limit_bytes=VMEM_BYTES),
        cost_estimate=pl.CostEstimate(
            flops=flops, bytes_accessed=4 * 2**20, transcendentals=0
        ),
    )


def swap(value, axis, partner, count):
    return lax.ppermute(value, axis, [(source, partner(source) % count) for source in range(count)])


def body(
    fine_state,
    fine_nbr,
    fine_mask,
    send_rows,
    coarse_nbr,
    coarse_mask,
    parent,
    interp_share,
    edge_w,
    node_w,
    biases,
):
    count, width = fine_state.shape
    own_coarse = coarse_nbr.shape[1]
    slots = coarse_nbr.shape[0]
    regions = lax.axis_size("region")
    domains = lax.axis_size("dom")
    group = domains * own_coarse
    rim = send_rows.shape[1]
    side = count // (8 * domains)
    fine_state, fine_nbr, fine_mask, send_rows, coarse_nbr, coarse_mask = (
        kept(value)
        for value in (fine_state, fine_nbr, fine_mask, send_rows, coarse_nbr, coarse_mask)
    )
    parent_row = kept(parent[None, :])
    share_row = kept(interp_share[None, :])
    weights = (kept(edge_w), kept(node_w), kept(biases))
    i32 = jnp.int32

    def even_partner(r):
        return r - 1 if r % 2 == 0 else r + 1

    def odd_partner(r):
        return r + 1 if r % 2 == 0 else r - 1

    def even_two_partner(r):
        return r - 2 if r // 2 % 2 == 0 else r + 2

    def odd_two_partner(r):
        return r + 2 if r // 2 % 2 == 0 else r - 2

    def even_swap(value):
        return swap(value, "region", even_partner, regions)

    def odd_swap(value):
        return swap(value, "region", odd_partner, regions)

    def dom_swap(value):
        return swap(value, "dom", lambda d: d + 1, domains)

    def both_swap(value, near, distant):
        pairs = []
        for r in range(regions):
            for d in range(domains):
                target = (near(r) if d == 0 else distant(r)) % regions
                pairs.append((r * domains + d, target * domains + d))
        return lax.ppermute(value, ("region", "dom"), pairs)

    columns_shape = (width, count)
    row_shape = ((1, count), i32)
    fine_slots = (fine_nbr.shape, i32)
    (
        even_out,
        odd_out,
        dom_out,
        sent_rows,
        state,
        parents,
        shares,
        nbr,
        mask,
        edge_first,
        node_first,
        bias_first,
    ) = kernel_call(
        functools.partial(pick_kernel, rim),
        [far()] * 11,
        [
            (rim, width),
            (rim, width),
            (2 * rim + 2 * slots, width),
            ((8, LANES), i32),
            fine_state.shape,
            row_shape,
            row_shape,
            fine_slots,
            fine_slots,
            edge_w.shape[1:],
            node_w.shape[1:],
            biases.shape[1:],
        ],
        [
            pltpu.SMEM(send_rows.shape, i32),
            pltpu.VMEM(coarse_nbr.shape, i32),
            pltpu.VMEM(coarse_mask.shape, i32),
        ],
        copies=11,
    )(
        send_rows,
        fine_state,
        coarse_nbr,
        coarse_mask,
        parent_row,
        share_row,
        fine_nbr,
        fine_mask,
        *weights,
    )
    meta_even = even_swap(even_out)
    meta_odd = odd_swap(odd_out)
    meta_dom = dom_swap(dom_out)

    later = edge_w.shape[0] - 1
    (
        own,
        node_term,
        partial,
        valid,
        factors,
        columns,
        place,
        side_facts,
        own_some,
        node_term_some,
        partial_some,
        nbr_some,
        valid_some,
        edge_later,
        node_later,
        bias_later,
    ) = kernel_call(
        functools.partial(before_kernel, rim, group, side, regions),
        [whole()] * 9 + [far()] * 3,
        [
            columns_shape,
            columns_shape,
            (slots, width, count),
            fine_mask.shape,
            ((6, 2 * width, width), bf16),
            (4, width, LANES),
            ((8, count), i32),
            (8, LANES),
            (width, LANES),
            (width, LANES),
            (slots, width, LANES),
            ((slots, LANES), i32),
            (slots, LANES),
            (later,) + edge_w.shape[1:],
            (later,) + node_w.shape[1:],
            (later,) + biases.shape[1:],
        ],
        copies=3,
        flops=4 * 10**9,
    )(
        state,
        sent_rows,
        parents,
        shares,
        nbr,
        mask,
        edge_first,
        node_first,
        bias_first,
        *weights,
    )

    block_rows = side + 8 + rim + 8
    dom_rows = group + 8 * (group // LANES) + 2 * rim + 8

    def first_body(*refs):
        first_kernel(rim, side, *refs[:5], count, *refs[5:])

    even_out, odd_out, dom_some, block = kernel_call(
        first_body,
        [whole()] * 11,
        [(block_rows, width), (block_rows, width), (2 * rim, width), (width, LANES)],
    )(
        own_some,
        node_term_some,
        partial_some,
        nbr_some,
        valid_some,
        factors,
        columns,
        side_facts,
        meta_even,
        meta_odd,
        meta_dom,
    )
    even_mine = even_swap(even_out)
    odd_mine = odd_swap(odd_out)

    fine_one, mine = kernel_call(
        functools.partial(fine_kernel, rim, group),
        [whole()] * 12,
        [columns_shape, (dom_rows, width)],
        flops=4 * 10**9,
    )(
        own,
        node_term,
        partial,
        nbr,
        valid,
        factors,
        columns,
        block,
        parents,
        shares,
        dom_some,
        side_facts,
    )
    (mine,) = kernel_call(
        functools.partial(gather_side_kernel, rim, group, side, regions),
        [whole()] * 3,
        [(dom_rows + 16, width)],
    )(mine, even_mine, odd_mine)
    other = dom_swap(mine)

    factors, columns, group_chosen, group_valid = kernel_call(
        functools.partial(prepare_kernel, rim),
        [whole()] * 6,
        [
            ((later - 1, 6, 2 * width, width), bf16),
            (later - 1, 4, width, LANES),
            ((slots, group, group), bf16),
            (slots, group),
        ],
        flops=10**9,
    )(mine, dom_out, meta_dom, edge_later, node_later, bias_later)

    coarse_group, coarse_out, first_out, second_out = kernel_call(
        functools.partial(coarse_kernel, rim, group, side),
        [whole()] * 6,
        [(width, group), (own_coarse, width), (width, LANES), (width, LANES)],
        [pltpu.VMEM((group, width), f32)],
    )(mine, other, group_chosen, group_valid, factors, columns)
    first = both_swap(first_out, even_partner, even_two_partner)
    second = both_swap(second_out, odd_partner, odd_two_partner)

    own, late, partial, late_index, weight, lanes, factors, columns = kernel_call(
        functools.partial(between_kernel, rim, group, side),
        [whole()] * 13,
        [
            columns_shape,
            (width, LANES),
            (slots, width, count),
            fine_slots,
            (8, 2 * LANES),
            ((16, 2 * LANES), i32),
            ((6, 2 * width, width), bf16),
            (4, width, LANES),
        ],
        flops=4 * 10**9,
    )(
        fine_one,
        even_mine,
        odd_mine,
        mine,
        other,
        coarse_group,
        nbr,
        place,
        parents,
        shares,
        edge_later,
        node_later,
        bias_later,
    )
    late, back = kernel_call(
        side_kernel, [whole()] * 5, [(width, LANES), (width, LANES)]
    )(weight, lanes, late, first, second)
    back = dom_swap(back)
    (fine_out,) = kernel_call(last_kernel, [whole()] * 9, [(count, width)])(
        own, late, back, partial, late_index, place, valid, factors, columns
    )
    return (fine_out, coarse_out)


def solution(mesh):
    return jax.shard_map(
        body,
        mesh=mesh,
        in_specs=(
            P(("region", "dom"), None),
            P(None, ("region", "dom")),
            P(None, ("region", "dom")),
            P(None, ("region", "dom")),
            P(None, ("region", "dom")),
            P(None, ("region", "dom")),
            P(("region", "dom")),
            P(("region", "dom")),
            P(),
            P(),
            P(),
        ),
        out_specs=(P(("region", "dom"), None), P(("region", "dom"), None)),
        check_vma=False,
    )
```

```python
import functools

import jax
import jax.numpy as jnp
from jax import lax
from jax.experimental import pallas as pl
from jax.experimental.pallas import tpu as pltpu
from jax.sharding import PartitionSpec as P

epsilon = 1e-05
f32 = jnp.float32
bf16 = jnp.bfloat16
LANES = 128
PARTS = 2
WIDE = 512
VMEM_BYTES = 32 * 2**20


def split(values):
    high = values.astype(bf16)
    low = (values - high.astype(f32)).astype(bf16)
    return high, low


def halves(weight):
    return jnp.concatenate(split(weight.T), axis=0)


def folded(stacked):
    half = stacked.shape[0] // 2
    return stacked[:half] + stacked[half:]


def times(factor, columns):
    stacked = jnp.concatenate(split(columns), axis=0)
    wide = jnp.concatenate([factor, factor], axis=1)
    return folded(jnp.dot(wide, stacked, preferred_element_type=f32))


def centered(weight):
    return weight - jnp.mean(weight, axis=-1, keepdims=True)


def bias_block(row):
    return jnp.broadcast_to(row, (LANES, row.shape[-1])).T


def spread_out(block, width):
    return jnp.concatenate([block] * (width // LANES), axis=1)


def scaled(columns):
    spread = jnp.mean(columns * columns, axis=0, keepdims=True)
    return columns * lax.rsqrt(spread + epsilon)


def iota(shape, axis):
    return lax.broadcasted_iota(jnp.int32, shape, axis)


def hot(rows, index):
    return (iota((rows, index.shape[1]), 0) == index).astype(f32)


def block_gather(block, index):
    features = block.shape[0]
    pieces = []
    for start in range(0, index.shape[1], LANES):
        wide = jnp.broadcast_to(index[:, start : start + LANES], (features, LANES))
        found = jnp.take_along_axis(block, wide & (LANES - 1), axis=1)
        pieces.append(jnp.where((wide >= 0) & (wide < LANES), found, 0.0))
    return jnp.concatenate(pieces, axis=1)


def hot_gather(stacked, index):
    chosen = hot(stacked.shape[1], index).astype(bf16)
    return folded(jnp.dot(stacked, chosen, preferred_element_type=f32))


def stacked_halves(columns):
    return jnp.concatenate(split(columns), axis=0)


def prepare(edge, node, bias, factors, columns):
    for place, weight in enumerate(
        (edge[0], edge[1], centered(edge[2]), node[0], node[1], centered(node[2]))
    ):
        factors[place] = halves(weight)
    for place in range(4):
        row = bias[place : place + 1]
        columns[place] = bias_block(centered(row) if place % 2 else row)


def edge_sum(before, validity, factor, column):
    slots, count = validity.shape
    second_bias = spread_out(column, count)
    total = None
    for slot in range(slots):
        message = times(factor, jnp.maximum(before(slot), 0.0)) + second_bias
        spread = jnp.mean(message * message, axis=0, keepdims=True)
        message = message * (lax.rsqrt(spread + epsilon) * validity[slot : slot + 1, :])
        total = message if total is None else total + message
    return total


def node_step(own, node_term, gathered, factors, columns):
    count = own.shape[1]
    inner_act = jnp.maximum(node_term + times(factors[4], gathered), 0.0)
    update = times(factors[5], inner_act) + spread_out(columns[3], count)
    return own + scaled(update)


def own_products(factors, columns, places, own):
    stacked = stacked_halves(own)
    rows = [jnp.concatenate([factors[place]] * 2, axis=1) for place in places]
    both = jnp.dot(jnp.concatenate(rows, axis=0), stacked, preferred_element_type=f32)
    results = []
    for number, place in enumerate(places):
        rows = 2 * own.shape[0]
        result = folded(both[number * rows : (number + 1) * rows])
        if place in (0, 3):
            result = result + spread_out(columns[0 if place == 0 else 2], own.shape[1])
        results.append(result)
    return results


def pick_columns(columns, index):
    picked = None
    for start in range(0, columns.shape[1], LANES):
        block = columns[:, start : start + LANES]
        wide = jnp.broadcast_to(index - start, block.shape)
        found = jnp.take_along_axis(block, wide & (LANES - 1), axis=1)
        picked = found if picked is None else jnp.where(wide >= 0, found, picked)
    return picked


def wide_row(rows, first, number):
    return jnp.concatenate([rows[slot : slot + 1, :] for slot in range(first, first + number)], axis=1)


def fetch(copies, semaphores):
    started = []
    for place, (source, target) in enumerate(copies):
        copy = pltpu.make_async_copy(source, target, semaphores.at[place])
        copy.start()
        started.append(copy)
    return started


def pick_kernel(
    rim,
    send_hbm,
    state_hbm,
    coarse_nbr_hbm,
    coarse_mask_hbm,
    parent_hbm,
    share_hbm,
    nbr_hbm,
    mask_hbm,
    edge_hbm,
    node_hbm,
    bias_hbm,
    even_ref,
    odd_ref,
    dom_ref,
    rows_ref,
    state_ref,
    parent_ref,
    share_ref,
    nbr_ref,
    mask_ref,
    edge_ref,
    node_ref,
    bias_ref,
    send_s,
    coarse_nbr,
    coarse_mask,
    semaphores,
):
    copies = fetch(
        (
            (send_hbm, send_s),
            (state_hbm, state_ref),
            (coarse_nbr_hbm, coarse_nbr),
            (coarse_mask_hbm, coarse_mask),
            (edge_hbm.at[0], edge_ref),
            (node_hbm.at[0], node_ref),
            (nbr_hbm, nbr_ref),
            (parent_hbm, parent_ref),
            (share_hbm, share_ref),
            (bias_hbm.at[0], bias_ref),
            (mask_hbm, mask_ref),
        ),
        semaphores,
    )
    for copy in copies[:2]:
        copy.wait()
    even = lax.rem(lax.axis_index("region"), 2) == 0
    first = jnp.where(even, 1, 0)
    lane = iota((1, LANES), 1)

    def fill(out, out_base, direction, lane_base, rows):
        for k in range(rim):
            row = send_s[direction, k]
            out[pl.ds(out_base + k, 1), :] = state_ref[pl.ds(row, 1), :]
            rows = jnp.where(lane == lane_base + k, row, rows)
        return rows

    rows = fill(even_ref, 0, first, first * rim, jnp.zeros((1, LANES), jnp.int32))
    rows = fill(odd_ref, 0, 1 - first, (1 - first) * rim, rows)
    rows = fill(dom_ref, 0, 2, 2 * rim, rows)
    rows = fill(dom_ref, rim, 3, 3 * rim, rows)
    rows_ref[...] = jnp.broadcast_to(rows, rows_ref.shape)
    for copy in copies[2:]:
        copy.wait()
    slots = coarse_nbr.shape[0]
    base = 2 * rim
    dom_ref[base : base + slots, :] = coarse_nbr[...].astype(f32)
    dom_ref[base + slots : base + 2 * slots, :] = coarse_mask[...].astype(f32)


def rim_rows(rim, even, recv_even, recv_odd, recv_dom):
    low = jnp.where(even, recv_even, recv_odd)
    high = jnp.where(even, recv_odd, recv_even)
    pad = jnp.zeros((LANES - 4 * rim, low.shape[1]), f32)
    return jnp.concatenate([low, high, recv_dom, pad], axis=0)


def before_kernel(
    rim,
    group,
    side,
    regions,
    state_ref,
    rows_ref,
    parent_ref,
    share_ref,
    nbr_ref,
    mask_ref,
    edge_ref,
    node_ref,
    bias_ref,
    edge_hbm,
    node_hbm,
    bias_hbm,
    own_ref,
    node_term_ref,
    partial_ref,
    valid_ref,
    factors,
    columns,
    place_ref,
    facts_ref,
    own_first,
    node_term_first,
    partial_first,
    nbr_first,
    valid_first,
    later_edge,
    later_node,
    later_bias,
    semaphores,
):
    later = later_edge.shape[0]
    copies = fetch(
        (
            (edge_hbm.at[pl.ds(1, later)], later_edge),
            (node_hbm.at[pl.ds(1, later)], later_node),
            (bias_hbm.at[pl.ds(1, later)], later_bias),
        ),
        semaphores,
    )
    parent = parent_ref[...]
    count = parent.shape[1]
    region = lax.axis_index("region")
    place = side_places(parent, region, regions, group, rim, side)
    place_ref[...] = jnp.broadcast_to(place, place_ref.shape)
    numbers = lax.dot_general(
        jnp.broadcast_to(iota((1, count), 1).astype(f32), (8, count)),
        hot(LANES, place),
        (((1,), (1,)), ((), ())),
        precision=lax.Precision.HIGHEST,
        preferred_element_type=f32,
    )
    rims = iota((1, LANES), 1) < 4 * rim
    chosen = jnp.where(rims, rows_ref[0:1, :], numbers[0:1].astype(jnp.int32))
    facts = [parent.astype(f32), share_ref[...].astype(f32), place.astype(f32)]
    facts = jnp.concatenate(facts + [jnp.zeros((5, count), f32)], axis=0)
    facts_ref[...] = pick_columns(facts, chosen)
    own = state_ref[...].T
    own_ref[...] = own
    valid = mask_ref[...].astype(f32)
    valid_ref[...] = valid
    prepare(edge_ref, node_ref, bias_ref, factors, columns)
    term, source, node_term = own_products(factors, columns, (0, 1, 3), own)
    node_term_ref[...] = node_term
    stacked = stacked_halves(source)
    slots = nbr_ref.shape[0]
    for slot in range(slots):
        partial_ref[slot] = term + hot_gather(stacked, nbr_ref[slot : slot + 1, :])
    own = pick_columns(own, chosen)
    own_first[...] = own
    term, node_term = own_products(factors, columns, (0, 3), own)
    node_term_first[...] = node_term
    valid_first[...] = pick_columns(valid, chosen)
    nbr = pick_columns(nbr_ref[...], chosen)
    nbr_first[...] = nbr
    together = WIDE // LANES
    for slot in range(0, slots, together):
        found = hot_gather(stacked, wide_row(nbr, slot, together))
        for number in range(together):
            partial_first[slot + number] = (
                term + found[:, number * LANES : (number + 1) * LANES]
            )
    for copy in copies:
        copy.wait()


def weighted(selection, rows):
    pair = jnp.concatenate(split(rows), axis=1)
    both = jnp.dot(selection.astype(bf16), pair, preferred_element_type=f32)
    return both[:, :LANES] + both[:, LANES:]


def first_kernel(
    rim,
    side,
    own_ref,
    node_term_ref,
    partial_ref,
    nbr_ref,
    valid_ref,
    count,
    factors,
    columns,
    facts_ref,
    recv_even,
    recv_odd,
    recv_dom,
    even_ref,
    odd_ref,
    dom_ref,
    block_ref,
):
    even = lax.rem(lax.axis_index("region"), 2) == 0
    outer = rim_rows(rim, even, recv_even[:rim], recv_odd[:rim], recv_dom[: 2 * rim]).T
    block = times(factors[1], outer)
    block_ref[...] = block

    def before(slot):
        return partial_ref[slot] + block_gather(block, nbr_ref[slot : slot + 1, :] - count)

    gathered = edge_sum(before, valid_ref, factors[2], columns[1])
    fine = node_step(own_ref[...], node_term_ref[...], gathered, factors, columns)
    rows = fine.T
    dom_ref[...] = rows[2 * rim : 4 * rim, :]
    late = (fine * facts_ref[1:2, :]).T
    low, high = late[4 * rim : 4 * rim + side], late[4 * rim + side : 4 * rim + 2 * side]
    up, down = rows[:rim], rows[rim : 2 * rim]
    for out, is_low in ((even_ref, even), (odd_ref, jnp.logical_not(even))):
        out[0:side, :] = jnp.where(is_low, low, high)
        out[side : side + 8, :] = facts_ref[...]
        out[side + 8 : side + 8 + rim, :] = jnp.where(is_low, down, up)
        out[side + 8 + rim :, :] = jnp.zeros((out.shape[0] - side - 8 - rim, LANES), f32)


def fine_kernel(
    rim,
    group,
    own_ref,
    node_term_ref,
    partial_ref,
    nbr_ref,
    valid_ref,
    factors,
    columns,
    block_ref,
    parent_ref,
    share_ref,
    dom_rows,
    side_facts,
    fine_ref,
    mine_ref,
):
    block = block_ref[...]
    count = own_ref.shape[1]

    def before(slot):
        return partial_ref[slot] + block_gather(block, nbr_ref[slot : slot + 1, :] - count)

    gathered = edge_sum(before, valid_ref, factors[2], columns[1])
    fine = node_step(own_ref[...], node_term_ref[...], gathered, factors, columns)
    fine_ref[...] = fine
    region = lax.axis_index("region")
    share = share_ref[...].astype(f32)
    chosen = hot(group, parent_ref[...] - region * group) * share
    mine_ref[0:group, :] = weighted(chosen, fine.T)
    totals = lax.dot_general(
        jnp.ones((8, count), f32), chosen, (((1,), (1,)), ((), ())), preferred_element_type=f32
    )
    base = group
    for start in range(0, group, LANES):
        mine_ref[base : base + 8, :] = totals[:, start : start + LANES]
        base += 8
    mine_ref[base : base + 2 * rim, :] = dom_rows[...]
    base += 2 * rim
    mine_ref[base : base + 8, :] = side_facts[...]


def side_places(parent, region, regions, group, rim, side):
    count = parent.shape[1]
    earlier = (iota((count, count), 0) < iota((count, count), 1)).astype(bf16)
    place = jnp.full(parent.shape, -1, jnp.int32)
    for number, steps in enumerate((regions - 1, 1)):
        local = parent - lax.rem(region + steps, regions) * group
        inside = (local >= 0) & (local < group)
        member = jnp.broadcast_to(jnp.where(inside, 1.0, 0.0), (8, count)).astype(bf16)
        rank = jnp.dot(member, earlier, preferred_element_type=f32)[0:1].astype(jnp.int32)
        place = jnp.where(inside, rank + (4 * rim + number * side), place)
    return place


def prepare_kernel(
    rim,
    token_ref,
    sent_dom,
    meta_dom,
    edge_ref,
    node_ref,
    bias_ref,
    factors,
    columns,
    chosen_ref,
    nbr_ref,
    valid_ref,
):
    slots, group = valid_ref.shape
    first = lax.axis_index("dom") == 0
    sent, received = sent_dom[2 * rim :, :], meta_dom[2 * rim :, :]
    tiles = jnp.concatenate(
        [jnp.where(first, sent, received), jnp.where(first, received, sent)], axis=1
    )
    valid_ref[...] = tiles[slots:]
    nbr = tiles[:slots].astype(jnp.int32)
    nbr_ref[...] = nbr
    for slot in range(slots):
        chosen_ref[slot] = hot(group, nbr[slot : slot + 1]).astype(bf16)
    for layer in range(factors.shape[0]):
        prepare(
            edge_ref.at[layer],
            node_ref.at[layer],
            bias_ref.at[layer],
            factors.at[layer],
            columns.at[layer],
        )


def late_places(nbr_ref, place_ref, late_ref):
    index = nbr_ref[...]
    slots, count = index.shape
    for start in range(0, count, LANES):
        now = index[:, start : start + LANES]
        late = jnp.where(now >= count, now - count, -1)
        for base in range(0, count, LANES):
            table = jnp.broadcast_to(place_ref[0:1, base : base + LANES], (slots, LANES))
            inner = now - base
            found = jnp.take_along_axis(table, inner & (LANES - 1), axis=1)
            late = jnp.where((inner >= 0) & (inner < LANES), found, late)
        late_ref[:, start : start + LANES] = late


def gather_side_kernel(rim, group, side, regions, mine_ref, even_mine, odd_mine, sum_ref):
    region = lax.axis_index("region")
    total = mine_ref[0:group, :]
    base = group + 8 * (group // LANES)
    weight = [mine_ref[group + 8 * b : group + 8 * b + 8, :] for b in range(group // LANES)]
    weight = jnp.concatenate(weight, axis=1)
    for block in (even_mine, odd_mine):
        depth = block.shape[0]
        facts = block[side : side + 8, :]
        index = facts[0:1].astype(jnp.int32) - region * group
        chosen = hot(group, jnp.where(iota((1, LANES), 1) < 4 * rim, -1, index))
        weight = weight + lax.dot_general(
            jnp.broadcast_to(facts[1:2], (8, LANES)),
            chosen,
            (((1,), (1,)), ((), ())),
            preferred_element_type=f32,
        )
        rows = block[0:side, :]
        spread = jnp.concatenate(
            [jnp.zeros((4 * rim, LANES), f32), rows, rows]
            + [jnp.zeros((LANES - 4 * rim - 2 * side, LANES), f32)] * (LANES > 4 * rim + 2 * side),
            axis=0,
        )
        both = jnp.dot(
            chosen.astype(bf16),
            jnp.concatenate(split(spread), axis=1),
            preferred_element_type=f32,
        )
        total = total + (both[:, :LANES] + both[:, LANES:])
    sum_ref[0:group, :] = total
    for b in range(group // LANES):
        sum_ref[group + 8 * b : group + 8 * b + 8, :] = weight[:, b * LANES : (b + 1) * LANES]
    count = mine_ref.shape[0]
    sum_ref[base:count, :] = mine_ref[base:, :]
    even = lax.rem(region, 2) == 0
    below, above = even_mine[side : side + 8, :], odd_mine[side : side + 8, :]
    sum_ref[count : count + 8, :] = jnp.where(even, below, above)
    sum_ref[count + 8 : count + 16, :] = jnp.where(even, above, below)


def known_facts(group, rim, dom, mine_ref, other_ref):
    base = group + 8 * (group // LANES) + 2 * rim
    first = dom == 0
    facts = []
    for place in range(3):
        rows = slice(base + 8 * place, base + 8 * place + 8)
        mine, other = mine_ref[rows, :], other_ref[rows, :]
        facts.append((jnp.where(first, mine, other), jnp.where(first, other, mine)))
    return facts


def moved(rows, steps):
    index = (iota(rows.shape, 1) - steps) & (LANES - 1)
    return jnp.take_along_axis(rows, index, axis=1)


def sides_below(region, dom):
    first = dom == 0
    near = (lax.rem(region, 2) == 0) == first
    far = (lax.rem(region // 2, 2) == 0) != first
    return near, far


def asked_columns(rim, side, region, dom, facts):
    own, below, above = facts
    near_below, far_below = sides_below(region, dom)
    lane = iota((8, LANES), 1)
    base = 4 * rim
    rims = jnp.where(
        near_below,
        jnp.where(lane < rim, moved(own[0], -rim), own[1]),
        jnp.where(lane < rim, own[0], moved(own[1], rim)),
    )
    beyond = jnp.where(
        far_below,
        jnp.where(lane < 3 * rim, moved(below[0], rim), moved(below[1], 2 * rim)),
        jnp.where(lane < 3 * rim, moved(above[0], 2 * rim), moved(above[1], 3 * rim)),
    )
    sides = jnp.where(
        near_below,
        jnp.where(lane < base + side, moved(below[0], -side), below[1]),
        jnp.where(lane < base + side, above[0], moved(above[1], side)),
    )
    asked = jnp.where(lane < 2 * rim, rims, jnp.where(lane < base, beyond, sides))
    return asked[0:1].astype(jnp.int32)


def answer_lanes(rim, side, region, dom, core, place):
    near_below, far_below = sides_below(region, dom)
    lane = iota((1, LANES), 1)
    base = 4 * rim
    second = core == 1
    skip = jnp.where(second, rim, 0)
    from_dom = (lane >= 2 * rim) & (lane < base)
    below_rim = lane < rim
    above_rim = (lane >= rim) & (lane < 2 * rim)
    low_place = (place >= base) & (place < base + side)
    low = jnp.where(
        from_dom,
        jnp.where(low_place, place + jnp.where(second, 0, side), -1),
        jnp.where(
            (lane >= base) & (lane < base + side),
            lane + jnp.where(second, side, 0),
            jnp.where(below_rim, lane + skip, -1),
        ),
    )
    high = jnp.where(
        from_dom,
        jnp.where(place >= base + side, place - jnp.where(second, side, 0), -1),
        jnp.where(
            lane >= base + side,
            lane - jnp.where(second, 0, side),
            jnp.where(above_rim, lane - rim + skip, -1),
        ),
    )
    far_low = jnp.where(below_rim, lane + 2 * rim + skip, -1)
    far_high = jnp.where(above_rim, lane + rim + skip, -1)
    return jnp.where(near_below, low, high), jnp.where(far_below, far_low, far_high)


def coarse_sources(own, factors):
    return stacked_halves(times(factors[1], own))


def coarse_layer(own, sources, chosen, valid, factors, columns):
    (term,) = own_products(factors, columns, (0,), own)
    (node_term,) = own_products(factors, columns, (3,), own)
    found = jnp.dot(sources, chosen, preferred_element_type=f32)
    count = own.shape[1]

    def before(slot):
        return folded(found[:, slot * count : (slot + 1) * count]) + term

    gathered = edge_sum(before, valid, factors[2], columns[1])
    return node_step(own, node_term, gathered, factors, columns)


def all_slots(chosen_ref):
    return jnp.concatenate([chosen_ref[slot] for slot in range(chosen_ref.shape[0])], axis=1)


def coarse_kernel(
    rim,
    group,
    side,
    mine_ref,
    other_ref,
    chosen_ref,
    nbr_ref,
    valid_ref,
    factors,
    columns,
    middle_ref,
    sources_ref,
    answer_ref,
):
    region, dom = lax.axis_index("region"), lax.axis_index("dom")
    facts = known_facts(group, rim, dom, mine_ref, other_ref)
    asked = asked_columns(rim, side, region, dom, facts) - region * group
    inside = (asked >= 0) & (asked < group)
    nbr = pick_columns(nbr_ref[...], asked)
    valid = pick_columns(valid_ref[...], asked)
    total = mine_ref[0:group, :] + other_ref[0:group, :]
    weight = [
        mine_ref[group + 8 * b : group + 8 * b + 1, :]
        + other_ref[group + 8 * b : group + 8 * b + 1, :]
        for b in range(group // LANES)
    ]
    own = total.T / jnp.maximum(jnp.concatenate(weight, axis=1), 1.0)
    sources = coarse_sources(own, factors.at[0])
    own = coarse_layer(
        own, sources, all_slots(chosen_ref), valid_ref[...], factors.at[0], columns.at[0]
    )
    middle_ref[...] = own
    sources = coarse_sources(own, factors.at[1])
    sources_ref[...] = sources
    chosen = hot(group, wide_row(nbr, 0, nbr.shape[0])).astype(bf16)
    some = pick_columns(own, asked)
    some = coarse_layer(some, sources, chosen, valid, factors.at[1], columns.at[1])
    answer_ref[...] = jnp.where(inside, some, 0.0)


def between_kernel(
    rim,
    group,
    side,
    fine_ref,
    even_mine,
    odd_mine,
    mine_ref,
    other_ref,
    middle_ref,
    sources_ref,
    chosen_ref,
    valid_ref,
    factors,
    columns,
    nbr_ref,
    parent_ref,
    share_ref,
    edge_ref,
    out_ref,
    own_ref,
    late_ref,
    partial_ref,
    weight_ref,
    lanes_ref,
    rows_ref,
    semaphores,
):
    coarse = coarse_layer(
        middle_ref[...],
        sources_ref[...],
        all_slots(chosen_ref),
        valid_ref[...],
        factors.at[1],
        columns.at[1],
    )
    rows_ref[...] = coarse.T
    rows = out_ref.shape[0]
    start = pl.multiple_of(lax.axis_index("dom") * rows, rows)
    copies = fetch(((rows_ref.at[pl.ds(start, rows)], out_ref),), semaphores)
    region = lax.axis_index("region")
    even = lax.rem(region, 2) == 0
    base = side + 8
    dom_base = group + 8 * (group // LANES)
    outer = rim_rows(
        rim,
        even,
        even_mine[base : base + rim, :],
        odd_mine[base : base + rim, :],
        other_ref[dom_base : dom_base + 2 * rim, :],
    ).T
    dom = lax.axis_index("dom")
    facts = known_facts(group, rim, dom, mine_ref, other_ref)
    own_facts, below, above = facts
    lane = iota((8, LANES), 1)
    late_facts = []
    for core in range(2):
        rims = jnp.where(lane < rim, below[core], above[core])
        sides = jnp.where(lane < 4 * rim, own_facts[1 - core], own_facts[core])
        late_facts.append(jnp.where(lane < 2 * rim, rims, sides))
    first = dom == 0
    mine = jnp.where(first, late_facts[0], late_facts[1])
    theirs = jnp.where(first, late_facts[1], late_facts[0])
    weight_ref[...] = jnp.concatenate([mine, theirs], axis=1) * 0.25
    places = [own_facts[1 - core][2:3].astype(jnp.int32) for core in range(2)]
    lanes = [
        answer_lanes(
            rim, side, region, dom, core, jnp.where(core == 0, places[0], places[1])
        )
        for core in (dom, 1 - dom)
    ]
    for row in range(2):
        pair = jnp.concatenate([lanes[0][row], lanes[1][row]], axis=1)
        lanes_ref[8 * row : 8 * row + 8, :] = jnp.broadcast_to(pair, (8, 2 * LANES))
    stacked = stacked_halves(coarse)
    local = mine[0:1].astype(jnp.int32) - region * group
    late_ref[...] = outer + (mine[1:2] * 0.25) * hot_gather(stacked, local)
    share = share_ref[...].astype(f32) * 0.25
    own = fine_ref[...] + share * hot_gather(stacked, parent_ref[...] - region * group)
    own_ref[...] = own
    stacked = stacked_halves(times(halves(edge_ref[edge_ref.shape[0] - 1, 1]), own))
    for slot in range(nbr_ref.shape[0]):
        partial_ref[slot] = hot_gather(stacked, nbr_ref[slot : slot + 1, :])
    for copy in copies:
        copy.wait()


def prepare_last_kernel(
    token_ref, nbr_ref, place_ref, edge_ref, node_ref, bias_ref, late_index, factors, columns
):
    last = edge_ref.shape[0] - 1
    prepare(edge_ref.at[last], node_ref.at[last], bias_ref.at[last], factors, columns)
    late_places(nbr_ref, place_ref, late_index)


def side_kernel(weight_ref, lanes_ref, late_in, first_in, second_in, late_ref, back_ref):
    first = lax.axis_index("dom") == 0
    near = jnp.where(first, first_in[...], second_in[...])
    far_rows = jnp.where(first, second_in[...], first_in[...])
    late = block_gather(near, lanes_ref[0:1, :]) + block_gather(far_rows, lanes_ref[8:9, :])
    late = late * weight_ref[1:2, :]
    late_ref[...] = late_in[...] + late[:, :LANES]
    back_ref[...] = late[:, LANES:]


def last_kernel(
    own_ref,
    late_in,
    back_ref,
    partial_ref,
    late_index,
    place_ref,
    valid_ref,
    factors,
    columns,
    out_ref,
    rows_ref,
    semaphores,
):
    late = late_in[...] + back_ref[...]
    own = own_ref[...] + block_gather(late, place_ref[0:1, :])
    block = times(factors[1], late)
    term, node_term = own_products(factors, columns, (0, 3), own)

    def before(slot):
        return partial_ref[slot] + block_gather(block, late_index[slot : slot + 1, :]) + term

    gathered = edge_sum(before, valid_ref, factors[2], columns[1])
    copies = []
    for place in range(PARTS):
        size = own.shape[1] // PARTS
        part = slice(place * size, (place + 1) * size)
        result = node_step(own[:, part], node_term[:, part], gathered[:, part], factors, columns)
        rows_ref[part, :] = result.T
        pair = (rows_ref.at[part], out_ref.at[part])
        copies += fetch((pair,), semaphores.at[pl.ds(place, 1)])
    for copy in copies:
        copy.wait()


def whole():
    return pl.BlockSpec(memory_space=pltpu.VMEM)


def far():
    return pl.BlockSpec(memory_space=pltpu.HBM)


def kept(value):
    return pltpu.with_memory_space_constraint(value, pltpu.HBM)


def scalars():
    return pl.BlockSpec(memory_space=pltpu.SMEM)


def kernel_call(body, in_specs, outs, scratch=(), copies=0, flops=0, sent=()):
    outs = [(out, f32) if isinstance(out[0], int) else out for out in outs]
    return pl.pallas_call(
        body,
        in_specs=in_specs,
        out_specs=tuple(far() if place in sent else whole() for place in range(len(outs))),
        out_shape=tuple(jax.ShapeDtypeStruct(shape, kind) for shape, kind in outs),
        scratch_shapes=list(scratch) + [pltpu.SemaphoreType.DMA((copies,))] * (copies > 0),
        compiler_params=pltpu.CompilerParams(vmem_limit_bytes=VMEM_BYTES),
        cost_estimate=pl.CostEstimate(
            flops=flops, bytes_accessed=4 * 2**20, transcendentals=0
        ),
    )


def swap(value, axis, partner, count):
    return lax.ppermute(value, axis, [(source, partner(source) % count) for source in range(count)])


def body(
    fine_state,
    fine_nbr,
    fine_mask,
    send_rows,
    coarse_nbr,
    coarse_mask,
    parent,
    interp_share,
    edge_w,
    node_w,
    biases,
):
    count, width = fine_state.shape
    own_coarse = coarse_nbr.shape[1]
    slots = coarse_nbr.shape[0]
    regions = lax.axis_size("region")
    domains = lax.axis_size("dom")
    group = domains * own_coarse
    rim = send_rows.shape[1]
    side = count // (8 * domains)
    fine_state, fine_nbr, fine_mask, send_rows, coarse_nbr, coarse_mask = (
        kept(value)
        for value in (fine_state, fine_nbr, fine_mask, send_rows, coarse_nbr, coarse_mask)
    )
    parent_row = kept(parent[None, :])
    share_row = kept(interp_share[None, :])
    weights = (kept(edge_w), kept(node_w), kept(biases))
    i32 = jnp.int32

    def even_partner(r):
        return r - 1 if r % 2 == 0 else r + 1

    def odd_partner(r):
        return r + 1 if r % 2 == 0 else r - 1

    def even_two_partner(r):
        return r - 2 if r // 2 % 2 == 0 else r + 2

    def odd_two_partner(r):
        return r + 2 if r // 2 % 2 == 0 else r - 2

    def even_swap(value):
        return swap(value, "region", even_partner, regions)

    def odd_swap(value):
        return swap(value, "region", odd_partner, regions)

    def dom_swap(value):
        return swap(value, "dom", lambda d: d + 1, domains)

    def both_swap(value, for_first, for_second):
        pairs = []
        for r in range(regions):
            for d in range(domains):
                target = (for_first(r) if d == 0 else for_second(r)) % regions
                pairs.append((r * domains + d, target * domains + d))
        return lax.ppermute(value, ("region", "dom"), pairs)

    columns_shape = (width, count)
    row_shape = ((1, count), i32)
    fine_slots = (fine_nbr.shape, i32)
    (
        even_out,
        odd_out,
        dom_out,
        sent_rows,
        state,
        parents,
        shares,
        nbr,
        mask,
        edge_first,
        node_first,
        bias_first,
    ) = kernel_call(
        functools.partial(pick_kernel, rim),
        [far()] * 11,
        [
            (rim, width),
            (rim, width),
            (2 * rim + 2 * slots, width),
            ((8, LANES), i32),
            fine_state.shape,
            row_shape,
            row_shape,
            fine_slots,
            fine_slots,
            edge_w.shape[1:],
            node_w.shape[1:],
            biases.shape[1:],
        ],
        [
            pltpu.SMEM(send_rows.shape, i32),
            pltpu.VMEM(coarse_nbr.shape, i32),
            pltpu.VMEM(coarse_mask.shape, i32),
        ],
        copies=11,
    )(
        send_rows,
        fine_state,
        coarse_nbr,
        coarse_mask,
        parent_row,
        share_row,
        fine_nbr,
        fine_mask,
        *weights,
    )
    meta_even = even_swap(even_out)
    meta_odd = odd_swap(odd_out)
    meta_dom = dom_swap(dom_out)

    later = edge_w.shape[0] - 1
    (
        own,
        node_term,
        partial,
        valid,
        factors,
        columns,
        place,
        side_facts,
        own_some,
        node_term_some,
        partial_some,
        nbr_some,
        valid_some,
        edge_later,
        node_later,
        bias_later,
    ) = kernel_call(
        functools.partial(before_kernel, rim, group, side, regions),
        [whole()] * 9 + [far()] * 3,
        [
            columns_shape,
            columns_shape,
            (slots, width, count),
            fine_mask.shape,
            ((6, 2 * width, width), bf16),
            (4, width, LANES),
            ((8, count), i32),
            (8, LANES),
            (width, LANES),
            (width, LANES),
            (slots, width, LANES),
            ((slots, LANES), i32),
            (slots, LANES),
            (later,) + edge_w.shape[1:],
            (later,) + node_w.shape[1:],
            (later,) + biases.shape[1:],
        ],
        copies=3,
        flops=4 * 10**9,
    )(
        state,
        sent_rows,
        parents,
        shares,
        nbr,
        mask,
        edge_first,
        node_first,
        bias_first,
        *weights,
    )

    block_rows = side + 8 + rim + 8
    dom_rows = group + 8 * (group // LANES) + 2 * rim + 8

    def first_body(*refs):
        first_kernel(rim, side, *refs[:5], count, *refs[5:])

    even_out, odd_out, dom_some, block = kernel_call(
        first_body,
        [whole()] * 11,
        [(block_rows, width), (block_rows, width), (2 * rim, width), (width, LANES)],
    )(
        own_some,
        node_term_some,
        partial_some,
        nbr_some,
        valid_some,
        factors,
        columns,
        side_facts,
        meta_even,
        meta_odd,
        meta_dom,
    )
    even_mine = even_swap(even_out)
    odd_mine = odd_swap(odd_out)

    fine_one, mine = kernel_call(
        functools.partial(fine_kernel, rim, group),
        [whole()] * 12,
        [columns_shape, (dom_rows, width)],
        flops=4 * 10**9,
    )(
        own,
        node_term,
        partial,
        nbr,
        valid,
        factors,
        columns,
        block,
        parents,
        shares,
        dom_some,
        side_facts,
    )
    (mine,) = kernel_call(
        functools.partial(gather_side_kernel, rim, group, side, regions),
        [whole()] * 3,
        [(dom_rows + 16, width)],
    )(mine, even_mine, odd_mine)
    other = dom_swap(mine)

    factors, columns, group_chosen, group_nbr, group_valid = kernel_call(
        functools.partial(prepare_kernel, rim),
        [whole()] * 6,
        [
            ((later - 1, 6, 2 * width, width), bf16),
            (later - 1, 4, width, LANES),
            ((slots, group, group), bf16),
            ((slots, group), i32),
            (slots, group),
        ],
        flops=10**9,
    )(mine, dom_out, meta_dom, edge_later, node_later, bias_later)

    middle, sources, answers = kernel_call(
        functools.partial(coarse_kernel, rim, group, side),
        [whole()] * 7,
        [(width, group), ((2 * width, group), bf16), (width, LANES)],
    )(mine, other, group_chosen, group_nbr, group_valid, factors, columns)
    first = both_swap(answers, even_partner, even_two_partner)
    second = both_swap(answers, odd_two_partner, odd_partner)

    coarse_out, own, late, partial, weight, lanes = kernel_call(
        functools.partial(between_kernel, rim, group, side),
        [whole()] * 15,
        [
            (own_coarse, width),
            columns_shape,
            (width, LANES),
            (slots, width, count),
            (8, 2 * LANES),
            ((16, 2 * LANES), i32),
        ],
        [pltpu.VMEM((group, width), f32)],
        copies=1,
        flops=8 * 10**9,
        sent=(0,),
    )(
        fine_one,
        even_mine,
        odd_mine,
        mine,
        other,
        middle,
        sources,
        group_chosen,
        group_valid,
        factors,
        columns,
        nbr,
        parents,
        shares,
        edge_later,
    )
    late, back = kernel_call(
        side_kernel, [whole()] * 5, [(width, LANES), (width, LANES)]
    )(weight, lanes, late, first, second)
    back_here = dom_swap(back)
    late_index, factors, columns = kernel_call(
        prepare_last_kernel,
        [whole()] * 6,
        [fine_slots, ((6, 2 * width, width), bf16), (4, width, LANES)],
        flops=10**9,
    )(back, nbr, place, edge_later, node_later, bias_later)
    (fine_out,) = kernel_call(
        last_kernel,
        [whole()] * 9,
        [(count, width)],
        [pltpu.VMEM((count, width), f32)],
        copies=PARTS,
        sent=(0,),
    )(
        own, late, back_here, partial, late_index, place, valid, factors, columns
    )
    return (fine_out, coarse_out)


def solution(mesh):
    return jax.shard_map(
        body,
        mesh=mesh,
        in_specs=(
            P(("region", "dom"), None),
            P(None, ("region", "dom")),
            P(None, ("region", "dom")),
            P(None, ("region", "dom")),
            P(None, ("region", "dom")),
            P(None, ("region", "dom")),
            P(("region", "dom")),
            P(("region", "dom")),
            P(),
            P(),
            P(),
        ),
        out_specs=(P(("region", "dom"), None), P(("region", "dom"), None)),
        check_vma=False,
    )
```

```python
import functools

import jax
import jax.numpy as jnp
from jax import lax
from jax.experimental import pallas as pl
from jax.experimental.pallas import tpu as pltpu
from jax.sharding import PartitionSpec as P

epsilon = 1e-05
f32 = jnp.float32
bf16 = jnp.bfloat16
LANES = 128
PARTS = 2
REST = 4
WIDE = 512
VMEM_BYTES = 32 * 2**20


def split(values):
    high = values.astype(bf16)
    low = (values - high.astype(f32)).astype(bf16)
    return high, low


def halves(weight):
    return jnp.concatenate(split(weight.T), axis=0)


def folded(stacked):
    half = stacked.shape[0] // 2
    return stacked[:half] + stacked[half:]


def times(factor, columns):
    stacked = jnp.concatenate(split(columns), axis=0)
    wide = jnp.concatenate([factor, factor], axis=1)
    return folded(jnp.dot(wide, stacked, preferred_element_type=f32))


def centered(weight):
    return weight - jnp.mean(weight, axis=-1, keepdims=True)


def bias_block(row):
    return jnp.broadcast_to(row, (LANES, row.shape[-1])).T


def spread_out(block, width):
    return jnp.concatenate([block] * (width // LANES), axis=1)


def scaled(columns):
    spread = jnp.mean(columns * columns, axis=0, keepdims=True)
    return columns * lax.rsqrt(spread + epsilon)


def iota(shape, axis):
    return lax.broadcasted_iota(jnp.int32, shape, axis)


def hot(rows, index):
    return (iota((rows, index.shape[1]), 0) == index).astype(f32)


def block_gather(block, index):
    features = block.shape[0]
    pieces = []
    for start in range(0, index.shape[1], LANES):
        wide = jnp.broadcast_to(index[:, start : start + LANES], (features, LANES))
        found = jnp.take_along_axis(block, wide & (LANES - 1), axis=1)
        pieces.append(jnp.where((wide >= 0) & (wide < LANES), found, 0.0))
    return jnp.concatenate(pieces, axis=1)


def hot_gather(stacked, index):
    chosen = hot(stacked.shape[1], index).astype(bf16)
    return folded(jnp.dot(stacked, chosen, preferred_element_type=f32))


def stacked_halves(columns):
    return jnp.concatenate(split(columns), axis=0)


def prepare(edge, node, bias, factors, columns):
    for place, weight in enumerate(
        (edge[0], edge[1], centered(edge[2]), node[0], node[1], centered(node[2]))
    ):
        factors[place] = halves(weight)
    for place in range(4):
        row = bias[place : place + 1]
        columns[place] = bias_block(centered(row) if place % 2 else row)


def edge_sum(before, validity, factor, column):
    slots, count = validity.shape
    second_bias = spread_out(column, count)
    total = None
    for slot in range(slots):
        message = times(factor, jnp.maximum(before(slot), 0.0)) + second_bias
        spread = jnp.mean(message * message, axis=0, keepdims=True)
        message = message * (lax.rsqrt(spread + epsilon) * validity[slot : slot + 1, :])
        total = message if total is None else total + message
    return total


def node_step(own, node_term, gathered, factors, columns):
    count = own.shape[1]
    inner_act = jnp.maximum(node_term + times(factors[4], gathered), 0.0)
    update = times(factors[5], inner_act) + spread_out(columns[3], count)
    return own + scaled(update)


def own_products(factors, columns, places, own):
    stacked = stacked_halves(own)
    rows = [jnp.concatenate([factors[place]] * 2, axis=1) for place in places]
    both = jnp.dot(jnp.concatenate(rows, axis=0), stacked, preferred_element_type=f32)
    results = []
    for number, place in enumerate(places):
        rows = 2 * own.shape[0]
        result = folded(both[number * rows : (number + 1) * rows])
        if place in (0, 3):
            result = result + spread_out(columns[0 if place == 0 else 2], own.shape[1])
        results.append(result)
    return results


def pick_columns(columns, index):
    picked = None
    for start in range(0, columns.shape[1], LANES):
        block = columns[:, start : start + LANES]
        wide = jnp.broadcast_to(index - start, block.shape)
        found = jnp.take_along_axis(block, wide & (LANES - 1), axis=1)
        picked = found if picked is None else jnp.where(wide >= 0, found, picked)
    return picked


def wide_row(rows, first, number):
    return jnp.concatenate([rows[slot : slot + 1, :] for slot in range(first, first + number)], axis=1)


def fetch(copies, semaphores):
    started = []
    for place, (source, target) in enumerate(copies):
        copy = pltpu.make_async_copy(source, target, semaphores.at[place])
        copy.start()
        started.append(copy)
    return started


def pick_kernel(
    rim,
    send_hbm,
    state_hbm,
    coarse_nbr_hbm,
    coarse_mask_hbm,
    parent_hbm,
    share_hbm,
    nbr_hbm,
    mask_hbm,
    edge_hbm,
    node_hbm,
    bias_hbm,
    even_ref,
    odd_ref,
    dom_ref,
    rows_ref,
    state_ref,
    parent_ref,
    share_ref,
    nbr_ref,
    mask_ref,
    edge_ref,
    node_ref,
    bias_ref,
    send_s,
    coarse_nbr,
    coarse_mask,
    semaphores,
):
    copies = fetch(
        (
            (send_hbm, send_s),
            (state_hbm, state_ref),
            (coarse_nbr_hbm, coarse_nbr),
            (coarse_mask_hbm, coarse_mask),
            (edge_hbm.at[0], edge_ref),
            (node_hbm.at[0], node_ref),
            (nbr_hbm, nbr_ref),
            (parent_hbm, parent_ref),
            (share_hbm, share_ref),
            (bias_hbm.at[0], bias_ref),
            (mask_hbm, mask_ref),
        ),
        semaphores,
    )
    for copy in copies[:2]:
        copy.wait()
    even = lax.rem(lax.axis_index("region"), 2) == 0
    first = jnp.where(even, 1, 0)
    lane = iota((1, LANES), 1)

    def fill(out, out_base, direction, lane_base, rows):
        for k in range(rim):
            row = send_s[direction, k]
            out[pl.ds(out_base + k, 1), :] = state_ref[pl.ds(row, 1), :]
            rows = jnp.where(lane == lane_base + k, row, rows)
        return rows

    rows = fill(even_ref, 0, first, first * rim, jnp.zeros((1, LANES), jnp.int32))
    rows = fill(odd_ref, 0, 1 - first, (1 - first) * rim, rows)
    rows = fill(dom_ref, 0, 2, 2 * rim, rows)
    rows = fill(dom_ref, rim, 3, 3 * rim, rows)
    rows_ref[...] = jnp.broadcast_to(rows, rows_ref.shape)
    for copy in copies[2:]:
        copy.wait()
    slots = coarse_nbr.shape[0]
    base = 2 * rim
    dom_ref[base : base + slots, :] = coarse_nbr[...].astype(f32)
    dom_ref[base + slots : base + 2 * slots, :] = coarse_mask[...].astype(f32)


def rim_rows(rim, even, recv_even, recv_odd, recv_dom):
    low = jnp.where(even, recv_even, recv_odd)
    high = jnp.where(even, recv_odd, recv_even)
    pad = jnp.zeros((LANES - 4 * rim, low.shape[1]), f32)
    return jnp.concatenate([low, high, recv_dom, pad], axis=0)


def before_kernel(
    rim,
    group,
    side,
    regions,
    state_ref,
    rows_ref,
    parent_ref,
    share_ref,
    nbr_ref,
    mask_ref,
    edge_ref,
    node_ref,
    bias_ref,
    edge_hbm,
    node_hbm,
    bias_hbm,
    own_ref,
    node_term_ref,
    partial_ref,
    valid_ref,
    factors,
    columns,
    place_ref,
    facts_ref,
    own_first,
    node_term_first,
    partial_first,
    nbr_first,
    valid_first,
    later_edge,
    later_node,
    later_bias,
    semaphores,
):
    later = later_edge.shape[0]
    copies = fetch(
        (
            (edge_hbm.at[pl.ds(1, later)], later_edge),
            (node_hbm.at[pl.ds(1, later)], later_node),
            (bias_hbm.at[pl.ds(1, later)], later_bias),
        ),
        semaphores,
    )
    parent = parent_ref[...]
    count = parent.shape[1]
    region = lax.axis_index("region")
    place = side_places(parent, region, regions, group, rim, side)
    place_ref[...] = jnp.broadcast_to(place, place_ref.shape)
    numbers = lax.dot_general(
        jnp.broadcast_to(iota((1, count), 1).astype(f32), (8, count)),
        hot(LANES, place),
        (((1,), (1,)), ((), ())),
        precision=lax.Precision.HIGHEST,
        preferred_element_type=f32,
    )
    rims = iota((1, LANES), 1) < 4 * rim
    chosen = jnp.where(rims, rows_ref[0:1, :], numbers[0:1].astype(jnp.int32))
    facts = [parent.astype(f32), share_ref[...].astype(f32), place.astype(f32)]
    facts = jnp.concatenate(facts + [jnp.zeros((5, count), f32)], axis=0)
    facts_ref[...] = pick_columns(facts, chosen)
    own = state_ref[...].T
    own_ref[...] = own
    valid = mask_ref[...].astype(f32)
    valid_ref[...] = valid
    prepare(edge_ref, node_ref, bias_ref, factors, columns)
    term, source, node_term = own_products(factors, columns, (0, 1, 3), own)
    node_term_ref[...] = node_term
    stacked = stacked_halves(source)
    slots = nbr_ref.shape[0]
    for slot in range(slots):
        partial_ref[slot] = term + hot_gather(stacked, nbr_ref[slot : slot + 1, :])
    own = pick_columns(own, chosen)
    own_first[...] = own
    term, node_term = own_products(factors, columns, (0, 3), own)
    node_term_first[...] = node_term
    valid_first[...] = pick_columns(valid, chosen)
    nbr = pick_columns(nbr_ref[...], chosen)
    nbr_first[...] = nbr
    together = WIDE // LANES
    for slot in range(0, slots, together):
        found = hot_gather(stacked, wide_row(nbr, slot, together))
        for number in range(together):
            partial_first[slot + number] = (
                term + found[:, number * LANES : (number + 1) * LANES]
            )
    for copy in copies:
        copy.wait()


def weighted(selection, rows):
    pair = jnp.concatenate(split(rows), axis=1)
    both = jnp.dot(selection.astype(bf16), pair, preferred_element_type=f32)
    return both[:, :LANES] + both[:, LANES:]


def first_kernel(
    rim,
    side,
    own_ref,
    node_term_ref,
    partial_ref,
    nbr_ref,
    valid_ref,
    count,
    factors,
    columns,
    facts_ref,
    recv_even,
    recv_odd,
    recv_dom,
    even_ref,
    odd_ref,
    dom_ref,
    block_ref,
):
    even = lax.rem(lax.axis_index("region"), 2) == 0
    outer = rim_rows(rim, even, recv_even[:rim], recv_odd[:rim], recv_dom[: 2 * rim]).T
    block = times(factors[1], outer)
    block_ref[...] = block

    def before(slot):
        return partial_ref[slot] + block_gather(block, nbr_ref[slot : slot + 1, :] - count)

    gathered = edge_sum(before, valid_ref, factors[2], columns[1])
    fine = node_step(own_ref[...], node_term_ref[...], gathered, factors, columns)
    rows = fine.T
    dom_ref[...] = rows[2 * rim : 4 * rim, :]
    late = (fine * facts_ref[1:2, :]).T
    low, high = late[4 * rim : 4 * rim + side], late[4 * rim + side : 4 * rim + 2 * side]
    up, down = rows[:rim], rows[rim : 2 * rim]
    for out, is_low in ((even_ref, even), (odd_ref, jnp.logical_not(even))):
        out[0:side, :] = jnp.where(is_low, low, high)
        out[side : side + 8, :] = facts_ref[...]
        out[side + 8 : side + 8 + rim, :] = jnp.where(is_low, down, up)
        out[side + 8 + rim :, :] = jnp.zeros((out.shape[0] - side - 8 - rim, LANES), f32)


def fine_kernel(
    rim,
    group,
    own_ref,
    node_term_ref,
    partial_ref,
    nbr_ref,
    valid_ref,
    factors,
    columns,
    block_ref,
    parent_ref,
    share_ref,
    dom_rows,
    side_facts,
    fine_ref,
    mine_ref,
):
    block = block_ref[...]
    count = own_ref.shape[1]

    def before(slot):
        return partial_ref[slot] + block_gather(block, nbr_ref[slot : slot + 1, :] - count)

    gathered = edge_sum(before, valid_ref, factors[2], columns[1])
    fine = node_step(own_ref[...], node_term_ref[...], gathered, factors, columns)
    fine_ref[...] = fine
    region = lax.axis_index("region")
    share = share_ref[...].astype(f32)
    chosen = hot(group, parent_ref[...] - region * group) * share
    mine_ref[0:group, :] = weighted(chosen, fine.T)
    totals = lax.dot_general(
        jnp.ones((8, count), f32), chosen, (((1,), (1,)), ((), ())), preferred_element_type=f32
    )
    base = group
    for start in range(0, group, LANES):
        mine_ref[base : base + 8, :] = totals[:, start : start + LANES]
        base += 8
    mine_ref[base : base + 2 * rim, :] = dom_rows[...]
    base += 2 * rim
    mine_ref[base : base + 8, :] = side_facts[...]


def side_places(parent, region, regions, group, rim, side):
    count = parent.shape[1]
    earlier = (iota((count, count), 0) < iota((count, count), 1)).astype(bf16)
    place = jnp.full(parent.shape, -1, jnp.int32)
    for number, steps in enumerate((regions - 1, 1)):
        local = parent - lax.rem(region + steps, regions) * group
        inside = (local >= 0) & (local < group)
        member = jnp.broadcast_to(jnp.where(inside, 1.0, 0.0), (8, count)).astype(bf16)
        rank = jnp.dot(member, earlier, preferred_element_type=f32)[0:1].astype(jnp.int32)
        place = jnp.where(inside, rank + (4 * rim + number * side), place)
    return place


def prepare_kernel(
    rim,
    token_ref,
    sent_dom,
    meta_dom,
    edge_ref,
    node_ref,
    bias_ref,
    factors,
    columns,
    chosen_ref,
    nbr_ref,
    valid_ref,
):
    slots, group = valid_ref.shape
    first = lax.axis_index("dom") == 0
    sent, received = sent_dom[2 * rim :, :], meta_dom[2 * rim :, :]
    tiles = jnp.concatenate(
        [jnp.where(first, sent, received), jnp.where(first, received, sent)], axis=1
    )
    valid_ref[...] = tiles[slots:]
    nbr = tiles[:slots].astype(jnp.int32)
    nbr_ref[...] = nbr
    for slot in range(slots):
        chosen_ref[slot] = hot(group, nbr[slot : slot + 1]).astype(bf16)
    for layer in range(factors.shape[0]):
        prepare(
            edge_ref.at[layer],
            node_ref.at[layer],
            bias_ref.at[layer],
            factors.at[layer],
            columns.at[layer],
        )


def late_places(nbr_ref, place_ref, late_ref):
    index = nbr_ref[...]
    slots, count = index.shape
    for start in range(0, count, LANES):
        now = index[:, start : start + LANES]
        late = jnp.where(now >= count, now - count, -1)
        for base in range(0, count, LANES):
            table = jnp.broadcast_to(place_ref[0:1, base : base + LANES], (slots, LANES))
            inner = now - base
            found = jnp.take_along_axis(table, inner & (LANES - 1), axis=1)
            late = jnp.where((inner >= 0) & (inner < LANES), found, late)
        late_ref[:, start : start + LANES] = late


def gather_side_kernel(rim, group, side, regions, mine_ref, even_mine, odd_mine, sum_ref):
    region = lax.axis_index("region")
    total = mine_ref[0:group, :]
    base = group + 8 * (group // LANES)
    weight = [mine_ref[group + 8 * b : group + 8 * b + 8, :] for b in range(group // LANES)]
    weight = jnp.concatenate(weight, axis=1)
    for block in (even_mine, odd_mine):
        depth = block.shape[0]
        facts = block[side : side + 8, :]
        index = facts[0:1].astype(jnp.int32) - region * group
        chosen = hot(group, jnp.where(iota((1, LANES), 1) < 4 * rim, -1, index))
        weight = weight + lax.dot_general(
            jnp.broadcast_to(facts[1:2], (8, LANES)),
            chosen,
            (((1,), (1,)), ((), ())),
            preferred_element_type=f32,
        )
        rows = block[0:side, :]
        spread = jnp.concatenate(
            [jnp.zeros((4 * rim, LANES), f32), rows, rows]
            + [jnp.zeros((LANES - 4 * rim - 2 * side, LANES), f32)] * (LANES > 4 * rim + 2 * side),
            axis=0,
        )
        both = jnp.dot(
            chosen.astype(bf16),
            jnp.concatenate(split(spread), axis=1),
            preferred_element_type=f32,
        )
        total = total + (both[:, :LANES] + both[:, LANES:])
    sum_ref[0:group, :] = total
    for b in range(group // LANES):
        sum_ref[group + 8 * b : group + 8 * b + 8, :] = weight[:, b * LANES : (b + 1) * LANES]
    count = mine_ref.shape[0]
    sum_ref[base:count, :] = mine_ref[base:, :]
    even = lax.rem(region, 2) == 0
    below, above = even_mine[side : side + 8, :], odd_mine[side : side + 8, :]
    sum_ref[count : count + 8, :] = jnp.where(even, below, above)
    sum_ref[count + 8 : count + 16, :] = jnp.where(even, above, below)


def known_facts(group, rim, dom, mine_ref, other_ref):
    base = group + 8 * (group // LANES) + 2 * rim
    first = dom == 0
    facts = []
    for place in range(3):
        rows = slice(base + 8 * place, base + 8 * place + 8)
        mine, other = mine_ref[rows, :], other_ref[rows, :]
        facts.append((jnp.where(first, mine, other), jnp.where(first, other, mine)))
    return facts


def moved(rows, steps):
    index = (iota(rows.shape, 1) - steps) & (LANES - 1)
    return jnp.take_along_axis(rows, index, axis=1)


def sides_below(region, dom):
    first = dom == 0
    near = (lax.rem(region, 2) == 0) == first
    far = (lax.rem(region // 2, 2) == 0) != first
    return near, far


def asked_columns(rim, side, region, dom, facts):
    own, below, above = facts
    near_below, far_below = sides_below(region, dom)
    lane = iota((8, LANES), 1)
    base = 4 * rim
    rims = jnp.where(
        near_below,
        jnp.where(lane < rim, moved(own[0], -rim), own[1]),
        jnp.where(lane < rim, own[0], moved(own[1], rim)),
    )
    beyond = jnp.where(
        far_below,
        jnp.where(lane < 3 * rim, moved(below[0], rim), moved(below[1], 2 * rim)),
        jnp.where(lane < 3 * rim, moved(above[0], 2 * rim), moved(above[1], 3 * rim)),
    )
    sides = jnp.where(
        near_below,
        jnp.where(lane < base + side, moved(below[0], -side), below[1]),
        jnp.where(lane < base + side, above[0], moved(above[1], side)),
    )
    asked = jnp.where(lane < 2 * rim, rims, jnp.where(lane < base, beyond, sides))
    return asked[0:1].astype(jnp.int32)


def answer_lanes(rim, side, region, dom, core, place):
    near_below, far_below = sides_below(region, dom)
    lane = iota((1, LANES), 1)
    base = 4 * rim
    second = core == 1
    skip = jnp.where(second, rim, 0)
    from_dom = (lane >= 2 * rim) & (lane < base)
    below_rim = lane < rim
    above_rim = (lane >= rim) & (lane < 2 * rim)
    low_place = (place >= base) & (place < base + side)
    low = jnp.where(
        from_dom,
        jnp.where(low_place, place + jnp.where(second, 0, side), -1),
        jnp.where(
            (lane >= base) & (lane < base + side),
            lane + jnp.where(second, side, 0),
            jnp.where(below_rim, lane + skip, -1),
        ),
    )
    high = jnp.where(
        from_dom,
        jnp.where(place >= base + side, place - jnp.where(second, side, 0), -1),
        jnp.where(
            lane >= base + side,
            lane - jnp.where(second, 0, side),
            jnp.where(above_rim, lane - rim + skip, -1),
        ),
    )
    far_low = jnp.where(below_rim, lane + 2 * rim + skip, -1)
    far_high = jnp.where(above_rim, lane + rim + skip, -1)
    return jnp.where(near_below, low, high), jnp.where(far_below, far_low, far_high)


def coarse_sources(own, factors):
    return stacked_halves(times(factors[1], own))


def coarse_layer(own, sources, chosen, valid, factors, columns):
    (term,) = own_products(factors, columns, (0,), own)
    (node_term,) = own_products(factors, columns, (3,), own)
    found = jnp.dot(sources, chosen, preferred_element_type=f32)
    count = own.shape[1]

    def before(slot):
        return folded(found[:, slot * count : (slot + 1) * count]) + term

    gathered = edge_sum(before, valid, factors[2], columns[1])
    return node_step(own, node_term, gathered, factors, columns)


def all_slots(chosen_ref):
    return jnp.concatenate([chosen_ref[slot] for slot in range(chosen_ref.shape[0])], axis=1)


def coarse_kernel(
    rim,
    group,
    side,
    mine_ref,
    other_ref,
    chosen_ref,
    nbr_ref,
    valid_ref,
    factors,
    columns,
    middle_ref,
    sources_ref,
    answer_ref,
):
    region, dom = lax.axis_index("region"), lax.axis_index("dom")
    facts = known_facts(group, rim, dom, mine_ref, other_ref)
    asked = asked_columns(rim, side, region, dom, facts) - region * group
    inside = (asked >= 0) & (asked < group)
    nbr = pick_columns(nbr_ref[...], asked)
    valid = pick_columns(valid_ref[...], asked)
    total = mine_ref[0:group, :] + other_ref[0:group, :]
    weight = [
        mine_ref[group + 8 * b : group + 8 * b + 1, :]
        + other_ref[group + 8 * b : group + 8 * b + 1, :]
        for b in range(group // LANES)
    ]
    own = total.T / jnp.maximum(jnp.concatenate(weight, axis=1), 1.0)
    sources = coarse_sources(own, factors.at[0])
    own = coarse_layer(
        own, sources, all_slots(chosen_ref), valid_ref[...], factors.at[0], columns.at[0]
    )
    middle_ref[...] = own
    sources = coarse_sources(own, factors.at[1])
    sources_ref[...] = sources
    chosen = hot(group, wide_row(nbr, 0, nbr.shape[0])).astype(bf16)
    some = pick_columns(own, asked)
    some = coarse_layer(some, sources, chosen, valid, factors.at[1], columns.at[1])
    answer_ref[...] = jnp.where(inside, some, 0.0)


def between_kernel(
    rim,
    group,
    side,
    fine_ref,
    even_mine,
    odd_mine,
    mine_ref,
    other_ref,
    middle_ref,
    sources_ref,
    chosen_ref,
    valid_ref,
    factors,
    columns,
    nbr_ref,
    parent_ref,
    share_ref,
    edge_ref,
    out_ref,
    own_ref,
    late_ref,
    partial_ref,
    weight_ref,
    lanes_ref,
    rows_ref,
    semaphores,
):
    coarse = coarse_layer(
        middle_ref[...],
        sources_ref[...],
        all_slots(chosen_ref),
        valid_ref[...],
        factors.at[1],
        columns.at[1],
    )
    rows_ref[...] = coarse.T
    rows = out_ref.shape[0]
    start = pl.multiple_of(lax.axis_index("dom") * rows, rows)
    copies = fetch(((rows_ref.at[pl.ds(start, rows)], out_ref),), semaphores)
    region = lax.axis_index("region")
    even = lax.rem(region, 2) == 0
    base = side + 8
    dom_base = group + 8 * (group // LANES)
    outer = rim_rows(
        rim,
        even,
        even_mine[base : base + rim, :],
        odd_mine[base : base + rim, :],
        other_ref[dom_base : dom_base + 2 * rim, :],
    ).T
    dom = lax.axis_index("dom")
    facts = known_facts(group, rim, dom, mine_ref, other_ref)
    own_facts, below, above = facts
    lane = iota((8, LANES), 1)
    late_facts = []
    for core in range(2):
        rims = jnp.where(lane < rim, below[core], above[core])
        sides = jnp.where(lane < 4 * rim, own_facts[1 - core], own_facts[core])
        late_facts.append(jnp.where(lane < 2 * rim, rims, sides))
    first = dom == 0
    mine = jnp.where(first, late_facts[0], late_facts[1])
    theirs = jnp.where(first, late_facts[1], late_facts[0])
    weight_ref[...] = jnp.concatenate([mine, theirs], axis=1) * 0.25
    places = [own_facts[1 - core][2:3].astype(jnp.int32) for core in range(2)]
    lanes = [
        answer_lanes(
            rim, side, region, dom, core, jnp.where(core == 0, places[0], places[1])
        )
        for core in (dom, 1 - dom)
    ]
    for row in range(2):
        pair = jnp.concatenate([lanes[0][row], lanes[1][row]], axis=1)
        lanes_ref[8 * row : 8 * row + 8, :] = jnp.broadcast_to(pair, (8, 2 * LANES))
    stacked = stacked_halves(coarse)
    local = mine[0:1].astype(jnp.int32) - region * group
    late_ref[...] = outer + (mine[1:2] * 0.25) * hot_gather(stacked, local)
    share = share_ref[...].astype(f32) * 0.25
    own = fine_ref[...] + share * hot_gather(stacked, parent_ref[...] - region * group)
    own_ref[...] = own
    stacked = stacked_halves(times(halves(edge_ref[edge_ref.shape[0] - 1, 1]), own))
    for slot in range(partial_ref.shape[0]):
        partial_ref[slot] = hot_gather(stacked, nbr_ref[slot : slot + 1, :])
    for copy in copies:
        copy.wait()


def prepare_last_kernel(
    token_ref,
    own_ref,
    nbr_ref,
    place_ref,
    edge_ref,
    node_ref,
    bias_ref,
    late_index,
    factors,
    columns,
    partial_ref,
):
    last = edge_ref.shape[0] - 1
    prepare(edge_ref.at[last], node_ref.at[last], bias_ref.at[last], factors, columns)
    late_places(nbr_ref, place_ref, late_index)
    stacked = stacked_halves(times(factors[1], own_ref[...]))
    left = nbr_ref.shape[0] - partial_ref.shape[0]
    for slot in range(partial_ref.shape[0]):
        row = left + slot
        partial_ref[slot] = hot_gather(stacked, nbr_ref[row : row + 1, :])


def side_kernel(weight_ref, lanes_ref, late_in, second_in, first_in, late_ref, back_ref):
    first = lax.axis_index("dom") == 0
    near = jnp.where(first, first_in[...], second_in[...])
    far_rows = jnp.where(first, second_in[...], first_in[...])
    late = block_gather(near, lanes_ref[0:1, :]) + block_gather(far_rows, lanes_ref[8:9, :])
    late = late * weight_ref[1:2, :]
    late_ref[...] = late_in[...] + late[:, :LANES]
    back_ref[...] = late[:, LANES:]


def last_kernel(
    own_ref,
    late_in,
    back_ref,
    partial_ref,
    partial_rest,
    late_index,
    place_ref,
    valid_ref,
    factors,
    columns,
    out_ref,
    rows_ref,
    semaphores,
):
    late = late_in[...] + back_ref[...]
    own = own_ref[...] + block_gather(late, place_ref[0:1, :])
    block = times(factors[1], late)
    term, node_term = own_products(factors, columns, (0, 3), own)

    early = partial_ref.shape[0]

    def before(slot):
        partial = partial_ref[slot] if slot < early else partial_rest[slot - early]
        return partial + block_gather(block, late_index[slot : slot + 1, :]) + term

    gathered = edge_sum(before, valid_ref, factors[2], columns[1])
    copies = []
    for place in range(PARTS):
        size = own.shape[1] // PARTS
        part = slice(place * size, (place + 1) * size)
        result = node_step(own[:, part], node_term[:, part], gathered[:, part], factors, columns)
        rows_ref[part, :] = result.T
        pair = (rows_ref.at[part], out_ref.at[part])
        copies += fetch((pair,), semaphores.at[pl.ds(place, 1)])
    for copy in copies:
        copy.wait()


def whole():
    return pl.BlockSpec(memory_space=pltpu.VMEM)


def far():
    return pl.BlockSpec(memory_space=pltpu.HBM)


def kept(value):
    return pltpu.with_memory_space_constraint(value, pltpu.HBM)


def scalars():
    return pl.BlockSpec(memory_space=pltpu.SMEM)


def kernel_call(body, in_specs, outs, scratch=(), copies=0, flops=0, sent=()):
    outs = [(out, f32) if isinstance(out[0], int) else out for out in outs]
    return pl.pallas_call(
        body,
        in_specs=in_specs,
        out_specs=tuple(far() if place in sent else whole() for place in range(len(outs))),
        out_shape=tuple(jax.ShapeDtypeStruct(shape, kind) for shape, kind in outs),
        scratch_shapes=list(scratch) + [pltpu.SemaphoreType.DMA((copies,))] * (copies > 0),
        compiler_params=pltpu.CompilerParams(vmem_limit_bytes=VMEM_BYTES),
        cost_estimate=pl.CostEstimate(
            flops=flops, bytes_accessed=4 * 2**20, transcendentals=0
        ),
    )


def swap(value, axis, partner, count):
    return lax.ppermute(value, axis, [(source, partner(source) % count) for source in range(count)])


def body(
    fine_state,
    fine_nbr,
    fine_mask,
    send_rows,
    coarse_nbr,
    coarse_mask,
    parent,
    interp_share,
    edge_w,
    node_w,
    biases,
):
    count, width = fine_state.shape
    own_coarse = coarse_nbr.shape[1]
    slots = coarse_nbr.shape[0]
    regions = lax.axis_size("region")
    domains = lax.axis_size("dom")
    group = domains * own_coarse
    rim = send_rows.shape[1]
    side = count // (8 * domains)
    fine_state, fine_nbr, fine_mask, send_rows, coarse_nbr, coarse_mask = (
        kept(value)
        for value in (fine_state, fine_nbr, fine_mask, send_rows, coarse_nbr, coarse_mask)
    )
    parent_row = kept(parent[None, :])
    share_row = kept(interp_share[None, :])
    weights = (kept(edge_w), kept(node_w), kept(biases))
    i32 = jnp.int32

    def even_partner(r):
        return r - 1 if r % 2 == 0 else r + 1

    def odd_partner(r):
        return r + 1 if r % 2 == 0 else r - 1

    def even_two_partner(r):
        return r - 2 if r // 2 % 2 == 0 else r + 2

    def odd_two_partner(r):
        return r + 2 if r // 2 % 2 == 0 else r - 2

    def even_swap(value):
        return swap(value, "region", even_partner, regions)

    def odd_swap(value):
        return swap(value, "region", odd_partner, regions)

    def dom_swap(value):
        return swap(value, "dom", lambda d: d + 1, domains)

    def both_swap(value, for_first, for_second):
        pairs = []
        for r in range(regions):
            for d in range(domains):
                target = (for_first(r) if d == 0 else for_second(r)) % regions
                pairs.append((r * domains + d, target * domains + d))
        return lax.ppermute(value, ("region", "dom"), pairs)

    columns_shape = (width, count)
    row_shape = ((1, count), i32)
    fine_slots = (fine_nbr.shape, i32)
    (
        even_out,
        odd_out,
        dom_out,
        sent_rows,
        state,
        parents,
        shares,
        nbr,
        mask,
        edge_first,
        node_first,
        bias_first,
    ) = kernel_call(
        functools.partial(pick_kernel, rim),
        [far()] * 11,
        [
            (rim, width),
            (rim, width),
            (2 * rim + 2 * slots, width),
            ((8, LANES), i32),
            fine_state.shape,
            row_shape,
            row_shape,
            fine_slots,
            fine_slots,
            edge_w.shape[1:],
            node_w.shape[1:],
            biases.shape[1:],
        ],
        [
            pltpu.SMEM(send_rows.shape, i32),
            pltpu.VMEM(coarse_nbr.shape, i32),
            pltpu.VMEM(coarse_mask.shape, i32),
        ],
        copies=11,
    )(
        send_rows,
        fine_state,
        coarse_nbr,
        coarse_mask,
        parent_row,
        share_row,
        fine_nbr,
        fine_mask,
        *weights,
    )
    meta_even = even_swap(even_out)
    meta_odd = odd_swap(odd_out)
    meta_dom = dom_swap(dom_out)

    later = edge_w.shape[0] - 1
    (
        own,
        node_term,
        partial,
        valid,
        factors,
        columns,
        place,
        side_facts,
        own_some,
        node_term_some,
        partial_some,
        nbr_some,
        valid_some,
        edge_later,
        node_later,
        bias_later,
    ) = kernel_call(
        functools.partial(before_kernel, rim, group, side, regions),
        [whole()] * 9 + [far()] * 3,
        [
            columns_shape,
            columns_shape,
            (slots, width, count),
            fine_mask.shape,
            ((6, 2 * width, width), bf16),
            (4, width, LANES),
            ((8, count), i32),
            (8, LANES),
            (width, LANES),
            (width, LANES),
            (slots, width, LANES),
            ((slots, LANES), i32),
            (slots, LANES),
            (later,) + edge_w.shape[1:],
            (later,) + node_w.shape[1:],
            (later,) + biases.shape[1:],
        ],
        copies=3,
        flops=4 * 10**9,
    )(
        state,
        sent_rows,
        parents,
        shares,
        nbr,
        mask,
        edge_first,
        node_first,
        bias_first,
        *weights,
    )

    block_rows = side + 8 + rim + 8
    dom_rows = group + 8 * (group // LANES) + 2 * rim + 8

    def first_body(*refs):
        first_kernel(rim, side, *refs[:5], count, *refs[5:])

    even_out, odd_out, dom_some, block = kernel_call(
        first_body,
        [whole()] * 11,
        [(block_rows, width), (block_rows, width), (2 * rim, width), (width, LANES)],
    )(
        own_some,
        node_term_some,
        partial_some,
        nbr_some,
        valid_some,
        factors,
        columns,
        side_facts,
        meta_even,
        meta_odd,
        meta_dom,
    )
    even_mine = even_swap(even_out)
    odd_mine = odd_swap(odd_out)

    fine_one, mine = kernel_call(
        functools.partial(fine_kernel, rim, group),
        [whole()] * 12,
        [columns_shape, (dom_rows, width)],
        flops=4 * 10**9,
    )(
        own,
        node_term,
        partial,
        nbr,
        valid,
        factors,
        columns,
        block,
        parents,
        shares,
        dom_some,
        side_facts,
    )
    (mine,) = kernel_call(
        functools.partial(gather_side_kernel, rim, group, side, regions),
        [whole()] * 3,
        [(dom_rows + 16, width)],
    )(mine, even_mine, odd_mine)
    other = dom_swap(mine)

    factors, columns, group_chosen, group_nbr, group_valid = kernel_call(
        functools.partial(prepare_kernel, rim),
        [whole()] * 6,
        [
            ((later - 1, 6, 2 * width, width), bf16),
            (later - 1, 4, width, LANES),
            ((slots, group, group), bf16),
            ((slots, group), i32),
            (slots, group),
        ],
        flops=10**9,
    )(mine, dom_out, meta_dom, edge_later, node_later, bias_later)

    middle, sources, answers = kernel_call(
        functools.partial(coarse_kernel, rim, group, side),
        [whole()] * 7,
        [(width, group), ((2 * width, group), bf16), (width, LANES)],
    )(mine, other, group_chosen, group_nbr, group_valid, factors, columns)
    first = both_swap(answers, even_partner, even_two_partner)
    second = both_swap(answers, odd_two_partner, odd_partner)

    rest = slots // REST
    coarse_out, own, late, partial, weight, lanes = kernel_call(
        functools.partial(between_kernel, rim, group, side),
        [whole()] * 15,
        [
            (own_coarse, width),
            columns_shape,
            (width, LANES),
            (slots - rest, width, count),
            (8, 2 * LANES),
            ((16, 2 * LANES), i32),
        ],
        [pltpu.VMEM((group, width), f32)],
        copies=1,
        flops=8 * 10**9,
        sent=(0,),
    )(
        fine_one,
        even_mine,
        odd_mine,
        mine,
        other,
        middle,
        sources,
        group_chosen,
        group_valid,
        factors,
        columns,
        nbr,
        parents,
        shares,
        edge_later,
    )
    late, back = kernel_call(
        side_kernel, [whole()] * 5, [(width, LANES), (width, LANES)]
    )(weight, lanes, late, second, first)
    back_here = dom_swap(back)
    late_index, factors, columns, partial_rest = kernel_call(
        prepare_last_kernel,
        [whole()] * 7,
        [
            fine_slots,
            ((6, 2 * width, width), bf16),
            (4, width, LANES),
            (rest, width, count),
        ],
        flops=10**9,
    )(back, own, nbr, place, edge_later, node_later, bias_later)
    (fine_out,) = kernel_call(
        last_kernel,
        [whole()] * 10,
        [(count, width)],
        [pltpu.VMEM((count, width), f32)],
        copies=PARTS,
        sent=(0,),
    )(
        own,
        late,
        back_here,
        partial,
        partial_rest,
        late_index,
        place,
        valid,
        factors,
        columns,
    )
    return (fine_out, coarse_out)


def solution(mesh):
    return jax.shard_map(
        body,
        mesh=mesh,
        in_specs=(
            P(("region", "dom"), None),
            P(None, ("region", "dom")),
            P(None, ("region", "dom")),
            P(None, ("region", "dom")),
            P(None, ("region", "dom")),
            P(None, ("region", "dom")),
            P(("region", "dom")),
            P(("region", "dom")),
            P(),
            P(),
            P(),
        ),
        out_specs=(P(("region", "dom"), None), P(("region", "dom"), None)),
        check_vma=False,
    )
```

```python
import functools

import jax
import jax.numpy as jnp
from jax import lax
from jax.experimental import pallas as pl
from jax.experimental.pallas import tpu as pltpu
from jax.sharding import PartitionSpec as P

epsilon = 1e-05
f32 = jnp.float32
bf16 = jnp.bfloat16
LANES = 128
PARTS = 2
REST = 3
WIDE = 512
VMEM_BYTES = 32 * 2**20


def split(values):
    high = values.astype(bf16)
    low = (values - high.astype(f32)).astype(bf16)
    return high, low


def halves(weight):
    return jnp.concatenate(split(weight.T), axis=0)


def folded(stacked):
    half = stacked.shape[0] // 2
    return stacked[:half] + stacked[half:]


def times(factor, columns):
    stacked = jnp.concatenate(split(columns), axis=0)
    wide = jnp.concatenate([factor, factor], axis=1)
    return folded(jnp.dot(wide, stacked, preferred_element_type=f32))


def centered(weight):
    return weight - jnp.mean(weight, axis=-1, keepdims=True)


def bias_block(row):
    return jnp.broadcast_to(row, (LANES, row.shape[-1])).T


def spread_out(block, width):
    return jnp.concatenate([block] * (width // LANES), axis=1)


def scaled(columns):
    spread = jnp.mean(columns * columns, axis=0, keepdims=True)
    return columns * lax.rsqrt(spread + epsilon)


def iota(shape, axis):
    return lax.broadcasted_iota(jnp.int32, shape, axis)


def hot(rows, index):
    return (iota((rows, index.shape[1]), 0) == index).astype(f32)


def block_gather(block, index):
    features = block.shape[0]
    pieces = []
    for start in range(0, index.shape[1], LANES):
        wide = jnp.broadcast_to(index[:, start : start + LANES], (features, LANES))
        found = jnp.take_along_axis(block, wide & (LANES - 1), axis=1)
        pieces.append(jnp.where((wide >= 0) & (wide < LANES), found, 0.0))
    return jnp.concatenate(pieces, axis=1)


def hot_gather(stacked, index):
    chosen = hot(stacked.shape[1], index).astype(bf16)
    return folded(jnp.dot(stacked, chosen, preferred_element_type=f32))


def stacked_halves(columns):
    return jnp.concatenate(split(columns), axis=0)


def prepare(edge, node, bias, factors, columns):
    for place, weight in enumerate(
        (edge[0], edge[1], centered(edge[2]), node[0], node[1], centered(node[2]))
    ):
        factors[place] = halves(weight)
    for place in range(4):
        row = bias[place : place + 1]
        columns[place] = bias_block(centered(row) if place % 2 else row)


def edge_sum(before, validity, factor, column):
    slots, count = validity.shape
    second_bias = spread_out(column, count)
    total = None
    for slot in range(slots):
        message = times(factor, jnp.maximum(before(slot), 0.0)) + second_bias
        spread = jnp.mean(message * message, axis=0, keepdims=True)
        message = message * (lax.rsqrt(spread + epsilon) * validity[slot : slot + 1, :])
        total = message if total is None else total + message
    return total


def node_step(own, node_term, gathered, factors, columns):
    count = own.shape[1]
    inner_act = jnp.maximum(node_term + times(factors[4], gathered), 0.0)
    update = times(factors[5], inner_act) + spread_out(columns[3], count)
    return own + scaled(update)


def own_products(factors, columns, places, own):
    stacked = stacked_halves(own)
    rows = [jnp.concatenate([factors[place]] * 2, axis=1) for place in places]
    both = jnp.dot(jnp.concatenate(rows, axis=0), stacked, preferred_element_type=f32)
    results = []
    for number, place in enumerate(places):
        rows = 2 * own.shape[0]
        result = folded(both[number * rows : (number + 1) * rows])
        if place in (0, 3):
            result = result + spread_out(columns[0 if place == 0 else 2], own.shape[1])
        results.append(result)
    return results


def pick_columns(columns, index):
    picked = None
    for start in range(0, columns.shape[1], LANES):
        block = columns[:, start : start + LANES]
        wide = jnp.broadcast_to(index - start, block.shape)
        found = jnp.take_along_axis(block, wide & (LANES - 1), axis=1)
        picked = found if picked is None else jnp.where(wide >= 0, found, picked)
    return picked


def wide_row(rows, first, number):
    return jnp.concatenate([rows[slot : slot + 1, :] for slot in range(first, first + number)], axis=1)


def fetch(copies, semaphores):
    started = []
    for place, (source, target) in enumerate(copies):
        copy = pltpu.make_async_copy(source, target, semaphores.at[place])
        copy.start()
        started.append(copy)
    return started


def pick_kernel(
    rim,
    send_hbm,
    state_hbm,
    coarse_nbr_hbm,
    coarse_mask_hbm,
    parent_hbm,
    share_hbm,
    nbr_hbm,
    mask_hbm,
    edge_hbm,
    node_hbm,
    bias_hbm,
    even_ref,
    odd_ref,
    dom_ref,
    rows_ref,
    state_ref,
    parent_ref,
    share_ref,
    nbr_ref,
    mask_ref,
    edge_ref,
    node_ref,
    bias_ref,
    send_s,
    coarse_nbr,
    coarse_mask,
    semaphores,
):
    copies = fetch(
        (
            (send_hbm, send_s),
            (state_hbm, state_ref),
            (coarse_nbr_hbm, coarse_nbr),
            (coarse_mask_hbm, coarse_mask),
            (edge_hbm.at[0], edge_ref),
            (node_hbm.at[0], node_ref),
            (nbr_hbm, nbr_ref),
            (parent_hbm, parent_ref),
            (share_hbm, share_ref),
            (bias_hbm.at[0], bias_ref),
            (mask_hbm, mask_ref),
        ),
        semaphores,
    )
    for copy in copies[:2]:
        copy.wait()
    even = lax.rem(lax.axis_index("region"), 2) == 0
    first = jnp.where(even, 1, 0)
    lane = iota((1, LANES), 1)

    def fill(out, out_base, direction, lane_base, rows):
        for k in range(rim):
            row = send_s[direction, k]
            out[pl.ds(out_base + k, 1), :] = state_ref[pl.ds(row, 1), :]
            rows = jnp.where(lane == lane_base + k, row, rows)
        return rows

    rows = fill(even_ref, 0, first, first * rim, jnp.zeros((1, LANES), jnp.int32))
    rows = fill(odd_ref, 0, 1 - first, (1 - first) * rim, rows)
    rows = fill(dom_ref, 0, 2, 2 * rim, rows)
    rows = fill(dom_ref, rim, 3, 3 * rim, rows)
    rows_ref[...] = jnp.broadcast_to(rows, rows_ref.shape)
    for copy in copies[2:]:
        copy.wait()
    slots = coarse_nbr.shape[0]
    base = 2 * rim
    dom_ref[base : base + slots, :] = coarse_nbr[...].astype(f32)
    dom_ref[base + slots : base + 2 * slots, :] = coarse_mask[...].astype(f32)


def rim_rows(rim, even, recv_even, recv_odd, recv_dom):
    low = jnp.where(even, recv_even, recv_odd)
    high = jnp.where(even, recv_odd, recv_even)
    pad = jnp.zeros((LANES - 4 * rim, low.shape[1]), f32)
    return jnp.concatenate([low, high, recv_dom, pad], axis=0)


def before_kernel(
    rim,
    group,
    side,
    regions,
    state_ref,
    rows_ref,
    parent_ref,
    share_ref,
    nbr_ref,
    mask_ref,
    edge_ref,
    node_ref,
    bias_ref,
    edge_hbm,
    node_hbm,
    bias_hbm,
    own_ref,
    node_term_ref,
    partial_ref,
    valid_ref,
    factors,
    columns,
    place_ref,
    facts_ref,
    own_first,
    node_term_first,
    partial_first,
    nbr_first,
    valid_first,
    later_edge,
    later_node,
    later_bias,
    semaphores,
):
    later = later_edge.shape[0]
    copies = fetch(
        (
            (edge_hbm.at[pl.ds(1, later)], later_edge),
            (node_hbm.at[pl.ds(1, later)], later_node),
            (bias_hbm.at[pl.ds(1, later)], later_bias),
        ),
        semaphores,
    )
    parent = parent_ref[...]
    count = parent.shape[1]
    region = lax.axis_index("region")
    place = side_places(parent, region, regions, group, rim, side)
    place_ref[...] = jnp.broadcast_to(place, place_ref.shape)
    numbers = lax.dot_general(
        jnp.broadcast_to(iota((1, count), 1).astype(f32), (8, count)),
        hot(LANES, place),
        (((1,), (1,)), ((), ())),
        precision=lax.Precision.HIGHEST,
        preferred_element_type=f32,
    )
    rims = iota((1, LANES), 1) < 4 * rim
    chosen = jnp.where(rims, rows_ref[0:1, :], numbers[0:1].astype(jnp.int32))
    facts = [parent.astype(f32), share_ref[...].astype(f32), place.astype(f32)]
    facts = jnp.concatenate(facts + [jnp.zeros((5, count), f32)], axis=0)
    facts_ref[...] = pick_columns(facts, chosen)
    own = state_ref[...].T
    own_ref[...] = own
    valid = mask_ref[...].astype(f32)
    valid_ref[...] = valid
    prepare(edge_ref, node_ref, bias_ref, factors, columns)
    term, source, node_term = own_products(factors, columns, (0, 1, 3), own)
    node_term_ref[...] = node_term
    stacked = stacked_halves(source)
    slots = nbr_ref.shape[0]
    for slot in range(slots):
        partial_ref[slot] = term + hot_gather(stacked, nbr_ref[slot : slot + 1, :])
    own = pick_columns(own, chosen)
    own_first[...] = own
    term, node_term = own_products(factors, columns, (0, 3), own)
    node_term_first[...] = node_term
    valid_first[...] = pick_columns(valid, chosen)
    nbr = pick_columns(nbr_ref[...], chosen)
    nbr_first[...] = nbr
    together = WIDE // LANES
    for slot in range(0, slots, together):
        found = hot_gather(stacked, wide_row(nbr, slot, together))
        for number in range(together):
            partial_first[slot + number] = (
                term + found[:, number * LANES : (number + 1) * LANES]
            )
    for copy in copies:
        copy.wait()


def weighted(selection, rows):
    pair = jnp.concatenate(split(rows), axis=1)
    both = jnp.dot(selection.astype(bf16), pair, preferred_element_type=f32)
    return both[:, :LANES] + both[:, LANES:]


def first_kernel(
    rim,
    side,
    own_ref,
    node_term_ref,
    partial_ref,
    nbr_ref,
    valid_ref,
    count,
    factors,
    columns,
    facts_ref,
    recv_even,
    recv_odd,
    recv_dom,
    even_ref,
    odd_ref,
    dom_ref,
    block_ref,
):
    even = lax.rem(lax.axis_index("region"), 2) == 0
    outer = rim_rows(rim, even, recv_even[:rim], recv_odd[:rim], recv_dom[: 2 * rim]).T
    block = times(factors[1], outer)
    block_ref[...] = block

    def before(slot):
        return partial_ref[slot] + block_gather(block, nbr_ref[slot : slot + 1, :] - count)

    gathered = edge_sum(before, valid_ref, factors[2], columns[1])
    fine = node_step(own_ref[...], node_term_ref[...], gathered, factors, columns)
    rows = fine.T
    dom_ref[...] = rows[2 * rim : 4 * rim, :]
    late = (fine * facts_ref[1:2, :]).T
    low, high = late[4 * rim : 4 * rim + side], late[4 * rim + side : 4 * rim + 2 * side]
    up, down = rows[:rim], rows[rim : 2 * rim]
    for out, is_low in ((even_ref, even), (odd_ref, jnp.logical_not(even))):
        out[0:side, :] = jnp.where(is_low, low, high)
        out[side : side + 8, :] = facts_ref[...]
        out[side + 8 : side + 8 + rim, :] = jnp.where(is_low, down, up)


def fine_kernel(
    rim,
    group,
    own_ref,
    node_term_ref,
    partial_ref,
    nbr_ref,
    valid_ref,
    factors,
    columns,
    block_ref,
    parent_ref,
    share_ref,
    dom_rows,
    side_facts,
    fine_ref,
    mine_ref,
):
    block = block_ref[...]
    count = own_ref.shape[1]

    def before(slot):
        return partial_ref[slot] + block_gather(block, nbr_ref[slot : slot + 1, :] - count)

    gathered = edge_sum(before, valid_ref, factors[2], columns[1])
    fine = node_step(own_ref[...], node_term_ref[...], gathered, factors, columns)
    fine_ref[...] = fine
    region = lax.axis_index("region")
    share = share_ref[...].astype(f32)
    chosen = hot(group, parent_ref[...] - region * group) * share
    mine_ref[0:group, :] = weighted(chosen, fine.T)
    totals = lax.dot_general(
        jnp.ones((8, count), f32), chosen, (((1,), (1,)), ((), ())), preferred_element_type=f32
    )
    base = group
    for start in range(0, group, LANES):
        mine_ref[base : base + 8, :] = totals[:, start : start + LANES]
        base += 8
    mine_ref[base : base + 2 * rim, :] = dom_rows[...]
    base += 2 * rim
    mine_ref[base : base + 8, :] = side_facts[...]


def side_places(parent, region, regions, group, rim, side):
    count = parent.shape[1]
    earlier = (iota((count, count), 0) < iota((count, count), 1)).astype(bf16)
    place = jnp.full(parent.shape, -1, jnp.int32)
    for number, steps in enumerate((regions - 1, 1)):
        local = parent - lax.rem(region + steps, regions) * group
        inside = (local >= 0) & (local < group)
        member = jnp.broadcast_to(jnp.where(inside, 1.0, 0.0), (8, count)).astype(bf16)
        rank = jnp.dot(member, earlier, preferred_element_type=f32)[0:1].astype(jnp.int32)
        place = jnp.where(inside, rank + (4 * rim + number * side), place)
    return place


def prepare_kernel(
    rim,
    token_ref,
    sent_dom,
    meta_dom,
    edge_ref,
    node_ref,
    bias_ref,
    factors,
    columns,
    chosen_ref,
    nbr_ref,
    valid_ref,
):
    slots, group = valid_ref.shape
    first = lax.axis_index("dom") == 0
    sent, received = sent_dom[2 * rim :, :], meta_dom[2 * rim :, :]
    tiles = jnp.concatenate(
        [jnp.where(first, sent, received), jnp.where(first, received, sent)], axis=1
    )
    valid_ref[...] = tiles[slots:]
    nbr = tiles[:slots].astype(jnp.int32)
    nbr_ref[...] = nbr
    for slot in range(slots):
        chosen_ref[slot] = hot(group, nbr[slot : slot + 1]).astype(bf16)
    for layer in range(factors.shape[0]):
        prepare(
            edge_ref.at[layer],
            node_ref.at[layer],
            bias_ref.at[layer],
            factors.at[layer],
            columns.at[layer],
        )


def late_places(nbr_ref, place_ref, late_ref):
    index = nbr_ref[...]
    slots, count = index.shape
    for start in range(0, count, LANES):
        now = index[:, start : start + LANES]
        late = jnp.where(now >= count, now - count, -1)
        for base in range(0, count, LANES):
            table = jnp.broadcast_to(place_ref[0:1, base : base + LANES], (slots, LANES))
            inner = now - base
            found = jnp.take_along_axis(table, inner & (LANES - 1), axis=1)
            late = jnp.where((inner >= 0) & (inner < LANES), found, late)
        late_ref[:, start : start + LANES] = late


def gather_side_kernel(rim, group, side, regions, mine_ref, even_mine, odd_mine, sum_ref):
    region = lax.axis_index("region")
    total = mine_ref[0:group, :]
    base = group + 8 * (group // LANES)
    weight = [mine_ref[group + 8 * b : group + 8 * b + 8, :] for b in range(group // LANES)]
    weight = jnp.concatenate(weight, axis=1)
    for block in (even_mine, odd_mine):
        depth = block.shape[0]
        facts = block[side : side + 8, :]
        index = facts[0:1].astype(jnp.int32) - region * group
        chosen = hot(group, jnp.where(iota((1, LANES), 1) < 4 * rim, -1, index))
        weight = weight + lax.dot_general(
            jnp.broadcast_to(facts[1:2], (8, LANES)),
            chosen,
            (((1,), (1,)), ((), ())),
            preferred_element_type=f32,
        )
        rows = block[0:side, :]
        spread = jnp.concatenate(
            [jnp.zeros((4 * rim, LANES), f32), rows, rows]
            + [jnp.zeros((LANES - 4 * rim - 2 * side, LANES), f32)] * (LANES > 4 * rim + 2 * side),
            axis=0,
        )
        both = jnp.dot(
            chosen.astype(bf16),
            jnp.concatenate(split(spread), axis=1),
            preferred_element_type=f32,
        )
        total = total + (both[:, :LANES] + both[:, LANES:])
    sum_ref[0:group, :] = total
    for b in range(group // LANES):
        sum_ref[group + 8 * b : group + 8 * b + 8, :] = weight[:, b * LANES : (b + 1) * LANES]
    count = mine_ref.shape[0]
    sum_ref[base:count, :] = mine_ref[base:, :]
    even = lax.rem(region, 2) == 0
    below, above = even_mine[side : side + 8, :], odd_mine[side : side + 8, :]
    sum_ref[count : count + 8, :] = jnp.where(even, below, above)
    sum_ref[count + 8 : count + 16, :] = jnp.where(even, above, below)


def known_facts(group, rim, dom, mine_ref, other_ref):
    base = group + 8 * (group // LANES) + 2 * rim
    first = dom == 0
    facts = []
    for place in range(3):
        rows = slice(base + 8 * place, base + 8 * place + 8)
        mine, other = mine_ref[rows, :], other_ref[rows, :]
        facts.append((jnp.where(first, mine, other), jnp.where(first, other, mine)))
    return facts


def moved(rows, steps):
    index = (iota(rows.shape, 1) - steps) & (LANES - 1)
    return jnp.take_along_axis(rows, index, axis=1)


def sides_below(region, dom):
    first = dom == 0
    near = (lax.rem(region, 2) == 0) == first
    far = (lax.rem(region // 2, 2) == 0) != first
    return near, far


def asked_columns(rim, side, region, dom, facts):
    own, below, above = facts
    near_below, far_below = sides_below(region, dom)
    lane = iota((8, LANES), 1)
    base = 4 * rim
    rims = jnp.where(
        near_below,
        jnp.where(lane < rim, moved(own[0], -rim), own[1]),
        jnp.where(lane < rim, own[0], moved(own[1], rim)),
    )
    beyond = jnp.where(
        far_below,
        jnp.where(lane < 3 * rim, moved(below[0], rim), moved(below[1], 2 * rim)),
        jnp.where(lane < 3 * rim, moved(above[0], 2 * rim), moved(above[1], 3 * rim)),
    )
    sides = jnp.where(
        near_below,
        jnp.where(lane < base + side, moved(below[0], -side), below[1]),
        jnp.where(lane < base + side, above[0], moved(above[1], side)),
    )
    asked = jnp.where(lane < 2 * rim, rims, jnp.where(lane < base, beyond, sides))
    return asked[0:1].astype(jnp.int32)


def answer_lanes(rim, side, region, dom, core, place):
    near_below, far_below = sides_below(region, dom)
    lane = iota((1, LANES), 1)
    base = 4 * rim
    second = core == 1
    skip = jnp.where(second, rim, 0)
    from_dom = (lane >= 2 * rim) & (lane < base)
    below_rim = lane < rim
    above_rim = (lane >= rim) & (lane < 2 * rim)
    low_place = (place >= base) & (place < base + side)
    low = jnp.where(
        from_dom,
        jnp.where(low_place, place + jnp.where(second, 0, side), -1),
        jnp.where(
            (lane >= base) & (lane < base + side),
            lane + jnp.where(second, side, 0),
            jnp.where(below_rim, lane + skip, -1),
        ),
    )
    high = jnp.where(
        from_dom,
        jnp.where(place >= base + side, place - jnp.where(second, side, 0), -1),
        jnp.where(
            lane >= base + side,
            lane - jnp.where(second, 0, side),
            jnp.where(above_rim, lane - rim + skip, -1),
        ),
    )
    far_low = jnp.where(below_rim, lane + 2 * rim + skip, -1)
    far_high = jnp.where(above_rim, lane + rim + skip, -1)
    return jnp.where(near_below, low, high), jnp.where(far_below, far_low, far_high)


def coarse_sources(own, factors):
    return stacked_halves(times(factors[1], own))


def coarse_layer(own, sources, chosen, valid, factors, columns):
    (term,) = own_products(factors, columns, (0,), own)
    (node_term,) = own_products(factors, columns, (3,), own)
    found = jnp.dot(sources, chosen, preferred_element_type=f32)
    count = own.shape[1]

    def before(slot):
        return folded(found[:, slot * count : (slot + 1) * count]) + term

    gathered = edge_sum(before, valid, factors[2], columns[1])
    return node_step(own, node_term, gathered, factors, columns)


def all_slots(chosen_ref):
    return jnp.concatenate([chosen_ref[slot] for slot in range(chosen_ref.shape[0])], axis=1)


def coarse_kernel(
    rim,
    group,
    side,
    mine_ref,
    other_ref,
    chosen_ref,
    nbr_ref,
    valid_ref,
    factors,
    columns,
    middle_ref,
    sources_ref,
    first_ref,
    second_ref,
):
    region, dom = lax.axis_index("region"), lax.axis_index("dom")
    facts = known_facts(group, rim, dom, mine_ref, other_ref)
    asked = asked_columns(rim, side, region, dom, facts) - region * group
    inside = (asked >= 0) & (asked < group)
    nbr = pick_columns(nbr_ref[...], asked)
    valid = pick_columns(valid_ref[...], asked)
    total = mine_ref[0:group, :] + other_ref[0:group, :]
    weight = [
        mine_ref[group + 8 * b : group + 8 * b + 1, :]
        + other_ref[group + 8 * b : group + 8 * b + 1, :]
        for b in range(group // LANES)
    ]
    own = total.T / jnp.maximum(jnp.concatenate(weight, axis=1), 1.0)
    sources = coarse_sources(own, factors.at[0])
    own = coarse_layer(
        own, sources, all_slots(chosen_ref), valid_ref[...], factors.at[0], columns.at[0]
    )
    middle_ref[...] = own
    sources = coarse_sources(own, factors.at[1])
    sources_ref[...] = sources
    chosen = hot(group, wide_row(nbr, 0, nbr.shape[0])).astype(bf16)
    some = pick_columns(own, asked)
    some = coarse_layer(some, sources, chosen, valid, factors.at[1], columns.at[1])
    rows = jnp.where(inside, some, 0.0).T
    near = jnp.concatenate([rows[: 2 * rim], rows[4 * rim :]], axis=0)
    beyond = rows[2 * rim : 2 * rim + near.shape[0]]
    first = dom == 0
    first_ref[...] = jnp.where(first, near, beyond)
    second_ref[...] = jnp.where(first, beyond, near)


def between_kernel(
    rim,
    group,
    side,
    fine_ref,
    even_mine,
    odd_mine,
    mine_ref,
    other_ref,
    middle_ref,
    sources_ref,
    chosen_ref,
    valid_ref,
    factors,
    columns,
    nbr_ref,
    parent_ref,
    share_ref,
    edge_ref,
    out_ref,
    own_ref,
    late_ref,
    partial_ref,
    weight_ref,
    lanes_ref,
    rows_ref,
    semaphores,
):
    coarse = coarse_layer(
        middle_ref[...],
        sources_ref[...],
        all_slots(chosen_ref),
        valid_ref[...],
        factors.at[1],
        columns.at[1],
    )
    rows_ref[...] = coarse.T
    rows = out_ref.shape[0]
    start = pl.multiple_of(lax.axis_index("dom") * rows, rows)
    copies = fetch(((rows_ref.at[pl.ds(start, rows)], out_ref),), semaphores)
    region = lax.axis_index("region")
    even = lax.rem(region, 2) == 0
    base = side + 8
    dom_base = group + 8 * (group // LANES)
    outer = rim_rows(
        rim,
        even,
        even_mine[base : base + rim, :],
        odd_mine[base : base + rim, :],
        other_ref[dom_base : dom_base + 2 * rim, :],
    ).T
    dom = lax.axis_index("dom")
    facts = known_facts(group, rim, dom, mine_ref, other_ref)
    own_facts, below, above = facts
    lane = iota((8, LANES), 1)
    late_facts = []
    for core in range(2):
        rims = jnp.where(lane < rim, below[core], above[core])
        sides = jnp.where(lane < 4 * rim, own_facts[1 - core], own_facts[core])
        late_facts.append(jnp.where(lane < 2 * rim, rims, sides))
    first = dom == 0
    mine = jnp.where(first, late_facts[0], late_facts[1])
    theirs = jnp.where(first, late_facts[1], late_facts[0])
    weight_ref[...] = jnp.concatenate([mine, theirs], axis=1) * 0.25
    places = [own_facts[1 - core][2:3].astype(jnp.int32) for core in range(2)]
    lanes = [
        answer_lanes(
            rim, side, region, dom, core, jnp.where(core == 0, places[0], places[1])
        )
        for core in (dom, 1 - dom)
    ]
    for row in range(2):
        pair = jnp.concatenate([lanes[0][row], lanes[1][row]], axis=1)
        lanes_ref[8 * row : 8 * row + 8, :] = jnp.broadcast_to(pair, (8, 2 * LANES))
    stacked = stacked_halves(coarse)
    local = mine[0:1].astype(jnp.int32) - region * group
    late_ref[...] = outer + (mine[1:2] * 0.25) * hot_gather(stacked, local)
    share = share_ref[...].astype(f32) * 0.25
    own = fine_ref[...] + share * hot_gather(stacked, parent_ref[...] - region * group)
    own_ref[...] = own
    stacked = stacked_halves(times(halves(edge_ref[edge_ref.shape[0] - 1, 1]), own))
    for slot in range(partial_ref.shape[0]):
        partial_ref[slot] = hot_gather(stacked, nbr_ref[slot : slot + 1, :])
    for copy in copies:
        copy.wait()


def prepare_last_kernel(
    token_ref,
    own_ref,
    nbr_ref,
    place_ref,
    edge_ref,
    node_ref,
    bias_ref,
    late_index,
    factors,
    columns,
    partial_ref,
):
    last = edge_ref.shape[0] - 1
    prepare(edge_ref.at[last], node_ref.at[last], bias_ref.at[last], factors, columns)
    late_places(nbr_ref, place_ref, late_index)
    stacked = stacked_halves(times(factors[1], own_ref[...]))
    left = nbr_ref.shape[0] - partial_ref.shape[0]
    for slot in range(partial_ref.shape[0]):
        row = left + slot
        partial_ref[slot] = hot_gather(stacked, nbr_ref[row : row + 1, :])


def side_kernel(rim, weight_ref, lanes_ref, late_in, first_in, second_in, late_ref, back_ref):
    first = lax.axis_index("dom") == 0
    near = jnp.where(first, first_in[...], second_in[...])
    beyond = jnp.where(first, second_in[...], first_in[...])
    rims = [near[: 2 * rim], beyond[: 2 * rim], near[2 * rim :]]
    came = jnp.concatenate(rims, axis=0).T
    late = block_gather(came, lanes_ref[0:1, :]) + block_gather(came, lanes_ref[8:9, :])
    late = late * weight_ref[1:2, :]
    late_ref[...] = late_in[...] + late[:, :LANES]
    back_ref[...] = late[:, LANES:]


def last_kernel(
    own_ref,
    late_in,
    back_ref,
    partial_ref,
    partial_rest,
    late_index,
    place_ref,
    valid_ref,
    factors,
    columns,
    out_ref,
    rows_ref,
    semaphores,
):
    late = late_in[...] + back_ref[...]
    own = own_ref[...] + block_gather(late, place_ref[0:1, :])
    block = times(factors[1], late)
    term, node_term = own_products(factors, columns, (0, 3), own)

    early = partial_ref.shape[0]

    def before(slot):
        partial = partial_ref[slot] if slot < early else partial_rest[slot - early]
        return partial + block_gather(block, late_index[slot : slot + 1, :]) + term

    gathered = edge_sum(before, valid_ref, factors[2], columns[1])
    copies = []
    for place in range(PARTS):
        size = own.shape[1] // PARTS
        part = slice(place * size, (place + 1) * size)
        result = node_step(own[:, part], node_term[:, part], gathered[:, part], factors, columns)
        rows_ref[part, :] = result.T
        pair = (rows_ref.at[part], out_ref.at[part])
        copies += fetch((pair,), semaphores.at[pl.ds(place, 1)])
    for copy in copies:
        copy.wait()


def whole():
    return pl.BlockSpec(memory_space=pltpu.VMEM)


def far():
    return pl.BlockSpec(memory_space=pltpu.HBM)


def kept(value):
    return pltpu.with_memory_space_constraint(value, pltpu.HBM)


def scalars():
    return pl.BlockSpec(memory_space=pltpu.SMEM)


def kernel_call(body, in_specs, outs, scratch=(), copies=0, flops=0, sent=()):
    outs = [(out, f32) if isinstance(out[0], int) else out for out in outs]
    return pl.pallas_call(
        body,
        in_specs=in_specs,
        out_specs=tuple(far() if place in sent else whole() for place in range(len(outs))),
        out_shape=tuple(jax.ShapeDtypeStruct(shape, kind) for shape, kind in outs),
        scratch_shapes=list(scratch) + [pltpu.SemaphoreType.DMA((copies,))] * (copies > 0),
        compiler_params=pltpu.CompilerParams(vmem_limit_bytes=VMEM_BYTES),
        cost_estimate=pl.CostEstimate(
            flops=flops, bytes_accessed=4 * 2**20, transcendentals=0
        ),
    )


def swap(value, axis, partner, count):
    return lax.ppermute(value, axis, [(source, partner(source) % count) for source in range(count)])


def body(
    fine_state,
    fine_nbr,
    fine_mask,
    send_rows,
    coarse_nbr,
    coarse_mask,
    parent,
    interp_share,
    edge_w,
    node_w,
    biases,
):
    count, width = fine_state.shape
    own_coarse = coarse_nbr.shape[1]
    slots = coarse_nbr.shape[0]
    regions = lax.axis_size("region")
    domains = lax.axis_size("dom")
    group = domains * own_coarse
    rim = send_rows.shape[1]
    side = count // (8 * domains)
    fine_state, fine_nbr, fine_mask, send_rows, coarse_nbr, coarse_mask = (
        kept(value)
        for value in (fine_state, fine_nbr, fine_mask, send_rows, coarse_nbr, coarse_mask)
    )
    parent_row = kept(parent[None, :])
    share_row = kept(interp_share[None, :])
    weights = (kept(edge_w), kept(node_w), kept(biases))
    i32 = jnp.int32

    def even_partner(r):
        return r - 1 if r % 2 == 0 else r + 1

    def odd_partner(r):
        return r + 1 if r % 2 == 0 else r - 1

    def even_two_partner(r):
        return r - 2 if r // 2 % 2 == 0 else r + 2

    def odd_two_partner(r):
        return r + 2 if r // 2 % 2 == 0 else r - 2

    def even_swap(value):
        return swap(value, "region", even_partner, regions)

    def odd_swap(value):
        return swap(value, "region", odd_partner, regions)

    def dom_swap(value):
        return swap(value, "dom", lambda d: d + 1, domains)

    def both_swap(value, for_first, for_second):
        pairs = []
        for r in range(regions):
            for d in range(domains):
                target = (for_first(r) if d == 0 else for_second(r)) % regions
                pairs.append((r * domains + d, target * domains + d))
        return lax.ppermute(value, ("region", "dom"), pairs)

    columns_shape = (width, count)
    row_shape = ((1, count), i32)
    fine_slots = (fine_nbr.shape, i32)
    (
        even_out,
        odd_out,
        dom_out,
        sent_rows,
        state,
        parents,
        shares,
        nbr,
        mask,
        edge_first,
        node_first,
        bias_first,
    ) = kernel_call(
        functools.partial(pick_kernel, rim),
        [far()] * 11,
        [
            (rim, width),
            (rim, width),
            (2 * rim + 2 * slots, width),
            ((8, LANES), i32),
            fine_state.shape,
            row_shape,
            row_shape,
            fine_slots,
            fine_slots,
            edge_w.shape[1:],
            node_w.shape[1:],
            biases.shape[1:],
        ],
        [
            pltpu.SMEM(send_rows.shape, i32),
            pltpu.VMEM(coarse_nbr.shape, i32),
            pltpu.VMEM(coarse_mask.shape, i32),
        ],
        copies=11,
    )(
        send_rows,
        fine_state,
        coarse_nbr,
        coarse_mask,
        parent_row,
        share_row,
        fine_nbr,
        fine_mask,
        *weights,
    )
    meta_even = even_swap(even_out)
    meta_odd = odd_swap(odd_out)
    meta_dom = dom_swap(dom_out)

    later = edge_w.shape[0] - 1
    (
        own,
        node_term,
        partial,
        valid,
        factors,
        columns,
        place,
        side_facts,
        own_some,
        node_term_some,
        partial_some,
        nbr_some,
        valid_some,
        edge_later,
        node_later,
        bias_later,
    ) = kernel_call(
        functools.partial(before_kernel, rim, group, side, regions),
        [whole()] * 9 + [far()] * 3,
        [
            columns_shape,
            columns_shape,
            (slots, width, count),
            fine_mask.shape,
            ((6, 2 * width, width), bf16),
            (4, width, LANES),
            ((8, count), i32),
            (8, LANES),
            (width, LANES),
            (width, LANES),
            (slots, width, LANES),
            ((slots, LANES), i32),
            (slots, LANES),
            (later,) + edge_w.shape[1:],
            (later,) + node_w.shape[1:],
            (later,) + biases.shape[1:],
        ],
        copies=3,
        flops=4 * 10**9,
    )(
        state,
        sent_rows,
        parents,
        shares,
        nbr,
        mask,
        edge_first,
        node_first,
        bias_first,
        *weights,
    )

    block_rows = side + 8 + rim
    dom_rows = group + 8 * (group // LANES) + 2 * rim + 8

    def first_body(*refs):
        first_kernel(rim, side, *refs[:5], count, *refs[5:])

    even_out, odd_out, dom_some, block = kernel_call(
        first_body,
        [whole()] * 11,
        [(block_rows, width), (block_rows, width), (2 * rim, width), (width, LANES)],
    )(
        own_some,
        node_term_some,
        partial_some,
        nbr_some,
        valid_some,
        factors,
        columns,
        side_facts,
        meta_even,
        meta_odd,
        meta_dom,
    )
    even_mine = even_swap(even_out)
    odd_mine = odd_swap(odd_out)

    fine_one, mine = kernel_call(
        functools.partial(fine_kernel, rim, group),
        [whole()] * 12,
        [columns_shape, (dom_rows, width)],
        flops=4 * 10**9,
    )(
        own,
        node_term,
        partial,
        nbr,
        valid,
        factors,
        columns,
        block,
        parents,
        shares,
        dom_some,
        side_facts,
    )
    (mine,) = kernel_call(
        functools.partial(gather_side_kernel, rim, group, side, regions),
        [whole()] * 3,
        [(dom_rows + 16, width)],
    )(mine, even_mine, odd_mine)
    other = dom_swap(mine)

    factors, columns, group_chosen, group_nbr, group_valid = kernel_call(
        functools.partial(prepare_kernel, rim),
        [whole()] * 6,
        [
            ((later - 1, 6, 2 * width, width), bf16),
            (later - 1, 4, width, LANES),
            ((slots, group, group), bf16),
            ((slots, group), i32),
            (slots, group),
        ],
        flops=10**9,
    )(mine, dom_out, meta_dom, edge_later, node_later, bias_later)

    near_rows = 2 * rim + 2 * side
    middle, sources, first_out, second_out = kernel_call(
        functools.partial(coarse_kernel, rim, group, side),
        [whole()] * 7,
        [
            (width, group),
            ((2 * width, group), bf16),
            (near_rows, width),
            (near_rows, width),
        ],
    )(mine, other, group_chosen, group_nbr, group_valid, factors, columns)
    first = both_swap(first_out, even_partner, even_two_partner)
    second = both_swap(second_out, odd_two_partner, odd_partner)

    rest = slots // REST
    coarse_out, own, late, partial, weight, lanes = kernel_call(
        functools.partial(between_kernel, rim, group, side),
        [whole()] * 15,
        [
            (own_coarse, width),
            columns_shape,
            (width, LANES),
            (slots - rest, width, count),
            (8, 2 * LANES),
            ((16, 2 * LANES), i32),
        ],
        [pltpu.VMEM((group, width), f32)],
        copies=1,
        flops=8 * 10**9,
        sent=(0,),
    )(
        fine_one,
        even_mine,
        odd_mine,
        mine,
        other,
        middle,
        sources,
        group_chosen,
        group_valid,
        factors,
        columns,
        nbr,
        parents,
        shares,
        edge_later,
    )
    late, back = kernel_call(
        functools.partial(side_kernel, rim), [whole()] * 5, [(width, LANES), (width, LANES)]
    )(weight, lanes, late, first, second)
    back_here = dom_swap(back)
    late_index, factors, columns, partial_rest = kernel_call(
        prepare_last_kernel,
        [whole()] * 7,
        [
            fine_slots,
            ((6, 2 * width, width), bf16),
            (4, width, LANES),
            (rest, width, count),
        ],
        flops=10**9,
    )(back, own, nbr, place, edge_later, node_later, bias_later)
    (fine_out,) = kernel_call(
        last_kernel,
        [whole()] * 10,
        [(count, width)],
        [pltpu.VMEM((count, width), f32)],
        copies=PARTS,
        sent=(0,),
    )(
        own,
        late,
        back_here,
        partial,
        partial_rest,
        late_index,
        place,
        valid,
        factors,
        columns,
    )
    return (fine_out, coarse_out)


def solution(mesh):
    return jax.shard_map(
        body,
        mesh=mesh,
        in_specs=(
            P(("region", "dom"), None),
            P(None, ("region", "dom")),
            P(None, ("region", "dom")),
            P(None, ("region", "dom")),
            P(None, ("region", "dom")),
            P(None, ("region", "dom")),
            P(("region", "dom")),
            P(("region", "dom")),
            P(),
            P(),
            P(),
        ),
        out_specs=(P(("region", "dom"), None), P(("region", "dom"), None)),
        check_vma=False,
    )
```
